32 devices in a mesh: dp: 16 (over z, y, core), sub: 2 (over x).
Axes of the slice: x: 2, y: 2, z: 4, core: 2. Of those that a mesh axis runs over, the one named last changes fastest.
Arguments:
- features: bfloat16 [16, 2, 300, 25, 256], P('dp', None, None, None, 'sub'), may hold values from -12 to 12
- presence: int32 [16, 2], P('dp'), may hold values from 0 to 1
- parents: int32 [25], replicated, may hold values from 0 to 23, as said below
- w_spatial: bfloat16 [256, 768], P(None, 'sub'), may hold values from -0.375 to 0.375
- importance: float32 [3, 25, 25], replicated, may hold values from 0.5 to 1.5
- gain_one: float32 [256], P('sub'), may hold values from 0.25 to 1.75
- shift_one: float32 [256], P('sub'), may hold values from -0.5 to 0.5
- w_temporal: bfloat16 [9, 256, 256], P(None, None, 'sub'), may hold values from -0.125 to 0.125
- gain_two: float32 [256], P('sub'), may hold values from 0.25 to 1.75
- shift_two: float32 [256], P('sub'), may hold values from -0.5 to 0.5
- cotangent: bfloat16 [16, 2, 300, 25, 256], P('dp', None, None, None, 'sub'), may hold values from -6 to 6
Outputs:
- activations: float32 [16, 2, 300, 25, 256], P('dp', None, None, None, 'sub')
- input_grad: float32 [16, 2, 300, 25, 256], P('dp', None, None, None, 'sub')
- spatial_grad: float32 [256, 768], P(None, 'sub')
- importance_grad: float32 [3, 25, 25], replicated
- gain_one_grad: float32 [256], P('sub')
- shift_one_grad: float32 [256], P('sub')
- temporal_grad: float32 [9, 256, 256], P(None, None, 'sub')
- gain_two_grad: float32 [256], P('sub')
- shift_two_grad: float32 [256], P('sub')
The draws below stay inside these ranges and needn't reach their ends.
Inputs may be any that keep to these rules, and one draw needn't show every extreme that they name: `parents`: entry 0 is 0, entry v is below v for v >= 1, and entry 24 is 23, so the entries form a tree rooted at joint 0.
All inputs are finite; a program needn't handle non-finite values.
Results may differ from the reference program's by a relative error of at most 0.0069.
Values may be sent and summed in bfloat16 or wider, within the bound.
A program may use at most 320 MiB of HBM per device.

```python
import jax
import jax.numpy as jnp
from jax import lax

C = 256
V = 25
KT = 9
FRAMES = 300
CLIPS = 16


def presence_bits(key):
    bits_key = jax.random.fold_in(key, 7)
    second = jax.random.randint(bits_key, (CLIPS, 1), 0, 2, dtype=jnp.int32)
    return jnp.concatenate([jnp.ones((CLIPS, 1), jnp.int32), second], axis=1)


def draw_presence(key, part):
    shared = presence_bits(key)
    return shared


def draw_parents(key, part):
    key = jax.random.fold_in(key, 13)
    position = jnp.arange(V, dtype=jnp.int32)
    upper = jnp.maximum(position, 1)
    picked = jax.random.randint(key, (V,), 0, upper, dtype=jnp.int32)
    picked = jnp.where(position == V - 1, V - 2, picked)
    return jnp.where(position == 0, 0, picked).astype(jnp.int32)


def draw_features(key, part):
    shared = presence_bits(key)
    key = jax.random.fold_in(key, 11)
    base_key, offset_key = jax.random.split(key, 2)
    full_shape = (CLIPS, 2, FRAMES, V, C)
    clip_ramp = 0.6 + 1.2 * jnp.arange(CLIPS, dtype=jnp.float32) / max(CLIPS - 1, 1)
    offset = 0.5 * jnp.clip(jax.random.normal(offset_key, (C,), jnp.float32), -3.0, 3.0)
    base_values = jnp.clip(jax.random.normal(base_key, full_shape, jnp.float32), -4.0, 4.0)
    present = 0.2 + 0.8 * shared.astype(jnp.float32)
    values = clip_ramp[:, None, None, None, None] * present[:, :, None, None, None] * (base_values + offset)
    return values.astype(jnp.bfloat16)


def shard_levels(key, shape, cuts, smallest, high):
    factor_of = 1.0
    for axis_at, parts in cuts:
        draws = jax.random.uniform(jax.random.fold_in(jax.random.fold_in(key, 6), axis_at), (parts,), jnp.float32, smallest / len(cuts), high / len(cuts))
        factor_of = factor_of * jnp.repeat(jnp.exp(draws), shape[axis_at] // parts).reshape((-1,) + (1,) * (len(shape) - 1 - axis_at))
    return factor_of


def bell_draw(own_key, dims, spread, limit, shards=(), kind=jnp.bfloat16):
    values = spread * jax.random.normal(own_key, dims, jnp.float32)
    if shards:
        values = values * shard_levels(own_key, dims, shards, -0.22, 0.18)
    return jnp.clip(values, -limit, limit).astype(kind)


def setup_inputs(seed: int = 0) -> dict:
    seeds = jax.random.split(jax.random.key(seed), 12)
    features = draw_features(jax.random.fold_in(seeds[11], 71), 0)
    presence = draw_presence(jax.random.fold_in(seeds[11], 71), 0)
    parents = draw_parents(jax.random.fold_in(seeds[11], 71), 0)
    w_spatial = bell_draw(seeds[3], (C, 3 * C), C ** -0.5, 0.375, ((1, 2),))
    importance = jnp.clip(jax.random.uniform(seeds[4], (3, V, V), jnp.float32, 0.5, 1.5), 0.5, 1.5)
    gain_one = jnp.clip(1.0 + 0.15 * jax.random.normal(seeds[5], (C,), jnp.float32), 0.25, 1.75)
    shift_one = jnp.clip(jax.random.uniform(seeds[6], (C,), jnp.float32, -0.5, 0.5) * shard_levels(seeds[6], (C,), ((0, 2),), -0.4, 0.0), -0.5, 0.5)
    w_temporal = bell_draw(seeds[7], (KT, C, C), (KT * C) ** -0.5, 0.125, ((2, 2),))
    gain_two = jnp.clip(1.0 + 0.15 * jax.random.normal(seeds[8], (C,), jnp.float32), 0.25, 1.75)
    shift_two = jnp.clip(jax.random.uniform(seeds[9], (C,), jnp.float32, -0.5, 0.5) * shard_levels(seeds[9], (C,), ((0, 2),), -0.4, 0.0), -0.5, 0.5)
    cotangent = bell_draw(seeds[10], (CLIPS, 2, FRAMES, V, C), 1.0, 6.0, ((0, 16), (4, 2)))
    return dict(features=features, presence=presence, parents=parents, w_spatial=w_spatial, importance=importance, gain_one=gain_one, shift_one=shift_one, w_temporal=w_temporal, gain_two=gain_two, shift_two=shift_two, cotangent=cotangent)


norm_eps = 1e-05
exact_mode = lax.Precision.HIGHEST

@jax.custom_vjp
def low(v):
    return lax.optimization_barrier(v.astype(jnp.bfloat16)).astype(jnp.float32)

@jax.custom_vjp
def low_back(v):
    return v

def low_keep(v):
    return (low(v), None)

def low_pass(kept, grad):
    return (grad,)

def back_keep(v):
    return (v, None)

def back_low(kept, grad):
    return (low(grad),)
low.defvjp(low_keep, low_pass)
low_back.defvjp(back_keep, back_low)

def adjacency(parents):
    joints = parents.shape[0]
    position = jnp.arange(joints, dtype=jnp.int32)
    toward = ((position[None, :] == parents[:, None]) & (position[:, None] != 0)).astype(jnp.float32)
    stacked = jnp.stack([jnp.eye(joints, dtype=jnp.float32), toward, toward.T])
    degree = lax.optimization_barrier(jnp.sum(stacked, axis=(0, 1)))
    return stacked / degree[None, None, :]

def batch_norm(values, present_weight, gain_vec, shift_vec, counted):
    average = lax.optimization_barrier(jnp.sum(values * present_weight, axis=(0, 1, 2, 3))) / counted
    centered = values - average
    variance = lax.optimization_barrier(jnp.sum(centered * centered * present_weight, axis=(0, 1, 2, 3))) / counted
    return centered * lax.rsqrt(variance + norm_eps) * gain_vec + shift_vec

def temporal(activity, weights):
    tap_count = weights.shape[0]
    frames = activity.shape[2]
    half_taps = tap_count // 2
    padded = jnp.pad(activity, ((0, 0), (0, 0), (half_taps, half_taps), (0, 0), (0, 0)))
    running = jnp.zeros(activity.shape[:4] + (weights.shape[2],), jnp.float32)
    for tap_index in range(tap_count):
        window = padded[:, :, tap_index:tap_index + frames]
        running = running + jnp.einsum('bptvc,co->bptvo', window, weights[tap_index], precision=exact_mode)
    return running

def reference(features, presence, parents, w_spatial, importance, gain_one, shift_one, w_temporal, gain_two, shift_two, cotangent):
    present_weight = presence.astype(jnp.float32)[:, :, None, None, None]
    counted = jnp.sum(presence.astype(jnp.float32)) * (FRAMES * V)
    adjacent = adjacency(parents)

    def forward(inputs_full, spatial_weights, edge_weights, gain_a, shift_a, temporal_weights, gain_b, shift_b):
        mixing = adjacent * edge_weights
        spatial = low_back(jnp.einsum('bptvc,cj->bptvj', inputs_full, spatial_weights, precision=exact_mode))
        spatial = spatial.reshape(inputs_full.shape[:4] + (3, C))
        summed = low_back(jnp.einsum('kvw,bptwkc->bptvc', mixing, spatial, precision=exact_mode))
        activity = low(jax.nn.gelu(batch_norm(summed, present_weight, gain_a, shift_a, counted)))
        conv = low_back(temporal(activity, temporal_weights))
        return jax.nn.gelu(batch_norm(conv, present_weight, gain_b, shift_b, counted) + inputs_full)
    primal, backward = jax.vjp(forward, features.astype(jnp.float32), w_spatial.astype(jnp.float32), importance, gain_one, shift_one, w_temporal.astype(jnp.float32), gain_two, shift_two)
    grads = backward(cotangent.astype(jnp.float32))
    return (primal, grads[0], grads[1], grads[2], grads[3], grads[4], grads[5], grads[6], grads[7])
```

```python
import functools

import jax
import jax.numpy as jnp
from jax import lax
from jax.experimental import pallas as pl
from jax.experimental.pallas import tpu as pltpu
from jax.sharding import PartitionSpec as P

norm_eps = 1e-05
exact_mode = lax.Precision.HIGHEST
MESH = pl.DeviceIdType.MESH
TAPS = 9
HALO = TAPS // 2
NB = 8
RW = 2 * NB
G = 4
tanh_scale = 0.7978845608028654
tanh_cubic = 0.044715


def gelu(x):
    t = jnp.tanh(tanh_scale * (x + tanh_cubic * x * x * x))
    return 0.5 * x * (1.0 + t)


def gelu_both(x):
    x2 = x * x
    t = jnp.tanh(tanh_scale * x * (1.0 + tanh_cubic * x2))
    h = 0.5 * (1.0 + t)
    slope = h + 0.5 * x * (1.0 - t * t) * (tanh_scale + (3.0 * tanh_scale * tanh_cubic) * x2)
    return x * h, slope


class Sizes:
    def __init__(self, n_dp, frames, joints, half):
        self.n_dp, self.frames, self.joints, self.half = n_dp, frames, joints, half
        self.chan = 2 * half
        self.blk = -(-frames // (2 * NB))
        self.win = self.blk * NB
        self.pad = 2 * self.win - frames
        self.rows = joints * RW
        self.total = self.blk * self.rows
        self.chips = n_dp // 2
        self.p1 = min(8, self.chips)
        self.p2 = self.chips // self.p1
        cut = self.blk - self.pad
        step = -(-cut // 3)
        self.chunks = [(a, min(a + step, cut)) for a in range(0, cut, step)]
        if self.pad:
            self.chunks.append((cut, self.blk))
        self.locals = [(0, cut)] + ([(cut, self.blk)] if self.pad else [])


def mega(
    z,
    feat,
    cot,
    wt_in,
    ws_in,
    imp,
    par,
    pres,
    g1,
    b1,
    g2,
    b2,
    act_own,
    act_rcv,
    ing_own,
    ing_rcv,
    tg_out,
    sg_out,
    sums_out,
    ig_out,
    xh,
    ct,
    wt,
    ws,
    parts,
    chain,
    mixed,
    summed,
    acth,
    conv,
    gch,
    zz,
    iz,
    gb,
    gb_core,
    gb_low,
    gb_chips,
    gb_far,
    gb_sum,
    gb_pair,
    gb_all,
    sg,
    prm,
    adj,
    edge,
    kin,
    halo_s,
    halo_r,
    arA,
    arB,
    arC,
    sem_l,
    sem_f,
    sem_c,
    sem_a,
    sem_i,
    sem_w,
    sem_h,
    sem_g,
    semA,
    semB,
    semC,
):
    f32, bf = jnp.float32, jnp.bfloat16
    J, C, H, L, R = z.joints, z.chan, z.half, z.blk, z.rows
    s = lax.axis_index("sub")
    dp = lax.axis_index("dp")
    o = 1 - s
    core = lax.rem(dp, 2)
    chip = lax.div(dp, 2)
    c1 = lax.rem(chip, z.p1)
    c2 = lax.div(chip, z.p1)
    partner = (dp, o)

    def peer_a(t):
        return (2 * chip + lax.div(t, 2), lax.rem(t, 2))

    def peer_b(t):
        return (2 * (c2 * z.p1 + t) + core, s)

    def peer_c(t):
        return (2 * (t * z.p1 + c1) + core, s)

    def remote(src, dst, ssem, rsem, dev):
        return pltpu.make_async_remote_copy(
            src_ref=src,
            dst_ref=dst,
            send_sem=ssem,
            recv_sem=rsem,
            device_id=dev,
            device_id_type=MESH,
        )

    def frame_row(w, b, a0, a1):
        at = w * z.win + (b * L + a0)
        if b == NB - 1 and z.pad and a0 >= L - z.pad:
            at = at - w * z.pad
        return at

    local = []
    for which, (src, dst) in enumerate(((feat, xh), (cot, ct))):
        for i, (a0, a1) in enumerate(z.locals):
            for b in range(NB):
                cp = pltpu.make_async_copy(
                    src.at[pl.ds(frame_row(s, b, a0, a1), a1 - a0)],
                    dst.at[s, pl.ds(a0, a1 - a0), :, b],
                    sem_l.at[which, i * NB + b],
                )
                cp.start()
                local.append(cp)
    lw = [
        pltpu.make_async_copy(ws_in, ws.at[:, pl.ds(pl.multiple_of(s * 3 * H, H), 3 * H)], sem_l.at[2, 0]),
        pltpu.make_async_copy(wt_in, wt.at[:, :, pl.ds(pl.multiple_of(s * H, H), H)], sem_l.at[2, 1]),
    ]
    for cp in lw:
        cp.start()
    for i, v in enumerate((g1, b1, g2, b2)):
        prm[s, i : i + 1] = v[...]

    bar = pltpu.get_barrier_semaphore()
    qa = core * 2 + s
    n_peers = 0
    for d in range(1, 4):
        pl.semaphore_signal(bar, inc=1, device_id=peer_a(lax.rem(qa + d, 4)), device_id_type=MESH)
        n_peers += 1
    for d in range(1, z.p1):
        pl.semaphore_signal(bar, inc=1, device_id=peer_b(lax.rem(c1 + d, z.p1)), device_id_type=MESH)
        n_peers += 1
    for d in range(1, z.p2):
        pl.semaphore_signal(bar, inc=1, device_id=peer_c(lax.rem(c2 + d, z.p2)), device_id_type=MESH)
        n_peers += 1
    with jax.named_scope("barrier"):
        pl.semaphore_wait(bar, n_peers)

    slice_rows = H // z.p1
    row0 = pl.multiple_of(core * H + c1 * slice_rows, slice_rows)

    def ws_at(half, r0, n):
        return ws.at[pl.ds(r0, n), pl.ds(pl.multiple_of(half * 3 * H, H), 3 * H)]

    def wt_at(half, r0, n):
        return wt.at[:, pl.ds(r0, n), pl.ds(pl.multiple_of(half * H, H), H)]

    sends = []

    def go(cp):
        cp.start()
        sends.append(cp)
        return cp

    def arrive(dst, rsem):
        remote(dst, dst, rsem, rsem, partner).wait_recv()

    go(remote(prm.at[s], prm.at[s], sem_w.at[0, 0], sem_w.at[1, 0], partner))
    go(remote(ws_in.at[pl.ds(row0, slice_rows)], ws_at(s, row0, slice_rows), sem_w.at[0, 1], sem_w.at[1, 1], partner))
    go(remote(wt_in.at[:, pl.ds(row0, slice_rows)], wt_at(s, row0, slice_rows), sem_w.at[0, 2], sem_w.at[1, 2], partner))

    def send_rows(src, dst, sem, j):
        a0, a1 = z.chunks[j]
        for b in range(NB):
            go(
                remote(
                    src.at[pl.ds(frame_row(o, b, a0, a1), a1 - a0)],
                    dst.at[s, pl.ds(a0, a1 - a0), :, b],
                    sem.at[0, j, b],
                    sem.at[1, j, b],
                    partner,
                )
            )

    def take_rows(dst, sem, j):
        a0, a1 = z.chunks[j]
        for b in range(NB):
            arrive(dst.at[o, pl.ds(a0, a1 - a0), :, b], sem.at[1, j, b])

    n_chunks = len(z.chunks)
    for j in range(n_chunks):
        send_rows(feat, xh, sem_f, j)

    ri = lax.broadcasted_iota(jnp.int32, (J, J), 0)
    ci = lax.broadcasted_iota(jnp.int32, (J, J), 1)
    eye = jnp.where(ri == ci, 1.0, 0.0).astype(f32)
    up = jnp.zeros((J, J), f32)
    down = jnp.zeros((J, J), f32)
    for v in range(1, J):
        pv = par[v]
        up = jnp.where((ri == v) & (ci == pv), 1.0, up)
        down = jnp.where((ci == v) & (ri == pv), 1.0, down)
    degree = jnp.sum(eye + up + down, axis=0, keepdims=True)
    adjacent = [eye / degree, up / degree, down / degree]
    mixing = [adjacent[k] * imp[k] for k in range(3)]
    for k in range(3):
        adj[k] = adjacent[k]
    last = (((1,), (1,)), ((), ()))
    first = (((0,), (0,)), ((), ()))
    wide = jnp.ones((J, C), f32)
    edge[0] = jnp.dot(mixing[0], wide, precision=exact_mode, preferred_element_type=f32)
    edge[1] = jnp.dot(mixing[1], wide, precision=exact_mode, preferred_element_type=f32)
    edge[2] = lax.dot_general(mixing[2], wide, first, precision=exact_mode, preferred_element_type=f32)

    def kin_body(v, _):
        pv = par[v]
        sibling = jnp.int32(0)
        child = jnp.int32(0)
        for w in range(J - 1, 0, -1):
            pw_ = par[w]
            sibling = jnp.where((pw_ == pv) & (w > v), w, sibling)
            child = jnp.where(pw_ == v, w, child)
        kin[0, v] = sibling
        kin[1, v] = child
        return 0

    lax.fori_loop(0, J, kin_body, 0)
    chain[0] = jnp.zeros((RW, C), f32)

    for i, at in ((0, ws_at), (1, wt_at)):
        arrive(at(o, row0, slice_rows), sem_w.at[1, 1 + i])
        for d in range(1, z.p1):
            t = lax.rem(c1 + d, z.p1)
            go(
                remote(
                    at(o, row0, slice_rows),
                    at(o, row0, slice_rows),
                    sem_w.at[0, 4 + i * 16 + d],
                    sem_w.at[1, 4 + i * 16 + d],
                    peer_b(t),
                )
            )
    for i, at in ((0, ws_at), (1, wt_at)):
        for d in range(1, z.p1):
            t = lax.rem(c1 + z.p1 - d, z.p1)
            arrive(
                at(o, pl.multiple_of(core * H + t * slice_rows, slice_rows), slice_rows),
                sem_w.at[1, 4 + i * 16 + d],
            )
        mine = pl.multiple_of(core * H, H)
        go(remote(at(o, mine, H), at(o, mine, H), sem_w.at[0, 36 + i], sem_w.at[1, 36 + i], (2 * chip + 1 - core, s)))
    theirs = pl.multiple_of((1 - core) * H, H)
    arrive(ws_at(o, theirs, H), sem_w.at[1, 36])
    for cp in lw:
        cp.wait()
    arrive(prm.at[o], sem_w.at[1, 0])
    p0 = pres[0, 0].astype(f32)
    p1 = pres[0, 1].astype(f32)
    ri16 = lax.broadcasted_iota(jnp.int32, (RW, C), 0)
    pw = jnp.where((ri16 & 1) == 0, p0, p1).astype(f32)
    tail = jnp.where(ri16 >= RW - 2, 1.0, 0.0).astype(f32)
    side = s.astype(f32)

    def real(a):
        late = jnp.where(a >= L - z.pad, side, 0.0) if z.pad else 0.0
        return 1.0 - tail * late

    def tiles(x):
        return x.reshape(-1, RW, C)

    def times(x, m):
        return (tiles(x) * m[None]).reshape(x.shape)

    def down_rows(x):
        return jnp.sum(tiles(x), axis=0)

    def row_sum(x):
        return jnp.sum(x, axis=0, keepdims=True)

    def param(i):
        return jnp.concatenate([prm[0, i : i + 1], prm[1, i : i + 1]], axis=1)

    def whole(ref, a):
        return jnp.concatenate([ref[0, a].reshape(R, H), ref[1, a].reshape(R, H)], axis=1)

    def put(ref, a, value):
        for h in range(2):
            ref[h, a] = value[:, h * H : (h + 1) * H].reshape(J, NB, 2, H)

    def spread(buf, sem, r, q, n, peer, val):
        buf[r, q] = val
        for d in range(1, n):
            go(remote(buf.at[r, q], buf.at[r, q], sem.at[0, r, d], sem.at[1, r, d], peer(lax.rem(q + d, n))))

    def gather(buf, sem, r, q, n):
        for d in range(1, n):
            arrive(buf.at[r, lax.rem(q + n - d, n)], sem.at[1, r, d])
        return [buf[r, i] for i in range(n)]

    def add_up(parts):
        t = parts[0]
        for x in parts[1:]:
            t = t + x
        return t

    def merge(parts):
        n = add_up([x[0:1] for x in parts])
        below = jnp.maximum(n, 1.0)
        mean = add_up([x[0:1] * x[1:2] for x in parts]) / below
        spread_up = add_up([x[2:3] + x[0:1] * (x[1:2] - mean) * (x[1:2] - mean) for x in parts])
        return jnp.concatenate([n, mean, spread_up, jnp.zeros((5, C), f32)], axis=0)

    def all_start(r, val):
        spread(arA, semA, r, qa, 4, peer_a, val)

    def all_next(r, join):
        val = join(gather(arA, semA, r, qa, 4))
        if z.p1 > 1:
            spread(arB, semB, r, c1, z.p1, peer_b, val)
        else:
            arB[r, 0] = val

    def all_end(r, join):
        val = join(gather(arB, semB, r, c1, z.p1))
        if z.p2 > 1:
            spread(arC, semC, r, c2, z.p2, peer_c, val)
            val = join(gather(arC, semC, r, c2, z.p2))
        return val

    def moments(val_k, s1, s2):
        n = (p0 + p1) * (z.win - z.pad * side) * J
        below = jnp.maximum(n, 1.0)
        s1, s2 = row_sum(s1), row_sum(s2)
        return jnp.concatenate(
            [jnp.zeros((1, C), f32) + n, val_k + s1 / below, s2 - s1 * s1 / below, jnp.zeros((5, C), f32)], axis=0
        )

    zero16 = jnp.zeros((RW, C), f32)
    zero1 = jnp.zeros((1, C), f32)

    def link(value, k):
        for v in range(J - 1, 0, -1):
            chain[v] = value(v) * edge[k, v : v + 1] + chain[kin[0, v]]

    def spatial_body(a, carry):
        k_shift, s1, s2 = carry
        f = whole(xh, a)
        for k in range(3):
            parts[k] = jnp.dot(f, ws[:, k * C : (k + 1) * C], preferred_element_type=f32).reshape(J, RW, C)
        link(lambda v: parts[2, v], 2)
        for v in range(J):
            t = parts[0, v] * edge[0, v : v + 1] + chain[kin[1, v]]
            if v:
                t = t + parts[1, par[v]] * edge[1, v : v + 1]
            summed[a, v] = t
        t = summed[a].reshape(R, C)
        k_shift = jnp.where(a == 0, row_sum(t) * (1.0 / R), k_shift)
        w = pw * real(a)
        d = tiles(t - k_shift)
        wd = d * w[None]
        return k_shift, s1 + jnp.sum(wd, axis=0), s2 + jnp.sum(wd * d, axis=0)

    carry = (zero1, zero16, zero16)
    n_local = len(z.locals) * NB
    for cp in local[:n_local]:
        cp.wait()
    for j, (a0, a1) in enumerate(z.chunks):
        with jax.named_scope("features_wait"):
            take_rows(xh, sem_f, j)
        if j == n_chunks - 1:
            for i in range(n_chunks):
                send_rows(cot, ct, sem_c, i)
        with jax.named_scope("spatial"):
            carry = lax.fori_loop(a0, a1, spatial_body, carry)

    lane = lax.broadcasted_iota(jnp.int32, (64, R), 1)
    line = lax.broadcasted_iota(jnp.int32, (64, R), 0)
    off = (RW - 2) * o
    pick = jnp.where(
        (lane == lax.shift_right_logical(line, 1) * RW + off + (line & 1)) & (line < 2 * J), 1.0, 0.0
    ).astype(bf)
    edge_a = (L - HALO) * o

    def halo_out(ref, slot, i):
        for h in range(HALO):
            halo_s[slot, h] = jnp.dot(pick, ref(edge_a + h).astype(bf), preferred_element_type=f32).astype(bf)
        go(remote(halo_s.at[slot], halo_r.at[slot], sem_h.at[0, i], sem_h.at[1, i], partner))

    def halo_in(slot, i):
        arrive(halo_r.at[slot], sem_h.at[1, i])

    row_in = lax.broadcasted_iota(jnp.int32, (R, C), 0) & (RW - 1)
    fside = 1.0 - side

    def fill_halo(buf, fresh):
        for h in range(HALO):
            extra = lax.dot_general(pick, fresh(h), first, preferred_element_type=f32)
            lower = pltpu.roll(buf[L + h].reshape(R, C).astype(f32), 2, 0)
            lower = jnp.where(row_in < 2, extra * side, lower)
            buf[h] = tiles(lower.astype(bf))
            upper = pltpu.roll(buf[HALO + h].reshape(R, C).astype(f32), R - 2, 0)
            upper = jnp.where(row_in >= RW - 2, extra * fside, upper)
            buf[HALO + L + h] = tiles(upper.astype(bf))

    halo_out(lambda a: summed[a].reshape(R, C), 0, 0)
    all_start(0, moments(*carry))
    with jax.named_scope("st1"):
        all_next(0, merge)
        st1 = all_end(0, merge)
    count = jnp.maximum(st1[0:1], 1.0)
    mean1 = st1[1:2]
    rstd1 = lax.rsqrt(st1[2:3] / count + norm_eps)
    gain1, shift1 = param(0), param(1)
    scale1 = rstd1 * gain1

    def act_body(a, _):
        t = gelu((summed[a].reshape(R, C) - mean1) * scale1 + shift1)
        acth[a + HALO] = tiles(times(t, real(a)).astype(bf))
        return 0

    with jax.named_scope("act"):
        lax.fori_loop(0, L, act_body, 0)
    halo_in(0, 0)
    fill_halo(acth, lambda h: gelu((halo_r[0, h].astype(f32) - mean1) * scale1 + shift1).astype(bf))

    arrive(wt_at(o, theirs, H), sem_w.at[1, 37])

    def conv_block(a0, n, carry):
        k_shift, s1, s2 = carry
        t = jnp.zeros((n * R, C), f32)
        for tap in range(TAPS):
            t = t + jnp.dot(acth[pl.ds(a0 + tap, n)].reshape(n * R, C), wt[tap], preferred_element_type=f32)
        conv[pl.ds(a0, n)] = t.reshape(n, R, C)
        k_shift = jnp.where(a0 == 0, row_sum(t[:R]) * (1.0 / R), k_shift)
        for i in range(n):
            w = pw * real(a0 + i)
            d = tiles(t[i * R : (i + 1) * R] - k_shift)
            wd = d * w[None]
            s1 = s1 + jnp.sum(wd, axis=0)
            s2 = s2 + jnp.sum(wd * d, axis=0)
        return k_shift, s1, s2

    def blocks(fun, carry):
        carry = lax.fori_loop(0, L // G, lambda i, c: fun(i * G, G, c), carry)
        if L % G:
            carry = fun(L // G * G, L % G, carry)
        return carry

    with jax.named_scope("conv"):
        carry = blocks(conv_block, (zero1, zero16, zero16))
    all_start(1, moments(*carry))
    with jax.named_scope("st2"):
        all_next(1, merge)
        st2 = all_end(1, merge)
    mean2 = st2[1:2]
    rstd2 = lax.rsqrt(st2[2:3] / count + norm_eps)
    gain2, shift2 = param(2), param(3)

    for cp in local[n_local:]:
        cp.wait()

    def out_body(a, carry):
        sa, sb = carry
        normed = (conv[a] - mean2) * rstd2
        level = normed * gain2 + shift2 + whole(xh, a).astype(f32)
        value, slope = gelu_both(level)
        put(zz, a, value.astype(bf))
        gp = whole(ct, a).astype(f32) * slope
        conv[a] = gp
        put(ct, a, normed.astype(bf))
        gm = tiles(gp) * real(a)[None]
        return sa + jnp.sum(gm, axis=0), sb + jnp.sum(gm * tiles(normed), axis=0)

    carry = (zero16, zero16)
    outs = []

    def ship(buf, own, rcv, sem, j):
        a0, a1 = z.chunks[j]
        at = pl.ds(a0, a1 - a0)
        go(remote(buf.at[o, at], rcv.at[at], sem.at[0, j], sem.at[1, j], partner))
        cp = pltpu.make_async_copy(buf.at[s, at], own.at[at], sem.at[2, j])
        cp.start()
        outs.append(cp)

    for j, (a0, a1) in enumerate(z.chunks):
        with jax.named_scope("cotangent_wait"):
            take_rows(ct, sem_c, j)
        with jax.named_scope("level_two"):
            carry = lax.fori_loop(a0, a1, out_body, carry)
        ship(zz, act_own, act_rcv, sem_a, j)

    halo_out(lambda a: conv[a], 1, 1)
    halo_out(lambda a: whole(ct, a), 2, 2)
    pad6 = jnp.zeros((6, C), f32)
    all_start(2, jnp.concatenate([row_sum(carry[0]), row_sum(carry[1]), pad6], axis=0))
    with jax.named_scope("sum2"):
        all_next(2, add_up)
        sum2 = all_end(2, add_up)
    out_scale = gain2 * rstd2
    out_shift = out_scale * sum2[0:1] / count
    out_slope = out_scale * sum2[1:2] / count

    def back(grad, x, scale, shift, slope):
        corr = tiles(x * slope + shift) * pw[None]
        return grad * scale - corr.reshape(grad.shape)

    def gconv_body(a, _):
        gp = conv[a]
        t = back(gp, whole(ct, a).astype(f32), out_scale, out_shift, out_slope)
        gch[a + HALO] = tiles(times(t, real(a)).astype(bf))
        put(ct, a, gp.astype(bf))
        return 0

    with jax.named_scope("gconv"):
        lax.fori_loop(0, L, gconv_body, 0)
    halo_in(1, 1)
    halo_in(2, 2)
    fill_halo(
        gch,
        lambda h: back(halo_r[1, h].astype(f32), halo_r[2, h].astype(f32), out_scale, out_shift, out_slope).astype(bf),
    )

    def gact_block(a0, n, carry):
        sa, sb = carry
        t = jnp.zeros((n * R, C), f32)
        for tap in range(TAPS):
            t = t + lax.dot_general(
                gch[pl.ds(a0 + TAPS - 1 - tap, n)].reshape(n * R, C), wt[tap], last, preferred_element_type=f32
            )
        for i in range(n):
            centred = summed[a0 + i].reshape(R, C) - mean1
            _, slope = gelu_both(centred * scale1 + shift1)
            gl = t[i * R : (i + 1) * R] * slope
            conv[a0 + i] = gl
            gm = tiles(gl) * real(a0 + i)[None]
            sa = sa + jnp.sum(gm, axis=0)
            sb = sb + jnp.sum(gm * tiles(centred * rstd1), axis=0)
        return sa, sb

    with jax.named_scope("grad_act"):
        carry = blocks(gact_block, (zero16, zero16))
    all_start(3, jnp.concatenate([row_sum(carry[0]), row_sum(carry[1]), pad6], axis=0))
    with jax.named_scope("sum1"):
        all_next(3, add_up)

    def tap_body(tap, _):
        t = lax.dot_general(
            acth[pl.ds(tap, L)].reshape(z.total, C),
            gch[pl.ds(HALO, L)].reshape(z.total, C),
            first,
            preferred_element_type=f32,
        )
        gb[0, tap] = t[:, :H]
        gb[1, tap] = t[:, H:]
        return 0

    with jax.named_scope("tap_grad"):
        lax.fori_loop(0, TAPS, tap_body, 0)
    with jax.named_scope("sum1_wait"):
        sum1 = all_end(3, add_up)
    in_scale = gain1 * rstd1
    in_shift = in_scale * sum1[0:1] / count
    in_slope = in_scale * rstd1 * sum1[1:2] / count

    neighbour = (2 * chip + 1 - core, s)
    core_rows = pl.multiple_of(core * H, H)
    other_rows = pl.multiple_of((1 - core) * H, H)
    chip_rows = pl.multiple_of(c1 * slice_rows, slice_rows)
    spans = (pl.ds(0, TAPS), pl.ds(TAPS, 3))

    def grad_core(i):
        cut = (slice(None), spans[i])
        go(
            remote(
                gb.at[(*cut, pl.ds(other_rows, H))], gb_core.at[cut], sem_g.at[0, i, 0], sem_g.at[1, i, 0], neighbour
            )
        )

    def grad_chips(i):
        cut = (slice(None), spans[i])
        arrive(gb_core.at[cut], sem_g.at[1, i, 0])
        total = gb[(*cut, pl.ds(core_rows, H))] + gb_core[cut]
        if z.p1 == 1:
            gb_sum[cut] = total
            return
        gb_low[cut] = total.astype(bf)
        for d in range(1, z.p1):
            t = lax.rem(c1 + d, z.p1)
            go(
                remote(
                    gb_low.at[(*cut, pl.ds(pl.multiple_of(t * slice_rows, slice_rows), slice_rows))],
                    gb_chips.at[(c1, *cut)],
                    sem_g.at[0, i, d],
                    sem_g.at[1, i, d],
                    peer_b(t),
                )
            )

    def grad_pair(i):
        cut = (slice(None), spans[i])
        if z.p1 > 1:
            gb_chips[(c1, *cut)] = gb_low[(*cut, pl.ds(chip_rows, slice_rows))]
            for d in range(1, z.p1):
                arrive(gb_chips.at[(lax.rem(c1 + z.p1 - d, z.p1), *cut)], sem_g.at[1, i, d])
            gb_sum[cut] = add_up([gb_chips[(p, *cut)].astype(f32) for p in range(z.p1)])
        if z.p2 > 1:
            gb_far[(c2, *cut)] = gb_sum[cut]
            for d in range(1, z.p2):
                t = lax.rem(c2 + d, z.p2)
                go(
                    remote(
                        gb_far.at[(c2, *cut)],
                        gb_far.at[(c2, *cut)],
                        sem_g.at[0, i, 24 + d],
                        sem_g.at[1, i, 24 + d],
                        peer_c(t),
                    )
                )
            for d in range(1, z.p2):
                arrive(gb_far.at[(lax.rem(c2 + z.p2 - d, z.p2), *cut)], sem_g.at[1, i, 24 + d])
            gb_sum[cut] = add_up([gb_far[(p, *cut)] for p in range(z.p2)])
        go(remote(gb_sum.at[o, spans[i]], gb_pair.at[spans[i]], sem_g.at[0, i, 8], sem_g.at[1, i, 8], partner))

    def grad_back(i):
        arrive(gb_pair.at[spans[i]], sem_g.at[1, i, 8])
        mine = gb_sum[s, spans[i]]
        other = gb_pair[spans[i]]
        own = pl.multiple_of(core_rows + chip_rows, slice_rows)
        gb_all[spans[i], pl.ds(own, slice_rows)] = mine + other
        at = gb_all.at[spans[i], pl.ds(own, slice_rows)]
        for d in range(1, z.p1):
            t = lax.rem(c1 + d, z.p1)
            go(remote(at, at, sem_g.at[0, i, 8 + d], sem_g.at[1, i, 8 + d], peer_b(t)))

    def grad_last(i):
        for d in range(1, z.p1):
            t = lax.rem(c1 + z.p1 - d, z.p1)
            at = pl.multiple_of(core_rows + t * slice_rows, slice_rows)
            arrive(gb_all.at[spans[i], pl.ds(at, slice_rows)], sem_g.at[1, i, 8 + d])
        at = gb_all.at[spans[i], pl.ds(core_rows, H)]
        go(remote(at, at, sem_g.at[0, i, 16], sem_g.at[1, i, 16], neighbour))

    def grad_done(i):
        arrive(gb_all.at[spans[i], pl.ds(other_rows, H)], sem_g.at[1, i, 16])

    grad_core(0)

    def input_body(a, _):
        gs = back(conv[a], summed[a].reshape(R, C) - mean1, in_scale, in_shift, in_slope)
        gs = times(gs, real(a)).astype(bf)
        gch[a + HALO] = tiles(gs)
        parts[0] = gs.astype(f32).reshape(J, RW, C)
        link(lambda v: parts[0, v], 1)
        for w in range(J):
            at = slice(w * RW, (w + 1) * RW)
            mixed[0, at] = (parts[0, w] * edge[0, w : w + 1]).astype(bf)
            mixed[1, at] = chain[kin[1, w]].astype(bf)
            mixed[2, at] = (parts[0, par[w]] * edge[2, w : w + 1]).astype(bf)
        t = whole(ct, a).astype(f32)
        for k in range(3):
            t = t + lax.dot_general(mixed[k], ws[:, k * C : (k + 1) * C], last, preferred_element_type=f32)
        put(iz, a, t.astype(bf))
        return 0

    for j, (a0, a1) in enumerate(z.chunks):
        with jax.named_scope("input_grad"):
            lax.fori_loop(a0, a1, input_body, 0)
        ship(iz, ing_own, ing_rcv, sem_i, j)
        with jax.named_scope("grad_reduce"):
            if j == 0:
                grad_chips(0)
            if j == n_chunks - 1:
                grad_pair(0)

    def edge_rows_f(v):
        return jnp.concatenate(
            [xh[0, :, pl.ds(v, 1)].reshape(L * RW, H), xh[1, :, pl.ds(v, 1)].reshape(L * RW, H)], axis=1
        )

    def edge_rows_g(v):
        return gch[pl.ds(HALO, L), pl.ds(v, 1)].reshape(L * RW, C)

    sg[...] = jnp.zeros_like(sg)

    def edge_body(v, acc):
        pv = par[v]
        hot = jnp.where(lax.broadcasted_iota(jnp.int32, (8, C), 1) == v, 1.0, 0.0)
        kind = lax.broadcasted_iota(jnp.int32, (8, C), 0)
        far = jnp.where(v > 0, 1.0, 0.0)
        f_v, g_v = edge_rows_f(v), edge_rows_g(v)
        f_p, g_p = edge_rows_f(pv), edge_rows_g(pv)
        for k, (fx, gx, on) in enumerate(((f_v, g_v, 1.0), (f_p, g_v, far), (f_v, g_p, far))):
            prod = lax.dot_general(fx, gx, first, preferred_element_type=f32)
            sg[k] = sg[k] + prod * edge[k, pl.ds(v, 1)]
            dot = jnp.sum(row_sum(prod * ws[:, k * C : (k + 1) * C].astype(f32)), axis=1, keepdims=True)
            acc = acc + jnp.where(kind == k, hot, 0.0) * (dot * on)
        return acc

    with jax.named_scope("edges"):
        dvec = lax.fori_loop(0, J, edge_body, jnp.zeros((8, C), f32))
    for j in range(6):
        k, h = j // 2, j % 2
        gb[j // 3, TAPS + j % 3] = sg[k, :, h * H : (h + 1) * H]
    grad_core(1)
    all_start(4, dvec)
    with jax.named_scope("grad_reduce"):
        grad_back(0)
        grad_chips(1)
        all_next(4, add_up)
        grad_pair(1)
        grad_back(1)
        grad_last(0)
        dvec = all_end(4, add_up)
        grad_last(1)
    for k in range(3):
        per_edge = dvec[k : k + 1, :J]
        if k == 1:
            per_edge = lax.dot_general(
                eye, jnp.broadcast_to(per_edge, (J, J)), last, precision=exact_mode, preferred_element_type=f32
            )
        ig_out[k] = adj[k] * per_edge
    for i, row in enumerate((sum1[1:2], sum1[0:1], sum2[1:2], sum2[0:1])):
        sums_out[i : i + 1] = jnp.where(s == 0, row[:, :H], row[:, H:])
    sums_out[4:8] = jnp.zeros((4, H), f32)
    with jax.named_scope("grad_reduce_end"):
        grad_done(0)
        grad_done(1)
        last_out = [pltpu.make_async_copy(gb_all.at[pl.ds(0, TAPS)], tg_out, sem_l.at[2, 2])]
        for j in range(3):
            last_out.append(
                pltpu.make_async_copy(gb_all.at[TAPS + j], sg_out.at[:, pl.ds(j * H, H)], sem_l.at[2, 3 + j])
            )
        for cp in last_out:
            cp.start()

    with jax.named_scope("last_waits"):
        for j in range(n_chunks):
            a0, a1 = z.chunks[j]
            at = pl.ds(a0, a1 - a0)
            arrive(act_rcv.at[at], sem_a.at[1, j])
            arrive(ing_rcv.at[at], sem_i.at[1, j])
        for cp in outs + last_out:
            cp.wait()
        for cp in sends:
            cp.wait_send()


def finish(
    z,
    act_own,
    act_rcv,
    ing_own,
    ing_rcv,
    tg_in,
    sg_in,
    sums_in,
    ig_in,
    act_out,
    ing_out,
    tg_out,
    sg_out,
    r0,
    r1,
    r2,
    r3,
    ig_out,
    low,
    full,
    tg,
    sg,
    sem_in,
    sem_out,
):
    J, L = z.joints, z.blk
    s = lax.axis_index("sub")
    jobs = [(act_own, act_out, s), (ing_own, ing_out, s), (act_rcv, act_out, 1 - s), (ing_rcv, ing_out, 1 - s)]
    ins = []
    for i, (src, _, _) in enumerate(jobs):
        cp = pltpu.make_async_copy(src, low.at[i], sem_in.at[i])
        cp.start()
        ins.append(cp)
    grads = []
    for i, (src, mid, dst) in enumerate(((tg_in, tg, tg_out), (sg_in, sg, sg_out))):
        cp = pltpu.make_async_copy(src, mid, sem_in.at[4 + i])
        cp.start()
        grads.append((cp, pltpu.make_async_copy(mid, dst, sem_in.at[6 + i])))
    for i, r in enumerate((r0, r1, r2, r3)):
        r[...] = sums_in[i : i + 1]
    ig_out[...] = ig_in[...]
    cut = L - z.pad

    def pieces(i, dst, w):
        for part, (a0, a1) in enumerate(z.locals):
            for b in range(NB):
                cp = pltpu.make_async_copy(
                    full.at[i, pl.ds(a0, a1 - a0), :, b],
                    dst.at[pl.ds(w * z.win + b * L + a0, a1 - a0)],
                    sem_out.at[i, part, b],
                )
                yield part == 1 and b == NB - 1, cp

    for i, (_, dst, w) in enumerate(jobs):
        ins[i].wait()

        def body(a, _, i=i):
            value = low[i, a].reshape(z.rows, z.half).astype(jnp.float32)
            full[i, a] = value.reshape(J, NB, 2, z.half)
            return 0

        lax.fori_loop(0, L, body, 0)
        for beyond, cp in pieces(i, dst, w):
            if beyond:
                pl.when(w == 0)(cp.start)
            else:
                cp.start()
    for cp_in, cp_out in grads:
        cp_in.wait()
        cp_out.start()
    for _, cp_out in grads:
        cp_out.wait()
    for i, (_, dst, w) in enumerate(jobs):
        for beyond, cp in pieces(i, dst, w):
            if beyond:
                pl.when(w == 0)(cp.wait)
            else:
                cp.wait()


def block(
    n_dp, features, presence, parents, w_spatial, importance, gain_one, shift_one, w_temporal, gain_two, shift_two, cotangent
):
    _, _, frames, joints, half = features.shape
    z = Sizes(n_dp, frames, joints, half)
    f32, bf = jnp.float32, jnp.bfloat16
    C, H, L, R, J = z.chan, z.half, z.blk, z.rows, z.joints

    def natural(x):
        return x.transpose(0, 2, 3, 1, 4).reshape(frames, joints, 2, half)

    any_, vmem, smem = (pl.BlockSpec(memory_space=m) for m in (pl.ANY, pltpu.VMEM, pltpu.SMEM))
    blocked = (L, J, NB, 2, H)
    sds = jax.ShapeDtypeStruct
    VM, DMA = pltpu.VMEM, pltpu.SemaphoreType.DMA
    nch = len(z.chunks)
    outs = pl.pallas_call(
        functools.partial(mega, z),
        name="graph_conv_block",
        out_shape=[sds(blocked, bf)] * 4
        + [sds((TAPS, C, H), f32), sds((C, 3 * H), f32), sds((8, H), f32), sds((3, J, J), f32)],
        in_specs=[any_] * 4 + [vmem, smem, smem] + [vmem] * 4,
        out_specs=[any_] * 6 + [vmem] * 2,
        scratch_shapes=[
            VM((2,) + blocked, bf),
            VM((2,) + blocked, bf),
            VM((TAPS, C, C), bf),
            VM((C, 3 * C), bf),
            VM((3, J, RW, C), f32),
            VM((J, RW, C), f32),
            VM((3, R, C), bf),
            VM((L, J, RW, C), f32),
            VM((L + 2 * HALO, J, RW, C), bf),
            VM((L, R, C), f32),
            VM((L + 2 * HALO, J, RW, C), bf),
            VM((2,) + blocked, bf),
            VM((2,) + blocked, bf),
            VM((2, TAPS + 3, C, H), f32),
            VM((2, TAPS + 3, H, H), f32),
            VM((2, TAPS + 3, H, H), bf),
            VM((z.p1, 2, TAPS + 3, H // z.p1, H), bf),
            VM((z.p2, 2, TAPS + 3, H // z.p1, H), f32),
            VM((2, TAPS + 3, H // z.p1, H), f32),
            VM((TAPS + 3, H // z.p1, H), f32),
            VM((TAPS + 3, C, H), f32),
            VM((3, C, C), f32),
            VM((2, 8, H), f32),
            VM((3, J, J), f32),
            VM((3, J, C), f32),
            pltpu.SMEM((2, J), jnp.int32),
            VM((3, HALO, 64, C), bf),
            VM((3, HALO, 64, C), bf),
            VM((5, 4, 8, C), f32),
            VM((5, z.p1, 8, C), f32),
            VM((5, max(z.p2, 2), 8, C), f32),
            DMA((3, 2 * NB)),
            DMA((2, nch, NB)),
            DMA((2, nch, NB)),
            DMA((3, nch)),
            DMA((3, nch)),
            DMA((2, 40)),
            DMA((2, 4)),
            DMA((2, 2, 32)),
            DMA((2, 5, 4)),
            DMA((2, 5, z.p1)),
            DMA((2, 5, max(z.p2, 2))),
        ],
        compiler_params=pltpu.CompilerParams(
            collective_id=0, has_side_effects=True, vmem_limit_bytes=62 * 2**20
        ),
    )(
        natural(features),
        natural(cotangent),
        w_temporal,
        w_spatial,
        importance,
        parents,
        presence,
        *(v.reshape(1, H) for v in (gain_one, shift_one, gain_two, shift_two)),
    )
    act, ing, tg, sg, r0, r1, r2, r3, ig = pl.pallas_call(
        functools.partial(finish, z),
        name="natural_order",
        out_shape=[sds((frames, joints, 2, H), f32)] * 2
        + [sds((TAPS, C, H), f32), sds((C, 3 * H), f32)]
        + [sds((1, H), f32)] * 4
        + [sds((3, J, J), f32)],
        in_specs=[any_] * 6 + [vmem] * 2,
        out_specs=[any_] * 4 + [vmem] * 5,
        scratch_shapes=[
            VM((4,) + blocked, bf),
            VM((4,) + blocked, f32),
            VM((TAPS, C, H), f32),
            VM((C, 3 * H), f32),
            DMA((8,)),
            DMA((4, 2, NB)),
        ],
        compiler_params=pltpu.CompilerParams(vmem_limit_bytes=60 * 2**20),
    )(*outs)

    def back(x):
        return x.reshape(1, frames, joints, 2, half).transpose(0, 3, 1, 2, 4)

    return (
        back(act),
        back(ing),
        sg,
        ig,
        *(r.reshape(H) for r in (r0, r1)),
        tg,
        *(r.reshape(H) for r in (r2, r3)),
    )


def solution(mesh):
    in_specs = (
        P("dp", None, None, None, "sub"),
        P("dp", None),
        P(),
        P(None, "sub"),
        P(),
        P("sub"),
        P("sub"),
        P(None, None, "sub"),
        P("sub"),
        P("sub"),
        P("dp", None, None, None, "sub"),
    )
    out_specs = (
        P("dp", None, None, None, "sub"),
        P("dp", None, None, None, "sub"),
        P(None, "sub"),
        P(),
        P("sub"),
        P("sub"),
        P(None, None, "sub"),
        P("sub"),
        P("sub"),
    )
    return jax.shard_map(
        functools.partial(block, mesh.shape["dp"]), mesh=mesh, in_specs=in_specs, out_specs=out_specs, check_vma=False
    )
```

```python
import functools

import jax
import jax.numpy as jnp
from jax import lax
from jax.experimental import pallas as pl
from jax.experimental.pallas import tpu as pltpu
from jax.sharding import PartitionSpec as P

norm_eps = 1e-05
exact_mode = lax.Precision.HIGHEST
MESH = pl.DeviceIdType.MESH
TAPS = 9
HALO = TAPS // 2
NB = 8
RW = 2 * NB
G = 4
tanh_scale = 0.7978845608028654
tanh_cubic = 0.044715


def gelu(x):
    t = jnp.tanh(tanh_scale * (x + tanh_cubic * x * x * x))
    return 0.5 * x * (1.0 + t)


def gelu_both(x):
    x2 = x * x
    t = jnp.tanh(tanh_scale * x * (1.0 + tanh_cubic * x2))
    h = 0.5 * (1.0 + t)
    slope = h + 0.5 * x * (1.0 - t * t) * (tanh_scale + (3.0 * tanh_scale * tanh_cubic) * x2)
    return x * h, slope


class Sizes:
    def __init__(self, n_dp, frames, joints, half):
        self.n_dp, self.frames, self.joints, self.half = n_dp, frames, joints, half
        self.chan = 2 * half
        self.blk = -(-frames // (2 * NB))
        self.win = self.blk * NB
        self.pad = 2 * self.win - frames
        self.rows = joints * RW
        self.total = self.blk * self.rows
        self.chips = n_dp // 2
        self.p1 = 8
        self.p2 = self.chips // self.p1
        self.quads = n_dp // 4
        self.q1 = 4
        self.q2 = self.quads // self.q1
        cut = self.blk - self.pad
        step = -(-cut // 3)
        self.chunks = [(a, min(a + step, cut)) for a in range(0, cut, step)]
        if self.pad:
            self.chunks.append((cut, self.blk))
        self.locals = [(0, cut)] + ([(cut, self.blk)] if self.pad else [])


def mega(
    z,
    feat,
    cot,
    wt_in,
    ws_in,
    imp,
    par,
    pres,
    g1,
    b1,
    g2,
    b2,
    act_own,
    act_rcv,
    ing_own,
    ing_rcv,
    tg_out,
    sg_out,
    sums_out,
    ig_out,
    xh,
    ct,
    wt,
    ws,
    parts,
    chain,
    mixed,
    summed,
    acth,
    conv,
    gch,
    zz,
    iz,
    gb,
    gb_core,
    gb_low,
    gb_chips,
    gb_far,
    gb_sum,
    gb_pair,
    gb_all,
    sg,
    prm,
    adj,
    edge,
    kin,
    halo_s,
    halo_m,
    halo_r,
    arA,
    arB,
    arC,
    arD,
    sem_l,
    sem_f,
    sem_c,
    sem_a,
    sem_i,
    sem_w,
    sem_h,
    sem_g,
    semA,
    semB,
    semC,
    semD,
):
    f32, bf = jnp.float32, jnp.bfloat16
    J, C, H, L, R = z.joints, z.chan, z.half, z.blk, z.rows
    s = lax.axis_index("sub")
    dp = lax.axis_index("dp")
    o = 1 - s
    core = lax.rem(dp, 2)
    chip = lax.div(dp, 2)
    c1 = lax.rem(chip, z.p1)
    c2 = lax.div(chip, z.p1)
    partner = (dp, o)

    quad = lax.div(dp, 4)
    q0 = lax.rem(dp, 4)
    q1 = lax.rem(quad, z.q1)
    q2 = lax.div(quad, z.q1)
    flip = dp + 4 - 8 * lax.rem(quad, 2)
    across = (flip, o)
    beside = (flip, s)

    def peer_b(t):
        return (2 * (c2 * z.p1 + t) + core, s)

    def peer_c(t):
        return (2 * (t * z.p1 + c1) + core, s)

    def peer_0(t):
        return (4 * quad + t, s)

    def peer_1(t):
        return (4 * (q2 * z.q1 + t) + q0, s)

    def peer_2(t):
        return (4 * (t * z.q1 + q1) + q0, s)

    def other_chip(t):
        return t + 2 - 4 * lax.rem(lax.div(t, 2), 2)

    def owned(t):
        return t + s * (other_chip(t) - t)

    def remote(src, dst, ssem, rsem, dev):
        return pltpu.make_async_remote_copy(
            src_ref=src,
            dst_ref=dst,
            send_sem=ssem,
            recv_sem=rsem,
            device_id=dev,
            device_id_type=MESH,
        )

    def frame_row(w, b, a0, a1):
        at = w * z.win + (b * L + a0)
        if b == NB - 1 and z.pad and a0 >= L - z.pad:
            at = at - w * z.pad
        return at

    local = []
    for which, (src, dst) in enumerate(((feat, xh), (cot, ct))):
        for i, (a0, a1) in enumerate(z.locals):
            for b in range(NB):
                cp = pltpu.make_async_copy(
                    src.at[pl.ds(frame_row(s, b, a0, a1), a1 - a0)],
                    dst.at[s, pl.ds(a0, a1 - a0), :, b],
                    sem_l.at[which, i * NB + b],
                )
                cp.start()
                local.append(cp)
    lw = [
        pltpu.make_async_copy(ws_in, ws.at[:, pl.ds(pl.multiple_of(s * 3 * H, H), 3 * H)], sem_l.at[2, 0]),
        pltpu.make_async_copy(wt_in, wt.at[:, :, pl.ds(pl.multiple_of(s * H, H), H)], sem_l.at[2, 1]),
    ]
    for cp in lw:
        cp.start()
    for i, v in enumerate((g1, b1, g2, b2)):
        prm[s, i : i + 1] = v[...]

    bar = pltpu.get_barrier_semaphore()
    greeted = [partner, across, (2 * chip + 1 - core, s)]
    greeted += [peer_b(lax.rem(c1 + d, z.p1)) for d in range(1, z.p1)]
    greeted += [peer_c(lax.rem(c2 + d, z.p2)) for d in range(1, z.p2)]
    greeted += [(4 * quad + 3 - q0, s)]
    n_peers = len(greeted)
    for dev in greeted:
        pl.semaphore_signal(bar, inc=1, device_id=dev, device_id_type=MESH)
    with jax.named_scope("barrier"):
        pl.semaphore_wait(bar, n_peers)

    slice_rows = H // z.p1
    row0 = pl.multiple_of(core * H + c1 * slice_rows, slice_rows)

    def ws_at(half, r0, n):
        return ws.at[pl.ds(r0, n), pl.ds(pl.multiple_of(half * 3 * H, H), 3 * H)]

    def wt_at(half, r0, n):
        return wt.at[:, pl.ds(r0, n), pl.ds(pl.multiple_of(half * H, H), H)]

    sends = []

    def go(cp):
        cp.start()
        sends.append(cp)
        return cp

    def arrive(dst, rsem):
        remote(dst, dst, rsem, rsem, partner).wait_recv()

    go(remote(prm.at[s], prm.at[s], sem_w.at[0, 0], sem_w.at[1, 0], partner))
    go(remote(ws_in.at[pl.ds(row0, slice_rows)], ws_at(s, row0, slice_rows), sem_w.at[0, 1], sem_w.at[1, 1], partner))
    go(remote(wt_in.at[:, pl.ds(row0, slice_rows)], wt_at(s, row0, slice_rows), sem_w.at[0, 2], sem_w.at[1, 2], partner))

    def send_rows(src, dst, sem, j):
        a0, a1 = z.chunks[j]
        for b in range(NB):
            go(
                remote(
                    src.at[pl.ds(frame_row(o, b, a0, a1), a1 - a0)],
                    dst.at[s, pl.ds(a0, a1 - a0), :, b],
                    sem.at[0, j, b],
                    sem.at[1, j, b],
                    partner,
                )
            )

    def take_rows(dst, sem, j):
        a0, a1 = z.chunks[j]
        for b in range(NB):
            arrive(dst.at[o, pl.ds(a0, a1 - a0), :, b], sem.at[1, j, b])

    n_chunks = len(z.chunks)
    for j in range(n_chunks):
        send_rows(feat, xh, sem_f, j)
    for j in range(n_chunks):
        send_rows(cot, ct, sem_c, j)

    ri = lax.broadcasted_iota(jnp.int32, (J, J), 0)
    ci = lax.broadcasted_iota(jnp.int32, (J, J), 1)
    eye = jnp.where(ri == ci, 1.0, 0.0).astype(f32)
    up = jnp.zeros((J, J), f32)
    down = jnp.zeros((J, J), f32)
    for v in range(1, J):
        pv = par[v]
        up = jnp.where((ri == v) & (ci == pv), 1.0, up)
        down = jnp.where((ci == v) & (ri == pv), 1.0, down)
    degree = jnp.sum(eye + up + down, axis=0, keepdims=True)
    adjacent = [eye / degree, up / degree, down / degree]
    mixing = [adjacent[k] * imp[k] for k in range(3)]
    for k in range(3):
        adj[k] = adjacent[k]
    last = (((1,), (1,)), ((), ()))
    first = (((0,), (0,)), ((), ()))
    wide = jnp.ones((J, C), f32)
    edge[0] = jnp.dot(mixing[0], wide, precision=exact_mode, preferred_element_type=f32)
    edge[1] = jnp.dot(mixing[1], wide, precision=exact_mode, preferred_element_type=f32)
    edge[2] = lax.dot_general(mixing[2], wide, first, precision=exact_mode, preferred_element_type=f32)

    def kin_body(v, _):
        pv = par[v]
        sibling = jnp.int32(0)
        child = jnp.int32(0)
        for w in range(J - 1, 0, -1):
            pw_ = par[w]
            sibling = jnp.where((pw_ == pv) & (w > v), w, sibling)
            child = jnp.where(pw_ == v, w, child)
        kin[0, v] = sibling
        kin[1, v] = child
        return 0

    lax.fori_loop(0, J, kin_body, 0)
    chain[0] = jnp.zeros((RW, C), f32)

    for i, at in ((0, ws_at), (1, wt_at)):
        arrive(at(o, row0, slice_rows), sem_w.at[1, 1 + i])
        for d in range(1, z.p1):
            t = lax.rem(c1 + d, z.p1)
            go(
                remote(
                    at(o, row0, slice_rows),
                    at(o, row0, slice_rows),
                    sem_w.at[0, 4 + i * 16 + d],
                    sem_w.at[1, 4 + i * 16 + d],
                    peer_b(t),
                )
            )
    for i, at in ((0, ws_at), (1, wt_at)):
        for d in range(1, z.p1):
            t = lax.rem(c1 + z.p1 - d, z.p1)
            arrive(
                at(o, pl.multiple_of(core * H + t * slice_rows, slice_rows), slice_rows),
                sem_w.at[1, 4 + i * 16 + d],
            )
        mine = pl.multiple_of(core * H, H)
        go(remote(at(o, mine, H), at(o, mine, H), sem_w.at[0, 36 + i], sem_w.at[1, 36 + i], (2 * chip + 1 - core, s)))
    theirs = pl.multiple_of((1 - core) * H, H)
    arrive(ws_at(o, theirs, H), sem_w.at[1, 36])
    for cp in lw:
        cp.wait()
    arrive(prm.at[o], sem_w.at[1, 0])
    p0 = pres[0, 0].astype(f32)
    p1 = pres[0, 1].astype(f32)
    ri16 = lax.broadcasted_iota(jnp.int32, (RW, C), 0)
    pw = jnp.where((ri16 & 1) == 0, p0, p1).astype(f32)
    tail = jnp.where(ri16 >= RW - 2, 1.0, 0.0).astype(f32)
    side = s.astype(f32)

    def real(a):
        late = jnp.where(a >= L - z.pad, side, 0.0) if z.pad else 0.0
        return 1.0 - tail * late

    def tiles(x):
        return x.reshape(-1, RW, C)

    def times(x, m):
        return (tiles(x) * m[None]).reshape(x.shape)

    def down_rows(x):
        return jnp.sum(tiles(x), axis=0)

    def row_sum(x):
        return jnp.sum(x, axis=0, keepdims=True)

    def param(i):
        return jnp.concatenate([prm[0, i : i + 1], prm[1, i : i + 1]], axis=1)

    def whole(ref, a):
        return jnp.concatenate([ref[0, a].reshape(R, H), ref[1, a].reshape(R, H)], axis=1)

    def put(ref, a, value):
        for h in range(2):
            ref[h, a] = value[:, h * H : (h + 1) * H].reshape(J, NB, 2, H)

    def spread(buf, sem, r, q, n, peer, val):
        buf[r, q] = val
        for d in range(1, n):
            go(remote(buf.at[r, q], buf.at[r, q], sem.at[0, r, d], sem.at[1, r, d], peer(lax.rem(q + d, n))))

    def gather(buf, sem, r, q, n):
        for d in range(1, n):
            arrive(buf.at[r, lax.rem(q + n - d, n)], sem.at[1, r, d])
        return [buf[r, i] for i in range(n)]

    def add_up(parts):
        t = parts[0]
        for x in parts[1:]:
            t = t + x
        return t

    def merge(parts):
        n = add_up([x[0:1] for x in parts])
        below = jnp.maximum(n, 1.0)
        mean = add_up([x[0:1] * x[1:2] for x in parts]) / below
        spread_up = add_up([x[2:3] + x[0:1] * (x[1:2] - mean) * (x[1:2] - mean) for x in parts])
        return jnp.concatenate([n, mean, spread_up, jnp.zeros((5, C), f32)], axis=0)

    def all_start(r, val):
        spread(arA, semA, r, q0, 4, peer_0, val)

    def all_next(r, join):
        spread(arB, semB, r, q1, z.q1, peer_1, join(gather(arA, semA, r, q0, 4)))

    def all_more(r, join):
        val = join(gather(arB, semB, r, q1, z.q1))
        if z.q2 > 1:
            spread(arC, semC, r, q2, z.q2, peer_2, val)
            val = join(gather(arC, semC, r, q2, z.q2))
        arD[r, s] = val
        go(remote(arD.at[r, s], arD.at[r, s], semD.at[0, r], semD.at[1, r], across))

    def all_end(r, join):
        arrive(arD.at[r, o], semD.at[1, r])
        return join([arD[r, 0], arD[r, 1]])

    def moments(val_k, s1, s2):
        n = (p0 + p1) * (z.win - z.pad * side) * J
        below = jnp.maximum(n, 1.0)
        s1, s2 = row_sum(s1), row_sum(s2)
        return jnp.concatenate(
            [jnp.zeros((1, C), f32) + n, val_k + s1 / below, s2 - s1 * s1 / below, jnp.zeros((5, C), f32)], axis=0
        )

    zero16 = jnp.zeros((RW, C), f32)
    zero1 = jnp.zeros((1, C), f32)

    def link(value, k):
        for v in range(J - 1, 0, -1):
            chain[v] = value(v) * edge[k, v : v + 1] + chain[kin[0, v]]

    def spatial_body(a, carry):
        k_shift, s1, s2 = carry
        f = whole(xh, a)
        for k in range(3):
            parts[k] = jnp.dot(f, ws[:, k * C : (k + 1) * C], preferred_element_type=f32).reshape(J, RW, C)
        link(lambda v: parts[2, v], 2)
        for v in range(J):
            t = parts[0, v] * edge[0, v : v + 1] + chain[kin[1, v]]
            if v:
                t = t + parts[1, par[v]] * edge[1, v : v + 1]
            summed[a, v] = t
        t = summed[a].reshape(R, C)
        k_shift = jnp.where(a == 0, row_sum(t) * (1.0 / R), k_shift)
        w = pw * real(a)
        d = tiles(t - k_shift)
        wd = d * w[None]
        return k_shift, s1 + jnp.sum(wd, axis=0), s2 + jnp.sum(wd * d, axis=0)

    carry = (zero1, zero16, zero16)
    n_local = len(z.locals) * NB
    for cp in local[:n_local]:
        cp.wait()
    for j, (a0, a1) in enumerate(z.chunks):
        with jax.named_scope("features_wait"):
            take_rows(xh, sem_f, j)
        with jax.named_scope("spatial"):
            carry = lax.fori_loop(a0, a1, spatial_body, carry)

    lane = lax.broadcasted_iota(jnp.int32, (64, R), 1)
    line = lax.broadcasted_iota(jnp.int32, (64, R), 0)
    off = (RW - 2) * o
    pick = jnp.where(
        (lane == lax.shift_right_logical(line, 1) * RW + off + (line & 1)) & (line < 2 * J), 1.0, 0.0
    ).astype(bf)
    edge_a = (L - HALO) * o

    def halo_out(r, refs):
        for i, ref in enumerate(refs):
            for h in range(HALO):
                row = jnp.dot(pick, ref(edge_a + h).astype(bf), preferred_element_type=f32)
                halo_s[r + i, h] = row.astype(bf)
        at = pl.ds(r, len(refs))
        go(remote(halo_s.at[at], halo_m.at[at], sem_h.at[0, r, 0], sem_h.at[1, r, 0], across))

    def halo_relay(r, n):
        at = pl.ds(r, n)
        arrive(halo_m.at[at], sem_h.at[1, r, 0])
        go(remote(halo_m.at[at], halo_r.at[at], sem_h.at[0, r, 1], sem_h.at[1, r, 1], beside))

    def halo_in(r, n):
        arrive(halo_r.at[pl.ds(r, n)], sem_h.at[1, r, 1])

    row_in = lax.broadcasted_iota(jnp.int32, (R, C), 0) & (RW - 1)
    fside = 1.0 - side

    def fill_halo(buf, fresh):
        for h in range(HALO):
            extra = lax.dot_general(pick, fresh(h), first, preferred_element_type=f32)
            lower = pltpu.roll(buf[L + h].reshape(R, C).astype(f32), 2, 0)
            lower = jnp.where(row_in < 2, extra * side, lower)
            buf[h] = tiles(lower.astype(bf))
            upper = pltpu.roll(buf[HALO + h].reshape(R, C).astype(f32), R - 2, 0)
            upper = jnp.where(row_in >= RW - 2, extra * fside, upper)
            buf[HALO + L + h] = tiles(upper.astype(bf))

    halo_out(0, [lambda a: summed[a].reshape(R, C)])
    all_start(0, moments(*carry))
    with jax.named_scope("st1"):
        all_next(0, merge)
        halo_relay(0, 1)
        all_more(0, merge)
        st1 = all_end(0, merge)
    count = jnp.maximum(st1[0:1], 1.0)
    mean1 = st1[1:2]
    rstd1 = lax.rsqrt(st1[2:3] / count + norm_eps)
    gain1, shift1 = param(0), param(1)
    scale1 = rstd1 * gain1

    def act_body(a, _):
        t = gelu((summed[a].reshape(R, C) - mean1) * scale1 + shift1)
        acth[a + HALO] = tiles(times(t, real(a)).astype(bf))
        return 0

    with jax.named_scope("act"):
        lax.fori_loop(0, L, act_body, 0)
    halo_in(0, 1)
    fill_halo(acth, lambda h: gelu((halo_r[0, h].astype(f32) - mean1) * scale1 + shift1).astype(bf))

    arrive(wt_at(o, theirs, H), sem_w.at[1, 37])

    def conv_block(a0, n, carry):
        k_shift, s1, s2 = carry
        t = jnp.zeros((n * R, C), f32)
        for tap in range(TAPS):
            t = t + jnp.dot(acth[pl.ds(a0 + tap, n)].reshape(n * R, C), wt[tap], preferred_element_type=f32)
        conv[pl.ds(a0, n)] = t.reshape(n, R, C)
        k_shift = jnp.where(a0 == 0, row_sum(t[:R]) * (1.0 / R), k_shift)
        for i in range(n):
            w = pw * real(a0 + i)
            d = tiles(t[i * R : (i + 1) * R] - k_shift)
            wd = d * w[None]
            s1 = s1 + jnp.sum(wd, axis=0)
            s2 = s2 + jnp.sum(wd * d, axis=0)
        return k_shift, s1, s2

    def blocks(fun, carry):
        carry = lax.fori_loop(0, L // G, lambda i, c: fun(i * G, G, c), carry)
        if L % G:
            carry = fun(L // G * G, L % G, carry)
        return carry

    with jax.named_scope("conv"):
        carry = blocks(conv_block, (zero1, zero16, zero16))
    all_start(1, moments(*carry))
    with jax.named_scope("st2"):
        all_next(1, merge)
        all_more(1, merge)
        st2 = all_end(1, merge)
    mean2 = st2[1:2]
    rstd2 = lax.rsqrt(st2[2:3] / count + norm_eps)
    gain2, shift2 = param(2), param(3)

    for cp in local[n_local:]:
        cp.wait()

    def out_body(a, carry):
        sa, sb = carry
        normed = (conv[a] - mean2) * rstd2
        level = normed * gain2 + shift2 + whole(xh, a).astype(f32)
        value, slope = gelu_both(level)
        put(zz, a, value.astype(bf))
        gp = whole(ct, a).astype(f32) * slope
        conv[a] = gp
        put(ct, a, normed.astype(bf))
        gm = tiles(gp) * real(a)[None]
        return sa + jnp.sum(gm, axis=0), sb + jnp.sum(gm * tiles(normed), axis=0)

    carry = (zero16, zero16)
    outs = []

    def ship(buf, own, rcv, sem, j):
        a0, a1 = z.chunks[j]
        at = pl.ds(a0, a1 - a0)
        go(remote(buf.at[o, at], rcv.at[at], sem.at[0, j], sem.at[1, j], partner))
        cp = pltpu.make_async_copy(buf.at[s, at], own.at[at], sem.at[2, j])
        cp.start()
        outs.append(cp)

    for j, (a0, a1) in enumerate(z.chunks):
        with jax.named_scope("cotangent_wait"):
            take_rows(ct, sem_c, j)
        with jax.named_scope("level_two"):
            carry = lax.fori_loop(a0, a1, out_body, carry)
        ship(zz, act_own, act_rcv, sem_a, j)

    halo_out(1, [lambda a: conv[a], lambda a: whole(ct, a)])
    pad6 = jnp.zeros((6, C), f32)
    all_start(2, jnp.concatenate([row_sum(carry[0]), row_sum(carry[1]), pad6], axis=0))
    with jax.named_scope("sum2"):
        all_next(2, add_up)
        halo_relay(1, 2)
        all_more(2, add_up)
        sum2 = all_end(2, add_up)
    out_scale = gain2 * rstd2
    out_shift = out_scale * sum2[0:1] / count
    out_slope = out_scale * sum2[1:2] / count

    def back(grad, x, scale, shift, slope):
        corr = tiles(x * slope + shift) * pw[None]
        return grad * scale - corr.reshape(grad.shape)

    def gconv_body(a, _):
        gp = conv[a]
        t = back(gp, whole(ct, a).astype(f32), out_scale, out_shift, out_slope)
        gch[a + HALO] = tiles(times(t, real(a)).astype(bf))
        put(ct, a, gp.astype(bf))
        return 0

    with jax.named_scope("gconv"):
        lax.fori_loop(0, L, gconv_body, 0)
    halo_in(1, 2)
    fill_halo(
        gch,
        lambda h: back(halo_r[1, h].astype(f32), halo_r[2, h].astype(f32), out_scale, out_shift, out_slope).astype(bf),
    )

    def gact_block(a0, n, carry):
        sa, sb = carry
        t = jnp.zeros((n * R, C), f32)
        for tap in range(TAPS):
            t = t + lax.dot_general(
                gch[pl.ds(a0 + TAPS - 1 - tap, n)].reshape(n * R, C), wt[tap], last, preferred_element_type=f32
            )
        for i in range(n):
            centred = summed[a0 + i].reshape(R, C) - mean1
            _, slope = gelu_both(centred * scale1 + shift1)
            gl = t[i * R : (i + 1) * R] * slope
            conv[a0 + i] = gl
            gm = tiles(gl) * real(a0 + i)[None]
            sa = sa + jnp.sum(gm, axis=0)
            sb = sb + jnp.sum(gm * tiles(centred * rstd1), axis=0)
        return sa, sb

    with jax.named_scope("grad_act"):
        carry = blocks(gact_block, (zero16, zero16))
    all_start(3, jnp.concatenate([row_sum(carry[0]), row_sum(carry[1]), pad6], axis=0))
    with jax.named_scope("sum1"):
        all_next(3, add_up)

    def tap_body(tap, _):
        t = lax.dot_general(
            acth[pl.ds(tap, L)].reshape(z.total, C),
            gch[pl.ds(HALO, L)].reshape(z.total, C),
            first,
            preferred_element_type=f32,
        )
        gb[0, tap] = t[:, :H]
        gb[1, tap] = t[:, H:]
        return 0

    with jax.named_scope("tap_grad"):
        lax.fori_loop(0, TAPS // 2, tap_body, 0)
        all_more(3, add_up)
        lax.fori_loop(TAPS // 2, TAPS, tap_body, 0)
    with jax.named_scope("sum1_wait"):
        sum1 = all_end(3, add_up)
    in_scale = gain1 * rstd1
    in_shift = in_scale * sum1[0:1] / count
    in_slope = in_scale * rstd1 * sum1[1:2] / count

    neighbour = (2 * chip + 1 - core, s)
    core_rows = pl.multiple_of(core * H, H)
    other_rows = pl.multiple_of((1 - core) * H, H)
    def slice_of(t):
        return pl.multiple_of(owned(t) * slice_rows, slice_rows)

    chip_rows = slice_of(c1)
    spans = (pl.ds(0, TAPS), pl.ds(TAPS, 3))

    def grad_core(i):
        cut = (slice(None), spans[i])
        go(
            remote(
                gb.at[(*cut, pl.ds(other_rows, H))], gb_core.at[cut], sem_g.at[0, i, 0], sem_g.at[1, i, 0], neighbour
            )
        )

    def grad_chips(i):
        cut = (slice(None), spans[i])
        arrive(gb_core.at[cut], sem_g.at[1, i, 0])
        total = gb[(*cut, pl.ds(core_rows, H))] + gb_core[cut]
        gb_low[cut] = total.astype(bf)
        for d in range(1, z.p1):
            t = lax.rem(c1 + d, z.p1)
            go(
                remote(
                    gb_low.at[(*cut, pl.ds(slice_of(t), slice_rows))],
                    gb_chips.at[(c1, *cut)],
                    sem_g.at[0, i, d],
                    sem_g.at[1, i, d],
                    peer_b(t),
                )
            )

    def grad_pair(i):
        cut = (slice(None), spans[i])
        gb_chips[(c1, *cut)] = gb_low[(*cut, pl.ds(chip_rows, slice_rows))]
        for d in range(1, z.p1):
            arrive(gb_chips.at[(lax.rem(c1 + z.p1 - d, z.p1), *cut)], sem_g.at[1, i, d])
        gb_sum[cut] = add_up([gb_chips[(p, *cut)].astype(f32) for p in range(z.p1)])
        if z.p2 > 1:
            gb_far[(c2, *cut)] = gb_sum[cut]
            for d in range(1, z.p2):
                t = lax.rem(c2 + d, z.p2)
                go(
                    remote(
                        gb_far.at[(c2, *cut)],
                        gb_far.at[(c2, *cut)],
                        sem_g.at[0, i, 24 + d],
                        sem_g.at[1, i, 24 + d],
                        peer_c(t),
                    )
                )
            for d in range(1, z.p2):
                arrive(gb_far.at[(lax.rem(c2 + z.p2 - d, z.p2), *cut)], sem_g.at[1, i, 24 + d])
            gb_sum[cut] = add_up([gb_far[(p, *cut)] for p in range(z.p2)])
        go(remote(gb_sum.at[o, spans[i]], gb_pair.at[spans[i]], sem_g.at[0, i, 8], sem_g.at[1, i, 8], across))

    def grad_back(i):
        arrive(gb_pair.at[spans[i]], sem_g.at[1, i, 8])
        mine = gb_sum[s, spans[i]]
        other = gb_pair[spans[i]]
        own = pl.multiple_of(core_rows + chip_rows, slice_rows)
        gb_all[spans[i], pl.ds(own, slice_rows)] = mine + other
        at = gb_all.at[spans[i], pl.ds(own, slice_rows)]
        for d in range(1, z.p1):
            t = lax.rem(c1 + d, z.p1)
            go(remote(at, at, sem_g.at[0, i, 8 + d], sem_g.at[1, i, 8 + d], peer_b(t)))

    def grad_last(i):
        for d in range(1, z.p1):
            t = lax.rem(c1 + z.p1 - d, z.p1)
            at = pl.multiple_of(core_rows + slice_of(t), slice_rows)
            arrive(gb_all.at[spans[i], pl.ds(at, slice_rows)], sem_g.at[1, i, 8 + d])
        at = gb_all.at[spans[i], pl.ds(core_rows, H)]
        go(remote(at, at, sem_g.at[0, i, 16], sem_g.at[1, i, 16], neighbour))

    def grad_done(i):
        arrive(gb_all.at[spans[i], pl.ds(other_rows, H)], sem_g.at[1, i, 16])

    grad_core(0)

    def input_body(a, _):
        gs = back(conv[a], summed[a].reshape(R, C) - mean1, in_scale, in_shift, in_slope)
        gs = times(gs, real(a)).astype(bf)
        gch[a + HALO] = tiles(gs)
        parts[0] = gs.astype(f32).reshape(J, RW, C)
        link(lambda v: parts[0, v], 1)
        for w in range(J):
            at = slice(w * RW, (w + 1) * RW)
            mixed[0, at] = (parts[0, w] * edge[0, w : w + 1]).astype(bf)
            mixed[1, at] = chain[kin[1, w]].astype(bf)
            mixed[2, at] = (parts[0, par[w]] * edge[2, w : w + 1]).astype(bf)
        t = whole(ct, a).astype(f32)
        for k in range(3):
            t = t + lax.dot_general(mixed[k], ws[:, k * C : (k + 1) * C], last, preferred_element_type=f32)
        put(iz, a, t.astype(bf))
        return 0

    for j, (a0, a1) in enumerate(z.chunks):
        with jax.named_scope("input_grad"):
            lax.fori_loop(a0, a1, input_body, 0)
        ship(iz, ing_own, ing_rcv, sem_i, j)
        with jax.named_scope("grad_reduce"):
            if j == 0:
                grad_chips(0)
            if j == n_chunks - 1:
                grad_pair(0)

    def edge_rows_f(v):
        return jnp.concatenate(
            [xh[0, :, pl.ds(v, 1)].reshape(L * RW, H), xh[1, :, pl.ds(v, 1)].reshape(L * RW, H)], axis=1
        )

    def edge_rows_g(v):
        return gch[pl.ds(HALO, L), pl.ds(v, 1)].reshape(L * RW, C)

    sg[...] = jnp.zeros_like(sg)

    def edge_body(v, acc):
        pv = par[v]
        hot = jnp.where(lax.broadcasted_iota(jnp.int32, (8, C), 1) == v, 1.0, 0.0)
        kind = lax.broadcasted_iota(jnp.int32, (8, C), 0)
        far = jnp.where(v > 0, 1.0, 0.0)
        f_v, g_v = edge_rows_f(v), edge_rows_g(v)
        f_p, g_p = edge_rows_f(pv), edge_rows_g(pv)
        for k, (fx, gx, on) in enumerate(((f_v, g_v, 1.0), (f_p, g_v, far), (f_v, g_p, far))):
            prod = lax.dot_general(fx, gx, first, preferred_element_type=f32)
            sg[k] = sg[k] + prod * edge[k, pl.ds(v, 1)]
            dot = jnp.sum(row_sum(prod * ws[:, k * C : (k + 1) * C].astype(f32)), axis=1, keepdims=True)
            acc = acc + jnp.where(kind == k, hot, 0.0) * (dot * on)
        return acc

    with jax.named_scope("edges"):
        dvec = lax.fori_loop(0, J, edge_body, jnp.zeros((8, C), f32))
    for j in range(6):
        k, h = j // 2, j % 2
        gb[j // 3, TAPS + j % 3] = sg[k, :, h * H : (h + 1) * H]
    grad_core(1)
    all_start(4, dvec)
    with jax.named_scope("grad_reduce"):
        grad_back(0)
        grad_chips(1)
        all_next(4, add_up)
        all_more(4, add_up)
        grad_pair(1)
        grad_back(1)
        grad_last(0)
        dvec = all_end(4, add_up)
        grad_last(1)
    for k in range(3):
        per_edge = dvec[k : k + 1, :J]
        if k == 1:
            per_edge = lax.dot_general(
                eye, jnp.broadcast_to(per_edge, (J, J)), last, precision=exact_mode, preferred_element_type=f32
            )
        ig_out[k] = adj[k] * per_edge
    for i, row in enumerate((sum1[1:2], sum1[0:1], sum2[1:2], sum2[0:1])):
        sums_out[i : i + 1] = jnp.where(s == 0, row[:, :H], row[:, H:])
    sums_out[4:8] = jnp.zeros((4, H), f32)
    with jax.named_scope("grad_reduce_end"):
        grad_done(0)
        grad_done(1)
        last_out = [pltpu.make_async_copy(gb_all.at[pl.ds(0, TAPS)], tg_out, sem_l.at[2, 2])]
        for j in range(3):
            last_out.append(
                pltpu.make_async_copy(gb_all.at[TAPS + j], sg_out.at[:, pl.ds(j * H, H)], sem_l.at[2, 3 + j])
            )
        for cp in last_out:
            cp.start()

    with jax.named_scope("last_waits"):
        for j in range(n_chunks):
            a0, a1 = z.chunks[j]
            at = pl.ds(a0, a1 - a0)
            arrive(act_rcv.at[at], sem_a.at[1, j])
            arrive(ing_rcv.at[at], sem_i.at[1, j])
        for cp in outs + last_out:
            cp.wait()
        for cp in sends:
            cp.wait_send()


def finish(
    z,
    act_own,
    act_rcv,
    ing_own,
    ing_rcv,
    tg_in,
    sg_in,
    sums_in,
    ig_in,
    act_out,
    ing_out,
    tg_out,
    sg_out,
    r0,
    r1,
    r2,
    r3,
    ig_out,
    low,
    full,
    tg,
    sg,
    sem_in,
    sem_out,
):
    J, L = z.joints, z.blk
    s = lax.axis_index("sub")
    jobs = [(act_own, act_out, s), (ing_own, ing_out, s), (act_rcv, act_out, 1 - s), (ing_rcv, ing_out, 1 - s)]
    ins = []
    for i, (src, _, _) in enumerate(jobs):
        cp = pltpu.make_async_copy(src, low.at[i], sem_in.at[i])
        cp.start()
        ins.append(cp)
    grads = []
    for i, (src, mid, dst) in enumerate(((tg_in, tg, tg_out), (sg_in, sg, sg_out))):
        cp = pltpu.make_async_copy(src, mid, sem_in.at[4 + i])
        cp.start()
        grads.append((cp, pltpu.make_async_copy(mid, dst, sem_in.at[6 + i])))
    for i, r in enumerate((r0, r1, r2, r3)):
        r[...] = sums_in[i : i + 1]
    ig_out[...] = ig_in[...]
    cut = L - z.pad

    def pieces(i, dst, w):
        for part, (a0, a1) in enumerate(z.locals):
            for b in range(NB):
                cp = pltpu.make_async_copy(
                    full.at[i, pl.ds(a0, a1 - a0), :, b],
                    dst.at[pl.ds(w * z.win + b * L + a0, a1 - a0)],
                    sem_out.at[i, part, b],
                )
                yield part == 1 and b == NB - 1, cp

    for i, (_, dst, w) in enumerate(jobs):
        ins[i].wait()

        def body(a, _, i=i):
            value = low[i, a].reshape(z.rows, z.half).astype(jnp.float32)
            full[i, a] = value.reshape(J, NB, 2, z.half)
            return 0

        lax.fori_loop(0, L, body, 0)
        for beyond, cp in pieces(i, dst, w):
            if beyond:
                pl.when(w == 0)(cp.start)
            else:
                cp.start()
    for cp_in, cp_out in grads:
        cp_in.wait()
        cp_out.start()
    for _, cp_out in grads:
        cp_out.wait()
    for i, (_, dst, w) in enumerate(jobs):
        for beyond, cp in pieces(i, dst, w):
            if beyond:
                pl.when(w == 0)(cp.wait)
            else:
                cp.wait()


def block(
    n_dp, features, presence, parents, w_spatial, importance, gain_one, shift_one, w_temporal, gain_two, shift_two, cotangent
):
    _, _, frames, joints, half = features.shape
    z = Sizes(n_dp, frames, joints, half)
    f32, bf = jnp.float32, jnp.bfloat16
    C, H, L, R, J = z.chan, z.half, z.blk, z.rows, z.joints

    def natural(x):
        return x.transpose(0, 2, 3, 1, 4).reshape(frames, joints, 2, half)

    any_, vmem, smem = (pl.BlockSpec(memory_space=m) for m in (pl.ANY, pltpu.VMEM, pltpu.SMEM))
    blocked = (L, J, NB, 2, H)
    sds = jax.ShapeDtypeStruct
    VM, DMA = pltpu.VMEM, pltpu.SemaphoreType.DMA
    nch = len(z.chunks)
    outs = pl.pallas_call(
        functools.partial(mega, z),
        name="graph_conv_block",
        out_shape=[sds(blocked, bf)] * 4
        + [sds((TAPS, C, H), f32), sds((C, 3 * H), f32), sds((8, H), f32), sds((3, J, J), f32)],
        in_specs=[any_] * 4 + [vmem, smem, smem] + [vmem] * 4,
        out_specs=[any_] * 6 + [vmem] * 2,
        scratch_shapes=[
            VM((2,) + blocked, bf),
            VM((2,) + blocked, bf),
            VM((TAPS, C, C), bf),
            VM((C, 3 * C), bf),
            VM((3, J, RW, C), f32),
            VM((J, RW, C), f32),
            VM((3, R, C), bf),
            VM((L, J, RW, C), f32),
            VM((L + 2 * HALO, J, RW, C), bf),
            VM((L, R, C), f32),
            VM((L + 2 * HALO, J, RW, C), bf),
            VM((2,) + blocked, bf),
            VM((2,) + blocked, bf),
            VM((2, TAPS + 3, C, H), f32),
            VM((2, TAPS + 3, H, H), f32),
            VM((2, TAPS + 3, H, H), bf),
            VM((z.p1, 2, TAPS + 3, H // z.p1, H), bf),
            VM((z.p2, 2, TAPS + 3, H // z.p1, H), f32),
            VM((2, TAPS + 3, H // z.p1, H), f32),
            VM((TAPS + 3, H // z.p1, H), f32),
            VM((TAPS + 3, C, H), f32),
            VM((3, C, C), f32),
            VM((2, 8, H), f32),
            VM((3, J, J), f32),
            VM((3, J, C), f32),
            pltpu.SMEM((2, J), jnp.int32),
            VM((3, HALO, 64, C), bf),
            VM((3, HALO, 64, C), bf),
            VM((3, HALO, 64, C), bf),
            VM((5, 4, 8, C), f32),
            VM((5, z.q1, 8, C), f32),
            VM((5, z.q2, 8, C), f32),
            VM((5, 2, 8, C), f32),
            DMA((3, 2 * NB)),
            DMA((2, nch, NB)),
            DMA((2, nch, NB)),
            DMA((3, nch)),
            DMA((3, nch)),
            DMA((2, 40)),
            DMA((2, 2, 2)),
            DMA((2, 2, 32)),
            DMA((2, 5, 4)),
            DMA((2, 5, z.q1)),
            DMA((2, 5, z.q2)),
            DMA((2, 5)),
        ],
        compiler_params=pltpu.CompilerParams(
            collective_id=0, has_side_effects=True, vmem_limit_bytes=62 * 2**20
        ),
    )(
        natural(features),
        natural(cotangent),
        w_temporal,
        w_spatial,
        importance,
        parents,
        presence,
        *(v.reshape(1, H) for v in (gain_one, shift_one, gain_two, shift_two)),
    )
    act, ing, tg, sg, r0, r1, r2, r3, ig = pl.pallas_call(
        functools.partial(finish, z),
        name="natural_order",
        out_shape=[sds((frames, joints, 2, H), f32)] * 2
        + [sds((TAPS, C, H), f32), sds((C, 3 * H), f32)]
        + [sds((1, H), f32)] * 4
        + [sds((3, J, J), f32)],
        in_specs=[any_] * 6 + [vmem] * 2,
        out_specs=[any_] * 4 + [vmem] * 5,
        scratch_shapes=[
            VM((4,) + blocked, bf),
            VM((4,) + blocked, f32),
            VM((TAPS, C, H), f32),
            VM((C, 3 * H), f32),
            DMA((8,)),
            DMA((4, 2, NB)),
        ],
        compiler_params=pltpu.CompilerParams(vmem_limit_bytes=60 * 2**20),
    )(*outs)

    def back(x):
        return x.reshape(1, frames, joints, 2, half).transpose(0, 3, 1, 2, 4)

    return (
        back(act),
        back(ing),
        sg,
        ig,
        *(r.reshape(H) for r in (r0, r1)),
        tg,
        *(r.reshape(H) for r in (r2, r3)),
    )


def solution(mesh):
    in_specs = (
        P("dp", None, None, None, "sub"),
        P("dp", None),
        P(),
        P(None, "sub"),
        P(),
        P("sub"),
        P("sub"),
        P(None, None, "sub"),
        P("sub"),
        P("sub"),
        P("dp", None, None, None, "sub"),
    )
    out_specs = (
        P("dp", None, None, None, "sub"),
        P("dp", None, None, None, "sub"),
        P(None, "sub"),
        P(),
        P("sub"),
        P("sub"),
        P(None, None, "sub"),
        P("sub"),
        P("sub"),
    )
    return jax.shard_map(
        functools.partial(block, mesh.shape["dp"]), mesh=mesh, in_specs=in_specs, out_specs=out_specs, check_vma=False
    )
```

```python
import functools

import jax
import jax.numpy as jnp
from jax import lax
from jax.experimental import pallas as pl
from jax.experimental.pallas import tpu as pltpu
from jax.sharding import PartitionSpec as P

norm_eps = 1e-05
exact_mode = lax.Precision.HIGHEST
MESH = pl.DeviceIdType.MESH
TAPS = 9
EARLY = 7
HALO = TAPS // 2
NB = 8
RW = 2 * NB
G = 4
tanh_scale = 0.7978845608028654
tanh_cubic = 0.044715


def gelu(x):
    t = jnp.tanh(x * (tanh_scale + (tanh_scale * tanh_cubic) * (x * x)))
    return x * (0.5 + 0.5 * t)


def gelu_both(x):
    x2 = x * x
    h = 0.5 + 0.5 * jnp.tanh(x * (tanh_scale + (tanh_scale * tanh_cubic) * x2))
    rise = x * (2.0 * tanh_scale + (6.0 * tanh_scale * tanh_cubic) * x2)
    return x * h, h + h * ((1.0 - h) * rise)


class Sizes:
    def __init__(self, n_dp, frames, joints, half):
        self.n_dp, self.frames, self.joints, self.half = n_dp, frames, joints, half
        self.chan = 2 * half
        self.blk = -(-frames // (2 * NB))
        self.win = self.blk * NB
        self.pad = 2 * self.win - frames
        self.rows = joints * RW
        self.total = self.blk * self.rows
        self.chips = n_dp // 2
        self.p1 = 8
        self.p2 = self.chips // self.p1
        self.near = 2 * self.p1
        cut = self.blk - self.pad
        step = -(-cut // 3)
        self.chunks = [(a, min(a + step, cut)) for a in range(0, cut, step)]
        if self.pad:
            self.chunks.append((cut, self.blk))
        self.locals = [(0, cut)] + ([(cut, self.blk)] if self.pad else [])


def mega(
    z,
    feat,
    cot,
    wt_in,
    ws_in,
    imp,
    par,
    pres,
    g1,
    b1,
    g2,
    b2,
    act_own,
    act_rcv,
    ing_own,
    ing_rcv,
    tg_out,
    sg_out,
    sums_out,
    ig_out,
    xh,
    ct,
    fx,
    wt,
    ws,
    summed,
    acth,
    conv,
    gch,
    iz,
    gb,
    gb_core,
    gb_low,
    gb_chips,
    gb_far,
    gb_sum,
    gb_pair,
    mixed,
    dots,
    prm,
    adj,
    edge,
    kin,
    halo_s,
    halo_m,
    halo_r,
    arA,
    arC,
    arD,
    sem_l,
    sem_f,
    sem_c,
    sem_a,
    sem_i,
    sem_w,
    sem_h,
    sem_g,
    semA,
    semC,
    semD,
):
    f32, bf = jnp.float32, jnp.bfloat16
    J, C, H, L, R = z.joints, z.chan, z.half, z.blk, z.rows
    s = lax.axis_index("sub")
    dp = lax.axis_index("dp")
    o = 1 - s
    core = lax.rem(dp, 2)
    chip = lax.div(dp, 2)
    c1 = lax.rem(chip, z.p1)
    c2 = lax.div(chip, z.p1)
    partner = (dp, o)

    d1 = lax.rem(dp, z.near)
    flip = dp + 4 - 8 * lax.rem(lax.div(dp, 4), 2)
    across = (flip, o)
    beside = (flip, s)

    def peer_b(t):
        return (2 * (c2 * z.p1 + t) + core, s)

    def peer_c(t):
        return (2 * (t * z.p1 + c1) + core, s)

    def peer_0(t):
        return (c2 * z.near + t, s)

    def other_chip(t):
        return t + 2 - 4 * lax.rem(lax.div(t, 2), 2)

    def owned(t):
        return t + s * (other_chip(t) - t)

    def remote(src, dst, ssem, rsem, dev):
        return pltpu.make_async_remote_copy(
            src_ref=src,
            dst_ref=dst,
            send_sem=ssem,
            recv_sem=rsem,
            device_id=dev,
            device_id_type=MESH,
        )

    bar = pltpu.get_barrier_semaphore()
    greeted = [partner, across]
    greeted += [peer_0(lax.rem(d1 + d, z.near)) for d in range(1, z.near)]
    greeted += [peer_c(lax.rem(c2 + d, z.p2)) for d in range(1, z.p2)]
    for dev in greeted:
        pl.semaphore_signal(bar, inc=1, device_id=dev, device_id_type=MESH)

    def frame_row(w, b, a0, a1):
        at = w * z.win + (b * L + a0)
        if b == NB - 1 and z.pad and a0 >= L - z.pad:
            at = at - w * z.pad
        return at

    local = []
    for which, (src, dst) in enumerate(((feat, xh), (cot, ct))):
        for i, (a0, a1) in enumerate(z.locals):
            for b in range(NB):
                cp = pltpu.make_async_copy(
                    src.at[pl.ds(frame_row(s, b, a0, a1), a1 - a0)],
                    dst.at[s, pl.ds(a0, a1 - a0), :, b],
                    sem_l.at[which, i * NB + b],
                )
                cp.start()
                local.append(cp)
    lw = [
        pltpu.make_async_copy(ws_in, ws.at[:, pl.ds(pl.multiple_of(s * 3 * H, H), 3 * H)], sem_l.at[2, 0]),
        pltpu.make_async_copy(wt_in, wt.at[:, :, pl.ds(pl.multiple_of(s * H, H), H)], sem_l.at[2, 1]),
    ]
    for cp in lw:
        cp.start()
    for i, v in enumerate((g1, b1, g2, b2)):
        prm[s, i : i + 1] = v[...]

    with jax.named_scope("barrier"):
        pl.semaphore_wait(bar, len(greeted))

    slice_rows = H // z.p1
    row0 = pl.multiple_of(core * H + c1 * slice_rows, slice_rows)

    def ws_at(half, r0, n):
        return ws.at[pl.ds(r0, n), pl.ds(pl.multiple_of(half * 3 * H, H), 3 * H)]

    def wt_at(half, r0, n):
        return wt.at[:, pl.ds(r0, n), pl.ds(pl.multiple_of(half * H, H), H)]

    sends = []

    def go(cp):
        cp.start()
        sends.append(cp)
        return cp

    def arrive(dst, rsem):
        remote(dst, dst, rsem, rsem, partner).wait_recv()

    go(remote(prm.at[s], prm.at[s], sem_w.at[0, 0], sem_w.at[1, 0], partner))
    go(remote(ws_in.at[pl.ds(row0, slice_rows)], ws_at(s, row0, slice_rows), sem_w.at[0, 1], sem_w.at[1, 1], partner))
    go(remote(wt_in.at[:, pl.ds(row0, slice_rows)], wt_at(s, row0, slice_rows), sem_w.at[0, 2], sem_w.at[1, 2], partner))

    def send_rows(src, dst, sem, j):
        a0, a1 = z.chunks[j]
        for b in range(NB):
            go(
                remote(
                    src.at[pl.ds(frame_row(o, b, a0, a1), a1 - a0)],
                    dst.at[s, pl.ds(a0, a1 - a0), :, b],
                    sem.at[0, j, b],
                    sem.at[1, j, b],
                    partner,
                )
            )

    def take_rows(dst, sem, j):
        a0, a1 = z.chunks[j]
        for b in range(NB):
            arrive(dst.at[o, pl.ds(a0, a1 - a0), :, b], sem.at[1, j, b])

    n_chunks = len(z.chunks)
    for j in range(n_chunks):
        send_rows(feat, xh, sem_f, j)
    for j in range(n_chunks):
        send_rows(cot, ct, sem_c, j)

    ri = lax.broadcasted_iota(jnp.int32, (J, J), 0)
    ci = lax.broadcasted_iota(jnp.int32, (J, J), 1)
    eye = jnp.where(ri == ci, 1.0, 0.0).astype(f32)
    up = jnp.zeros((J, J), f32)
    down = jnp.zeros((J, J), f32)
    for v in range(1, J):
        pv = par[v]
        up = jnp.where((ri == v) & (ci == pv), 1.0, up)
        down = jnp.where((ci == v) & (ri == pv), 1.0, down)
    degree = jnp.sum(eye + up + down, axis=0, keepdims=True)
    adjacent = [eye / degree, up / degree, down / degree]
    mixing = [adjacent[k] * imp[k] for k in range(3)]
    for k in range(3):
        adj[k] = adjacent[k]
    last = (((1,), (1,)), ((), ()))
    first = (((0,), (0,)), ((), ()))
    wide = jnp.ones((J, C), f32)
    edge[0] = jnp.dot(mixing[0], wide, precision=exact_mode, preferred_element_type=f32)
    edge[1] = jnp.dot(mixing[1], wide, precision=exact_mode, preferred_element_type=f32)
    edge[2] = lax.dot_general(mixing[2], wide, first, precision=exact_mode, preferred_element_type=f32)

    def kin_body(v, _):
        pv = par[v]
        sibling = jnp.int32(0)
        child = jnp.int32(0)
        for w in range(J - 1, 0, -1):
            pw_ = par[w]
            sibling = jnp.where((pw_ == pv) & (w > v), w, sibling)
            child = jnp.where(pw_ == v, w, child)
        kin[0, v] = sibling
        kin[1, v] = child
        return 0

    lax.fori_loop(0, J, kin_body, 0)

    for i, at in ((0, ws_at), (1, wt_at)):
        arrive(at(o, row0, slice_rows), sem_w.at[1, 1 + i])
        for d in range(1, z.p1):
            t = lax.rem(c1 + d, z.p1)
            go(
                remote(
                    at(o, row0, slice_rows),
                    at(o, row0, slice_rows),
                    sem_w.at[0, 4 + i * 16 + d],
                    sem_w.at[1, 4 + i * 16 + d],
                    peer_b(t),
                )
            )
    for i, at in ((0, ws_at), (1, wt_at)):
        for d in range(1, z.p1):
            t = lax.rem(c1 + z.p1 - d, z.p1)
            arrive(
                at(o, pl.multiple_of(core * H + t * slice_rows, slice_rows), slice_rows),
                sem_w.at[1, 4 + i * 16 + d],
            )
        mine = pl.multiple_of(core * H, H)
        go(remote(at(o, mine, H), at(o, mine, H), sem_w.at[0, 36 + i], sem_w.at[1, 36 + i], (2 * chip + 1 - core, s)))
    theirs = pl.multiple_of((1 - core) * H, H)
    arrive(ws_at(o, theirs, H), sem_w.at[1, 36])
    for cp in lw:
        cp.wait()
    arrive(prm.at[o], sem_w.at[1, 0])
    p0 = pres[0, 0].astype(f32)
    p1 = pres[0, 1].astype(f32)
    ri16 = lax.broadcasted_iota(jnp.int32, (RW, C), 0)
    pw = jnp.where((ri16 & 1) == 0, p0, p1).astype(f32)
    tail = jnp.where(ri16 >= RW - 2, 1.0, 0.0).astype(f32)
    side = s.astype(f32)

    real = 1.0 - tail * side
    cut = L - z.pad

    def tiles(x):
        return x.reshape(-1, RW, C)

    def flat(x):
        return x.reshape(R, C)

    def keep(x, late):
        return (tiles(x) * real[None]).reshape(x.shape) if late else x

    def down_rows(x):
        return jnp.sum(tiles(x), axis=0)

    def each(body, carry):
        carry = lax.fori_loop(0, cut, body(False), carry)
        return lax.fori_loop(cut, L, body(True), carry) if z.pad else carry

    def row_sum(x):
        return jnp.sum(x, axis=0, keepdims=True)

    def param(i):
        return jnp.concatenate([prm[0, i : i + 1], prm[1, i : i + 1]], axis=1)

    def whole(ref, a):
        return jnp.concatenate([ref[0, a].reshape(R, H), ref[1, a].reshape(R, H)], axis=1)

    def put(ref, a, value):
        for h in range(2):
            ref[h, a] = value[:, h * H : (h + 1) * H].reshape(J, RW, H)

    def land(ref, a, value):
        for h in range(2):
            ref[h, a] = value[:, h * H : (h + 1) * H].reshape(J, NB, 2, H)

    def spread(buf, sem, r, q, n, peer, val):
        buf[r, q] = val
        for d in range(1, n):
            go(remote(buf.at[r, q], buf.at[r, q], sem.at[0, r, d], sem.at[1, r, d], peer(lax.rem(q + d, n))))

    def gather(buf, sem, r, q, n):
        for d in range(1, n):
            arrive(buf.at[r, lax.rem(q + n - d, n)], sem.at[1, r, d])
        return [buf[r, i] for i in range(n)]

    def add_up(parts):
        t = parts[0]
        for x in parts[1:]:
            t = t + x
        return t

    def merge(parts):
        n = add_up([x[0:1] for x in parts])
        below = jnp.maximum(n, 1.0)
        mean = add_up([x[0:1] * x[1:2] for x in parts]) / below
        spread_up = add_up([x[2:3] + x[0:1] * (x[1:2] - mean) * (x[1:2] - mean) for x in parts])
        return jnp.concatenate([n, mean, spread_up, jnp.zeros((5, C), f32)], axis=0)

    def all_start(r, val):
        spread(arA, semA, r, d1, z.near, peer_0, val)

    def all_more(r, join):
        val = join(gather(arA, semA, r, d1, z.near))
        if z.p2 > 1:
            spread(arC, semC, r, c2, z.p2, peer_c, val)
            val = join(gather(arC, semC, r, c2, z.p2))
        arD[r, s] = val
        go(remote(arD.at[r, s], arD.at[r, s], semD.at[0, r], semD.at[1, r], across))

    def all_end(r, join):
        arrive(arD.at[r, o], semD.at[1, r])
        return join([arD[r, 0], arD[r, 1]])

    def moments(val_k, s1, s2):
        n = (p0 + p1) * (z.win - z.pad * side) * J
        below = jnp.maximum(n, 1.0)
        s1, s2 = row_sum(s1), row_sum(s2)
        return jnp.concatenate(
            [jnp.zeros((1, C), f32) + n, val_k + s1 / below, s2 - s1 * s1 / below, jnp.zeros((5, C), f32)], axis=0
        )

    def scaled(sums, rstd):
        return jnp.concatenate([sums[0:1], sums[1:2] * rstd], axis=0)

    zero16 = jnp.zeros((RW, C), f32)
    zero1 = jnp.zeros((1, C), f32)

    def spatial_chunk(a0, a1, carry):
        k_shift, s1, s2 = carry
        n = a1 - a0
        span, up_at, down_at, link = pl.ds(a0, n), pl.ds(0, n), pl.ds(n, n), pl.ds(2 * n, n)

        def body(i, _):
            f = whole(xh, a0 + i)
            put(fx, a0 + i, f)
            for k, (buf, at) in enumerate(((summed, a0 + i), (conv, i), (conv, n + i))):
                buf[at] = tiles(jnp.dot(f, ws[:, k * C : (k + 1) * C], preferred_element_type=f32))
            return 0

        lax.fori_loop(0, n, body, 0)
        conv[link, 0] = jnp.zeros((n, RW, C), f32)
        for v in range(J - 1, 0, -1):
            conv[link, v] = conv[down_at, v] * edge[2, v : v + 1] + conv[link, kin[0, v]]
        w = (pw * real if a0 >= cut else pw)[None]
        for v in range(J):
            t = summed[span, v] * edge[0, v : v + 1] + conv[link, kin[1, v]]
            if v:
                t = t + conv[up_at, par[v]] * edge[1, v : v + 1]
            summed[span, v] = t
            if a0 == 0 and v == 0:
                k_shift = row_sum(jnp.sum(t, axis=0)) * (1.0 / (n * RW))
            d = t - k_shift
            wd = d * w
            s1 = s1 + jnp.sum(wd, axis=0)
            s2 = s2 + jnp.sum(wd * d, axis=0)
        return k_shift, s1, s2

    carry = (zero1, zero16, zero16)
    n_local = len(z.locals) * NB
    for cp in local[:n_local]:
        cp.wait()
    for j, (a0, a1) in enumerate(z.chunks):
        with jax.named_scope("features_wait"):
            take_rows(xh, sem_f, j)
        with jax.named_scope("spatial"):
            carry = spatial_chunk(a0, a1, carry)

    lane = lax.broadcasted_iota(jnp.int32, (64, R), 1)
    line = lax.broadcasted_iota(jnp.int32, (64, R), 0)
    off = (RW - 2) * o
    pick = jnp.where(
        (lane == lax.shift_right_logical(line, 1) * RW + off + (line & 1)) & (line < 2 * J), 1.0, 0.0
    ).astype(bf)
    edge_a = (L - HALO) * o

    def halo_out(r, refs):
        for i, ref in enumerate(refs):
            for h in range(HALO):
                row = jnp.dot(pick, ref(edge_a + h).astype(bf), preferred_element_type=f32)
                halo_s[r + i, h] = row.astype(bf)
        at = pl.ds(r, len(refs))
        go(remote(halo_s.at[at], halo_m.at[at], sem_h.at[0, r, 0], sem_h.at[1, r, 0], across))

    def halo_relay(r, n):
        at = pl.ds(r, n)
        arrive(halo_m.at[at], sem_h.at[1, r, 0])
        go(remote(halo_m.at[at], halo_r.at[at], sem_h.at[0, r, 1], sem_h.at[1, r, 1], beside))

    def halo_in(r, n):
        arrive(halo_r.at[pl.ds(r, n)], sem_h.at[1, r, 1])

    row_in = lax.broadcasted_iota(jnp.int32, (R, C), 0) & (RW - 1)
    fside = 1.0 - side

    def fill_halo(buf, fresh):
        for h in range(HALO):
            extra = lax.dot_general(pick, fresh(h), first, preferred_element_type=f32)
            lower = pltpu.roll(buf[L + h].reshape(R, C).astype(f32), 2, 0)
            lower = jnp.where(row_in < 2, extra * side, lower)
            buf[h] = tiles(lower.astype(bf))
            upper = pltpu.roll(buf[HALO + h].reshape(R, C).astype(f32), R - 2, 0)
            upper = jnp.where(row_in >= RW - 2, extra * fside, upper)
            buf[HALO + L + h] = tiles(upper.astype(bf))

    all_start(0, moments(*carry))
    halo_out(0, [lambda a: flat(summed[a])])
    with jax.named_scope("st1"):
        all_more(0, merge)
        halo_relay(0, 1)
        st1 = all_end(0, merge)
    count = jnp.maximum(st1[0:1], 1.0)
    mean1 = st1[1:2]
    rstd1 = lax.rsqrt(st1[2:3] / count + norm_eps)
    gain1, shift1 = param(0), param(1)
    scale1 = rstd1 * gain1

    def act_body(late):
        def body(a, _):
            t = gelu((flat(summed[a]) - mean1) * scale1 + shift1)
            acth[a + HALO] = tiles(keep(t, late).astype(bf))
            return 0

        return body

    with jax.named_scope("act"):
        each(act_body, 0)
    halo_in(0, 1)
    fill_halo(acth, lambda h: gelu((halo_r[0, h].astype(f32) - mean1) * scale1 + shift1).astype(bf))

    arrive(wt_at(o, theirs, H), sem_w.at[1, 37])

    def conv_block(a0, late, carry):
        k_shift, s1, s2 = carry
        n = len(late)
        t = jnp.zeros((n * R, C), f32)
        for tap in range(TAPS):
            t = t + jnp.dot(acth[pl.ds(a0 + tap, n)].reshape(n * R, C), wt[tap], preferred_element_type=f32)
        conv[pl.ds(a0, n)] = t.reshape(n, J, RW, C)
        k_shift = jnp.where(a0 == 0, row_sum(t[:R]) * (1.0 / R), k_shift)
        for i in range(n):
            w = pw * real if late[i] else pw
            d = tiles(t[i * R : (i + 1) * R] - k_shift)
            wd = d * w[None]
            s1 = s1 + jnp.sum(wd, axis=0)
            s2 = s2 + jnp.sum(wd * d, axis=0)
        return k_shift, s1, s2

    def blocks(fun, carry):
        plain = cut // G
        carry = lax.fori_loop(0, plain, lambda i, c: fun(i * G, [False] * G, c), carry)
        for a0 in range(plain * G, L, G):
            carry = fun(a0, [a >= cut for a in range(a0, min(a0 + G, L))], carry)
        return carry

    with jax.named_scope("conv"):
        carry = blocks(conv_block, (zero1, zero16, zero16))
    all_start(1, moments(*carry))
    with jax.named_scope("st2"):
        all_more(1, merge)
        st2 = all_end(1, merge)
    mean2 = st2[1:2]
    rstd2 = lax.rsqrt(st2[2:3] / count + norm_eps)
    gain2, shift2 = param(2), param(3)

    for cp in local[n_local:]:
        cp.wait()

    scale2 = rstd2 * gain2

    def out_body(late):
        def body(a, carry):
            sa, sb = carry
            centred = flat(conv[a]) - mean2
            level = centred * scale2 + (shift2 + whole(fx, a).astype(f32))
            value, slope = gelu_both(level)
            land(xh, a, value.astype(bf))
            gp = whole(ct, a).astype(f32) * slope
            conv[a] = tiles(gp)
            put(iz, a, centred.astype(bf))
            gm = keep(gp, late)
            return sa + down_rows(gm), sb + down_rows(gm * centred)

        return body

    carry = (zero16, zero16)
    outs = []

    def ship(buf, own, rcv, sem, j):
        a0, a1 = z.chunks[j]
        at = pl.ds(a0, a1 - a0)
        go(remote(buf.at[o, at], rcv.at[at], sem.at[0, j], sem.at[1, j], partner))
        cp = pltpu.make_async_copy(buf.at[s, at], own.at[at], sem.at[2, j])
        cp.start()
        outs.append(cp)

    for j, (a0, a1) in enumerate(z.chunks):
        with jax.named_scope("cotangent_wait"):
            take_rows(ct, sem_c, j)
        with jax.named_scope("level_two"):
            carry = lax.fori_loop(a0, a1, out_body(a0 >= cut), carry)
        ship(xh, act_own, act_rcv, sem_a, j)

    pad6 = jnp.zeros((6, C), f32)
    all_start(2, jnp.concatenate([row_sum(carry[0]), row_sum(carry[1]), pad6], axis=0))
    halo_out(1, [lambda a: flat(conv[a]), lambda a: whole(iz, a)])
    with jax.named_scope("sum2"):
        all_more(2, add_up)
        halo_relay(1, 2)
        sum2 = all_end(2, add_up)
    sum2 = scaled(sum2, rstd2)

    def corrections(scale, rstd, sums):
        shift = scale * sums[0:1] / count
        slope = scale * rstd * sums[1:2] / count
        return scale, (shift * pw)[None], (slope * pw)[None]

    def back(grad, centred, scale, shift, slope):
        return grad * scale - (tiles(centred) * slope + shift).reshape(grad.shape)

    out_corr = corrections(scale2, rstd2, sum2)

    def gconv_body(late):
        def body(a, _):
            gp = flat(conv[a])
            t = back(gp, whole(iz, a).astype(f32), *out_corr)
            gch[a + HALO] = tiles(keep(t, late).astype(bf))
            put(iz, a, gp.astype(bf))
            return 0

        return body

    with jax.named_scope("gconv"):
        each(gconv_body, 0)
    halo_in(1, 2)
    fill_halo(
        gch,
        lambda h: back(halo_r[1, h].astype(f32), halo_r[2, h].astype(f32), *out_corr).astype(bf),
    )

    def gact_block(a0, late, carry):
        sa, sb = carry
        n = len(late)
        t = jnp.zeros((n * R, C), f32)
        for tap in range(TAPS):
            t = t + lax.dot_general(
                gch[pl.ds(a0 + TAPS - 1 - tap, n)].reshape(n * R, C), wt[tap], last, preferred_element_type=f32
            )
        for i in range(n):
            centred = flat(summed[a0 + i]) - mean1
            _, slope = gelu_both(centred * scale1 + shift1)
            gl = t[i * R : (i + 1) * R] * slope
            conv[a0 + i] = tiles(gl)
            gm = keep(gl, late[i])
            sa = sa + down_rows(gm)
            sb = sb + down_rows(gm * centred)
        return sa, sb

    with jax.named_scope("grad_act"):
        carry = blocks(gact_block, (zero16, zero16))
    all_start(3, jnp.concatenate([row_sum(carry[0]), row_sum(carry[1]), pad6], axis=0))

    def tap_body(tap, _):
        t = lax.dot_general(
            acth[pl.ds(tap, L)].reshape(z.total, C),
            gch[pl.ds(HALO, L)].reshape(z.total, C),
            first,
            preferred_element_type=f32,
        )
        gb[0, tap] = t[:, :H]
        gb[1, tap] = t[:, H:]
        return 0

    with jax.named_scope("tap_grad"):
        lax.fori_loop(0, EARLY // 2, tap_body, 0)
        all_more(3, add_up)
        lax.fori_loop(EARLY // 2, EARLY, tap_body, 0)
    with jax.named_scope("sum1_wait"):
        sum1 = all_end(3, add_up)
    sum1 = scaled(sum1, rstd1)
    in_corr = corrections(scale1, rstd1, sum1)

    neighbour = (2 * chip + 1 - core, s)
    core_rows = pl.multiple_of(core * H, H)
    other_rows = pl.multiple_of((1 - core) * H, H)
    def slice_of(t):
        return pl.multiple_of(owned(t) * slice_rows, slice_rows)

    chip_rows = slice_of(c1)
    spans = (pl.ds(0, EARLY), pl.ds(EARLY, TAPS + 3 - EARLY))

    core_sends = []

    def grad_core(i):
        cut = (slice(None), spans[i])
        cp = remote(
            gb.at[(*cut, pl.ds(other_rows, H))], gb_core.at[cut], sem_g.at[0, i, 0], sem_g.at[1, i, 0], neighbour
        )
        cp.start()
        core_sends.append(cp)

    def grad_chips(i):
        cut = (slice(None), spans[i])
        core_sends[i].wait_send()
        arrive(gb_core.at[cut], sem_g.at[1, i, 0])
        total = gb[(*cut, pl.ds(core_rows, H))] + gb_core[cut]
        gb_low[cut] = total.astype(bf)
        for d in range(1, z.p1):
            t = lax.rem(c1 + d, z.p1)
            go(
                remote(
                    gb_low.at[(*cut, pl.ds(slice_of(t), slice_rows))],
                    gb_chips.at[(c1, *cut)],
                    sem_g.at[0, i, d],
                    sem_g.at[1, i, d],
                    peer_b(t),
                )
            )

    def grad_pair(i):
        cut = (slice(None), spans[i])
        gb_chips[(c1, *cut)] = gb_low[(*cut, pl.ds(chip_rows, slice_rows))]
        for d in range(1, z.p1):
            arrive(gb_chips.at[(lax.rem(c1 + z.p1 - d, z.p1), *cut)], sem_g.at[1, i, d])
        gb_sum[cut] = add_up([gb_chips[(p, *cut)].astype(f32) for p in range(z.p1)])
        if z.p2 > 1:
            gb_far[(c2, *cut)] = gb_sum[cut].astype(bf)
            for d in range(1, z.p2):
                t = lax.rem(c2 + d, z.p2)
                go(
                    remote(
                        gb_far.at[(c2, *cut)],
                        gb_far.at[(c2, *cut)],
                        sem_g.at[0, i, 24 + d],
                        sem_g.at[1, i, 24 + d],
                        peer_c(t),
                    )
                )
            for d in range(1, z.p2):
                arrive(gb_far.at[(lax.rem(c2 + z.p2 - d, z.p2), *cut)], sem_g.at[1, i, 24 + d])
            gb_sum[cut] = add_up([gb_far[(p, *cut)].astype(f32) for p in range(z.p2)])
        go(remote(gb_sum.at[o, spans[i]], gb_pair.at[spans[i]], sem_g.at[0, i, 8], sem_g.at[1, i, 8], across))

    def grad_back(i):
        arrive(gb_pair.at[spans[i]], sem_g.at[1, i, 8])
        mine = gb_sum[s, spans[i]]
        other = gb_pair[spans[i]]
        own = pl.multiple_of(core_rows + chip_rows, slice_rows)
        gb[0, spans[i], pl.ds(own, slice_rows)] = mine + other
        at = gb.at[0, spans[i], pl.ds(own, slice_rows)]
        for d in range(1, z.p1):
            t = lax.rem(c1 + d, z.p1)
            go(remote(at, at, sem_g.at[0, i, 8 + d], sem_g.at[1, i, 8 + d], peer_b(t)))

    def grad_last(i):
        for d in range(1, z.p1):
            t = lax.rem(c1 + z.p1 - d, z.p1)
            at = pl.multiple_of(core_rows + slice_of(t), slice_rows)
            arrive(gb.at[0, spans[i], pl.ds(at, slice_rows)], sem_g.at[1, i, 8 + d])
        at = gb.at[0, spans[i], pl.ds(core_rows, H)]
        go(remote(at, at, sem_g.at[0, i, 16], sem_g.at[1, i, 16], neighbour))

    def grad_done(i):
        arrive(gb.at[0, spans[i], pl.ds(other_rows, H)], sem_g.at[1, i, 16])

    grad_core(0)

    def grad_body(late):
        def body(a, _):
            gs = back(flat(conv[a]), flat(summed[a]) - mean1, *in_corr)
            gs = keep(gs, late).astype(bf)
            conv[a] = tiles(gs.astype(f32))
            return 0

        return body

    with jax.named_scope("grad_sum"):
        each(grad_body, 0)

    def input_chunk(j):
        a0, a1 = z.chunks[j]
        n = a1 - a0
        span = pl.ds(a0, n)
        summed[span, 0] = jnp.zeros((n, RW, C), f32)
        for v in range(J - 1, 0, -1):
            summed[span, v] = conv[span, v] * edge[1, v : v + 1] + summed[span, kin[0, v]]
        for w in range(J):
            mixed[0, pl.ds(0, n), w] = summed[span, kin[1, w]].astype(bf)
            mixed[1, pl.ds(0, n), w] = (conv[span, par[w]] * edge[2, w : w + 1]).astype(bf)

        def out(i, _):
            t = whole(iz, a0 + i).astype(f32)
            own = (conv[a0 + i] * edge[0][:, None, :]).astype(bf)
            for k, rows in enumerate((own, mixed[0, i], mixed[1, i])):
                t = t + lax.dot_general(
                    flat(rows), ws[:, k * C : (k + 1) * C], last, preferred_element_type=f32
                )
            put(iz, a0 + i, t.astype(bf))
            return 0

        lax.fori_loop(0, n, out, 0)

        ship(iz, ing_own, ing_rcv, sem_i, j)

    def edge_rows_f(v):
        return jnp.concatenate(
            [fx[0, :, pl.ds(v, 1)].reshape(L * RW, H), fx[1, :, pl.ds(v, 1)].reshape(L * RW, H)], axis=1
        )

    def edge_rows_g(v):
        return conv[:, pl.ds(v, 1)].reshape(L * RW, C).astype(bf)

    gb[:, TAPS:] = jnp.zeros((2, 3, C, H), f32)

    dots[...] = jnp.zeros_like(dots)
    unroll = 5 if J % 5 == 0 else 1

    def edge_body(i, _):
        for u in range(unroll):
            v = i * unroll + u
            pv = par[v]
            f_v, f_p, g_v, g_p = edge_rows_f(v), edge_rows_f(pv), edge_rows_g(v), edge_rows_g(pv)
            both = lax.dot_general(
                f_v, jnp.concatenate([g_v, g_p], axis=1), first, preferred_element_type=f32
            )
            up_prod = lax.dot_general(f_p, g_v, first, preferred_element_type=f32)
            for k, prod in enumerate((both[:, :C], up_prod, both[:, C:])):
                part = prod * edge[k, pl.ds(v, 1)]
                for h in range(2):
                    j = 2 * k + h
                    gb[j // 3, TAPS + j % 3] += part[:, h * H : (h + 1) * H]
                dots[k, pl.ds(v, 1)] = row_sum(prod * ws[:, k * C : (k + 1) * C].astype(f32))
        return 0

    def edges():
        lax.fori_loop(0, J // unroll, edge_body, 0)
        ones = jnp.ones((8, C), f32)
        rows = [
            lax.dot_general(ones, dots[k], last, precision=exact_mode, preferred_element_type=f32)[0:1]
            for k in range(3)
        ]
        val = jnp.concatenate(rows + [jnp.zeros((5, H), f32)], axis=0)
        return jnp.concatenate([val, jnp.zeros((8, C - H), f32)], axis=1)

    input_chunk(0)
    grad_chips(0)
    with jax.named_scope("tap_grad_late"):
        lax.fori_loop(EARLY, TAPS, tap_body, 0)
    for j in range(1, n_chunks // 2):
        input_chunk(j)
    grad_pair(0)
    with jax.named_scope("edges"):
        dvec = edges()
    grad_core(1)
    for j in range(n_chunks // 2, n_chunks):
        input_chunk(j)
        if j == n_chunks // 2:
            grad_chips(1)
            all_start(4, dvec)
            grad_back(0)
    with jax.named_scope("grad_reduce"):
        grad_pair(1)
        all_more(4, add_up)
        grad_last(0)
        grad_back(1)
        dvec = all_end(4, add_up)
        grad_last(1)
    for k in range(3):
        per_edge = dvec[k : k + 1, :J]
        if k == 1:
            per_edge = lax.dot_general(
                eye, jnp.broadcast_to(per_edge, (J, J)), last, precision=exact_mode, preferred_element_type=f32
            )
        ig_out[k] = adj[k] * per_edge
    for i, row in enumerate((sum1[1:2], sum1[0:1], sum2[1:2], sum2[0:1])):
        sums_out[i : i + 1] = jnp.where(s == 0, row[:, :H], row[:, H:])
    sums_out[4:8] = jnp.zeros((4, H), f32)
    with jax.named_scope("grad_reduce_end"):
        grad_done(0)
        grad_done(1)
        last_out = [pltpu.make_async_copy(gb.at[0, pl.ds(0, TAPS)], tg_out, sem_l.at[2, 2])]
        for j in range(3):
            last_out.append(
                pltpu.make_async_copy(gb.at[0, TAPS + j], sg_out.at[:, pl.ds(j * H, H)], sem_l.at[2, 3 + j])
            )
        for cp in last_out:
            cp.start()

    with jax.named_scope("last_waits"):
        for j in range(n_chunks):
            a0, a1 = z.chunks[j]
            at = pl.ds(a0, a1 - a0)
            arrive(act_rcv.at[at], sem_a.at[1, j])
            arrive(ing_rcv.at[at], sem_i.at[1, j])
        for cp in outs + last_out:
            cp.wait()
        for cp in sends:
            cp.wait_send()


def finish(
    z,
    act_own,
    act_rcv,
    ing_own,
    ing_rcv,
    tg_in,
    sg_in,
    sums_in,
    ig_in,
    act_out,
    ing_out,
    tg_out,
    sg_out,
    r0,
    r1,
    r2,
    r3,
    ig_out,
    low_act,
    low_ing,
    full,
    tg,
    sg,
    sem_in,
    sem_out,
):
    J, L = z.joints, z.blk
    s = lax.axis_index("sub")
    jobs = [(act_own, act_out, s), (act_rcv, act_out, 1 - s), (ing_own, ing_out, s), (ing_rcv, ing_out, 1 - s)]
    ins = []
    for i, (src, _, _) in enumerate(jobs):
        cp = pltpu.make_async_copy(src, (low_act if i < 2 else low_ing).at[i % 2], sem_in.at[i])
        cp.start()
        ins.append(cp)
    grads = []
    for i, (src, mid, dst) in enumerate(((tg_in, tg, tg_out), (sg_in, sg, sg_out))):
        cp = pltpu.make_async_copy(src, mid, sem_in.at[4 + i])
        cp.start()
        grads.append((cp, pltpu.make_async_copy(mid, dst, sem_in.at[6 + i])))
    for i, r in enumerate((r0, r1, r2, r3)):
        r[...] = sums_in[i : i + 1]
    ig_out[...] = ig_in[...]
    cut = L - z.pad
    fr = full.reshape(4, L, J, RW, z.half)
    lows = (low_act.reshape(2, L, J, RW, z.half), low_ing)

    def pieces(i, dst, w):
        for part, (a0, a1) in enumerate(z.locals):
            for b in range(NB):
                cp = pltpu.make_async_copy(
                    full.at[i, pl.ds(a0, a1 - a0), :, b],
                    dst.at[pl.ds(w * z.win + b * L + a0, a1 - a0)],
                    sem_out.at[i, part, b],
                )
                yield part == 1 and b == NB - 1, cp

    for i, (_, dst, w) in enumerate(jobs):
        ins[i].wait()

        def body(a, _, i=i):
            fr[i, a] = lows[i // 2][i % 2, a].astype(jnp.float32)
            return 0

        lax.fori_loop(0, L, body, 0)
        for beyond, cp in pieces(i, dst, w):
            if beyond:
                pl.when(w == 0)(cp.start)
            else:
                cp.start()
    for cp_in, cp_out in grads:
        cp_in.wait()
        cp_out.start()
    for _, cp_out in grads:
        cp_out.wait()
    for i, (_, dst, w) in enumerate(jobs):
        for beyond, cp in pieces(i, dst, w):
            if beyond:
                pl.when(w == 0)(cp.wait)
            else:
                cp.wait()


def block(
    n_dp, features, presence, parents, w_spatial, importance, gain_one, shift_one, w_temporal, gain_two, shift_two, cotangent
):
    _, _, frames, joints, half = features.shape
    z = Sizes(n_dp, frames, joints, half)
    f32, bf = jnp.float32, jnp.bfloat16
    C, H, L, R, J = z.chan, z.half, z.blk, z.rows, z.joints

    def natural(x):
        return x.transpose(0, 2, 3, 1, 4).reshape(frames, joints, 2, half)

    any_, vmem, smem = (pl.BlockSpec(memory_space=m) for m in (pl.ANY, pltpu.VMEM, pltpu.SMEM))
    landing = (L, J, NB, 2, H)
    blocked = (L, J, RW, H)
    sds = jax.ShapeDtypeStruct
    VM, DMA = pltpu.VMEM, pltpu.SemaphoreType.DMA
    nch = len(z.chunks)
    outs = pl.pallas_call(
        functools.partial(mega, z),
        name="graph_conv_block",
        out_shape=[sds(landing, bf)] * 2
        + [sds(blocked, bf)] * 2
        + [sds((TAPS, C, H), f32), sds((C, 3 * H), f32), sds((8, H), f32), sds((3, J, J), f32)],
        in_specs=[any_] * 4 + [vmem, smem, smem] + [vmem] * 4,
        out_specs=[any_] * 6 + [vmem] * 2,
        scratch_shapes=[
            VM((2,) + landing, bf),
            VM((2,) + landing, bf),
            VM((2,) + blocked, bf),
            VM((TAPS, C, C), bf),
            VM((C, 3 * C), bf),
            VM((L, J, RW, C), f32),
            VM((L + 2 * HALO, J, RW, C), bf),
            VM((L, J, RW, C), f32),
            VM((L + 2 * HALO, J, RW, C), bf),
            VM((2,) + blocked, bf),
            VM((2, TAPS + 3, C, H), f32),
            VM((2, TAPS + 3, H, H), f32),
            VM((2, TAPS + 3, H, H), bf),
            VM((z.p1, 2, TAPS + 3, H // z.p1, H), bf),
            VM((z.p2, 2, TAPS + 3, H // z.p1, H), bf),
            VM((2, TAPS + 3, H // z.p1, H), f32),
            VM((TAPS + 3, H // z.p1, H), f32),
            VM((2, max(a1 - a0 for a0, a1 in z.chunks), J, RW, C), bf),
            VM((3, H, C), f32),
            VM((2, 8, H), f32),
            VM((3, J, J), f32),
            VM((3, J, C), f32),
            pltpu.SMEM((2, J), jnp.int32),
            VM((3, HALO, 64, C), bf),
            VM((3, HALO, 64, C), bf),
            VM((3, HALO, 64, C), bf),
            VM((5, z.near, 8, C), f32),
            VM((5, z.p2, 8, C), f32),
            VM((5, 2, 8, C), f32),
            DMA((3, 2 * NB)),
            DMA((2, nch, NB)),
            DMA((2, nch, NB)),
            DMA((3, nch)),
            DMA((3, nch)),
            DMA((2, 40)),
            DMA((2, 2, 2)),
            DMA((2, 2, 32)),
            DMA((2, 5, z.near)),
            DMA((2, 5, z.p2)),
            DMA((2, 5)),
        ],
        compiler_params=pltpu.CompilerParams(
            collective_id=0, has_side_effects=True, vmem_limit_bytes=63 * 2**20
        ),
    )(
        natural(features),
        natural(cotangent),
        w_temporal,
        w_spatial,
        importance,
        parents,
        presence,
        *(v.reshape(1, H) for v in (gain_one, shift_one, gain_two, shift_two)),
    )
    act, ing, tg, sg, r0, r1, r2, r3, ig = pl.pallas_call(
        functools.partial(finish, z),
        name="natural_order",
        out_shape=[sds((frames, joints, 2, H), f32)] * 2
        + [sds((TAPS, C, H), f32), sds((C, 3 * H), f32)]
        + [sds((1, H), f32)] * 4
        + [sds((3, J, J), f32)],
        in_specs=[any_] * 6 + [vmem] * 2,
        out_specs=[any_] * 4 + [vmem] * 5,
        scratch_shapes=[
            VM((2,) + landing, bf),
            VM((2,) + blocked, bf),
            VM((4,) + landing, f32),
            VM((TAPS, C, H), f32),
            VM((C, 3 * H), f32),
            DMA((8,)),
            DMA((4, 2, NB)),
        ],
        compiler_params=pltpu.CompilerParams(vmem_limit_bytes=60 * 2**20),
    )(*outs)

    def back(x):
        return x.reshape(1, frames, joints, 2, half).transpose(0, 3, 1, 2, 4)

    return (
        back(act),
        back(ing),
        sg,
        ig,
        *(r.reshape(H) for r in (r0, r1)),
        tg,
        *(r.reshape(H) for r in (r2, r3)),
    )


def solution(mesh):
    in_specs = (
        P("dp", None, None, None, "sub"),
        P("dp", None),
        P(),
        P(None, "sub"),
        P(),
        P("sub"),
        P("sub"),
        P(None, None, "sub"),
        P("sub"),
        P("sub"),
        P("dp", None, None, None, "sub"),
    )
    out_specs = (
        P("dp", None, None, None, "sub"),
        P("dp", None, None, None, "sub"),
        P(None, "sub"),
        P(),
        P("sub"),
        P("sub"),
        P(None, None, "sub"),
        P("sub"),
        P("sub"),
    )
    return jax.shard_map(
        functools.partial(block, mesh.shape["dp"]), mesh=mesh, in_specs=in_specs, out_specs=out_specs, check_vma=False
    )
```

```python
import functools

import jax
import jax.numpy as jnp
from jax import lax
from jax.experimental import pallas as pl
from jax.experimental.pallas import tpu as pltpu
from jax.sharding import PartitionSpec as P

norm_eps = 1e-05
exact_mode = lax.Precision.HIGHEST
MESH = pl.DeviceIdType.MESH
TAPS = 9
EARLY = 7
HALO = TAPS // 2
NB = 8
RW = 2 * NB
G = 4
tanh_scale = 0.7978845608028654
tanh_cubic = 0.044715


def gelu(x):
    t = jnp.tanh(x * (tanh_scale + (tanh_scale * tanh_cubic) * (x * x)))
    return x * (0.5 + 0.5 * t)


def gelu_both(x):
    x2 = x * x
    h = 0.5 + 0.5 * jnp.tanh(x * (tanh_scale + (tanh_scale * tanh_cubic) * x2))
    rise = x * (2.0 * tanh_scale + (6.0 * tanh_scale * tanh_cubic) * x2)
    return x * h, h + h * ((1.0 - h) * rise)


class Sizes:
    def __init__(self, n_dp, frames, joints, half):
        self.n_dp, self.frames, self.joints, self.half = n_dp, frames, joints, half
        self.chan = 2 * half
        self.blk = -(-frames // (2 * NB))
        self.win = self.blk * NB
        self.pad = 2 * self.win - frames
        self.rows = joints * RW
        self.total = self.blk * self.rows
        self.chips = n_dp // 2
        self.p1 = 8
        self.p2 = self.chips // self.p1
        self.near = 2 * self.p1
        cut = self.blk - self.pad
        step = -(-cut // 3)
        self.chunks = [(a, min(a + step, cut)) for a in range(0, cut, step)]
        if self.pad:
            self.chunks.append((cut, self.blk))
        self.locals = [(0, cut)] + ([(cut, self.blk)] if self.pad else [])


def mega(
    z,
    feat,
    cot,
    wt_in,
    ws_in,
    imp,
    par,
    pres,
    g1,
    b1,
    g2,
    b2,
    act_own,
    act_rcv,
    ing_own,
    ing_rcv,
    tg_out,
    sg_out,
    sums_out,
    ig_out,
    xh,
    ct,
    fx,
    wt,
    ws,
    summed,
    acth,
    conv,
    gch,
    iz,
    gb,
    gb_core,
    gb_low,
    gb_chips,
    gb_far,
    gb_sum,
    gb_pair,
    gb_fin,
    mixed,
    dots,
    prm,
    adj,
    edge,
    kin,
    halo_s,
    halo_m,
    halo_r,
    arA,
    arC,
    arD,
    sem_l,
    sem_f,
    sem_c,
    sem_a,
    sem_i,
    sem_w,
    sem_h,
    sem_g,
    semA,
    semC,
    semD,
):
    f32, bf = jnp.float32, jnp.bfloat16
    J, C, H, L, R = z.joints, z.chan, z.half, z.blk, z.rows
    s = lax.axis_index("sub")
    dp = lax.axis_index("dp")
    o = 1 - s
    core = lax.rem(dp, 2)
    chip = lax.div(dp, 2)
    c1 = lax.rem(chip, z.p1)
    c2 = lax.div(chip, z.p1)
    partner = (dp, o)

    d1 = lax.rem(dp, z.near)
    flip = dp + 4 - 8 * lax.rem(lax.div(dp, 4), 2)
    across = (flip, o)
    beside = (flip, s)

    def peer_b(t):
        return (2 * (c2 * z.p1 + t) + core, s)

    def peer_c(t):
        return (2 * (t * z.p1 + c1) + core, s)

    def peer_0(t):
        return (c2 * z.near + t, s)

    def other_chip(t):
        return t + 2 - 4 * lax.rem(lax.div(t, 2), 2)

    def owned(t):
        return t + s * (other_chip(t) - t)

    def remote(src, dst, ssem, rsem, dev):
        return pltpu.make_async_remote_copy(
            src_ref=src,
            dst_ref=dst,
            send_sem=ssem,
            recv_sem=rsem,
            device_id=dev,
            device_id_type=MESH,
        )

    bar = pltpu.get_barrier_semaphore()
    greeted = [partner, across]
    greeted += [peer_0(lax.rem(d1 + d, z.near)) for d in range(1, z.near)]
    greeted += [peer_c(lax.rem(c2 + d, z.p2)) for d in range(1, z.p2)]
    for dev in greeted:
        pl.semaphore_signal(bar, inc=1, device_id=dev, device_id_type=MESH)

    def frame_row(w, b, a0, a1):
        at = w * z.win + (b * L + a0)
        if b == NB - 1 and z.pad and a0 >= L - z.pad:
            at = at - w * z.pad
        return at

    local = []
    for which, (src, dst) in enumerate(((feat, xh), (cot, ct))):
        for i, (a0, a1) in enumerate(z.locals):
            for b in range(NB):
                cp = pltpu.make_async_copy(
                    src.at[pl.ds(frame_row(s, b, a0, a1), a1 - a0)],
                    dst.at[s, pl.ds(a0, a1 - a0), :, b],
                    sem_l.at[which, i * NB + b],
                )
                cp.start()
                local.append(cp)
    lw = [
        pltpu.make_async_copy(ws_in, ws.at[:, pl.ds(pl.multiple_of(s * 3 * H, H), 3 * H)], sem_l.at[2, 0]),
        pltpu.make_async_copy(wt_in, wt.at[:, :, pl.ds(pl.multiple_of(s * H, H), H)], sem_l.at[2, 1]),
    ]
    for cp in lw:
        cp.start()
    for i, v in enumerate((g1, b1, g2, b2)):
        prm[s, i : i + 1] = v[...]

    with jax.named_scope("barrier"):
        pl.semaphore_wait(bar, len(greeted))

    slice_rows = H // z.p1
    row0 = pl.multiple_of(core * H + c1 * slice_rows, slice_rows)

    def ws_at(half, r0, n):
        return ws.at[pl.ds(r0, n), pl.ds(pl.multiple_of(half * 3 * H, H), 3 * H)]

    def wt_at(half, r0, n):
        return wt.at[:, pl.ds(r0, n), pl.ds(pl.multiple_of(half * H, H), H)]

    sends = []

    def go(cp):
        cp.start()
        sends.append(cp)
        return cp

    def arrive(dst, rsem):
        remote(dst, dst, rsem, rsem, partner).wait_recv()

    go(remote(prm.at[s], prm.at[s], sem_w.at[0, 0], sem_w.at[1, 0], partner))
    go(remote(ws_in.at[pl.ds(row0, slice_rows)], ws_at(s, row0, slice_rows), sem_w.at[0, 1], sem_w.at[1, 1], partner))
    go(remote(wt_in.at[:, pl.ds(row0, slice_rows)], wt_at(s, row0, slice_rows), sem_w.at[0, 2], sem_w.at[1, 2], partner))

    def send_rows(src, dst, sem, j):
        a0, a1 = z.chunks[j]
        for b in range(NB):
            go(
                remote(
                    src.at[pl.ds(frame_row(o, b, a0, a1), a1 - a0)],
                    dst.at[s, pl.ds(a0, a1 - a0), :, b],
                    sem.at[0, j, b],
                    sem.at[1, j, b],
                    partner,
                )
            )

    def take_rows(dst, sem, j):
        a0, a1 = z.chunks[j]
        for b in range(NB):
            arrive(dst.at[o, pl.ds(a0, a1 - a0), :, b], sem.at[1, j, b])

    n_chunks = len(z.chunks)
    for j in range(n_chunks):
        send_rows(feat, xh, sem_f, j)
    order = [n_chunks - 1] + list(range(n_chunks - 1))
    for j in order:
        send_rows(cot, ct, sem_c, j)

    ri = lax.broadcasted_iota(jnp.int32, (J, J), 0)
    ci = lax.broadcasted_iota(jnp.int32, (J, J), 1)
    eye = jnp.where(ri == ci, 1.0, 0.0).astype(f32)
    up = jnp.zeros((J, J), f32)
    down = jnp.zeros((J, J), f32)
    for v in range(1, J):
        pv = par[v]
        up = jnp.where((ri == v) & (ci == pv), 1.0, up)
        down = jnp.where((ci == v) & (ri == pv), 1.0, down)
    degree = jnp.sum(eye + up + down, axis=0, keepdims=True)
    adjacent = [eye / degree, up / degree, down / degree]
    mixing = [adjacent[k] * imp[k] for k in range(3)]
    for k in range(3):
        adj[k] = adjacent[k]
    last = (((1,), (1,)), ((), ()))
    first = (((0,), (0,)), ((), ()))
    wide = jnp.ones((J, C), f32)
    edge[0] = jnp.dot(mixing[0], wide, precision=exact_mode, preferred_element_type=f32)
    edge[1] = jnp.dot(mixing[1], wide, precision=exact_mode, preferred_element_type=f32)
    edge[2] = lax.dot_general(mixing[2], wide, first, precision=exact_mode, preferred_element_type=f32)

    def kin_body(v, _):
        pv = par[v]
        sibling = jnp.int32(0)
        child = jnp.int32(0)
        for w in range(J - 1, 0, -1):
            pw_ = par[w]
            sibling = jnp.where((pw_ == pv) & (w > v), w, sibling)
            child = jnp.where(pw_ == v, w, child)
        kin[0, v] = sibling
        kin[1, v] = child
        return 0

    lax.fori_loop(0, J, kin_body, 0)

    for i, at in ((0, ws_at), (1, wt_at)):
        arrive(at(o, row0, slice_rows), sem_w.at[1, 1 + i])
        for d in range(1, z.p1):
            t = lax.rem(c1 + d, z.p1)
            go(
                remote(
                    at(o, row0, slice_rows),
                    at(o, row0, slice_rows),
                    sem_w.at[0, 4 + i * 16 + d],
                    sem_w.at[1, 4 + i * 16 + d],
                    peer_b(t),
                )
            )
    for i, at in ((0, ws_at), (1, wt_at)):
        for d in range(1, z.p1):
            t = lax.rem(c1 + z.p1 - d, z.p1)
            arrive(
                at(o, pl.multiple_of(core * H + t * slice_rows, slice_rows), slice_rows),
                sem_w.at[1, 4 + i * 16 + d],
            )
        mine = pl.multiple_of(core * H, H)
        go(remote(at(o, mine, H), at(o, mine, H), sem_w.at[0, 36 + i], sem_w.at[1, 36 + i], (2 * chip + 1 - core, s)))
    theirs = pl.multiple_of((1 - core) * H, H)
    arrive(ws_at(o, theirs, H), sem_w.at[1, 36])
    for cp in lw:
        cp.wait()
    arrive(prm.at[o], sem_w.at[1, 0])
    p0 = pres[0, 0].astype(f32)
    p1 = pres[0, 1].astype(f32)
    ri16 = lax.broadcasted_iota(jnp.int32, (RW, C), 0)
    pw = jnp.where((ri16 & 1) == 0, p0, p1).astype(f32)
    tail = jnp.where(ri16 >= RW - 2, 1.0, 0.0).astype(f32)
    side = s.astype(f32)

    real = 1.0 - tail * side
    cut = L - z.pad

    def tiles(x):
        return x.reshape(-1, RW, C)

    def flat(x):
        return x.reshape(R, C)

    def keep(x, late):
        return (tiles(x) * real[None]).reshape(x.shape) if late else x

    def down_rows(x):
        return jnp.sum(tiles(x), axis=0)

    def each(body, carry):
        carry = lax.fori_loop(0, cut, body(False), carry)
        return lax.fori_loop(cut, L, body(True), carry) if z.pad else carry

    def row_sum(x):
        return jnp.sum(x, axis=0, keepdims=True)

    def param(i):
        return jnp.concatenate([prm[0, i : i + 1], prm[1, i : i + 1]], axis=1)

    def whole(ref, a):
        return jnp.concatenate([ref[0, a].reshape(R, H), ref[1, a].reshape(R, H)], axis=1)

    def put(ref, a, value):
        for h in range(2):
            ref[h, a] = value[:, h * H : (h + 1) * H].reshape(J, RW, H)

    def land(ref, a, value):
        for h in range(2):
            ref[h, a] = value[:, h * H : (h + 1) * H].reshape(J, NB, 2, H)

    def spread(buf, sem, r, q, n, peer, val):
        buf[r, q] = val
        for d in range(1, n):
            go(remote(buf.at[r, q], buf.at[r, q], sem.at[0, r, d], sem.at[1, r, d], peer(lax.rem(q + d, n))))

    def gather(buf, sem, r, q, n):
        for d in range(1, n):
            arrive(buf.at[r, lax.rem(q + n - d, n)], sem.at[1, r, d])
        return [buf[r, i] for i in range(n)]

    def add_up(parts):
        t = parts[0]
        for x in parts[1:]:
            t = t + x
        return t

    def merge(parts):
        n = add_up([x[0:1] for x in parts])
        below = jnp.maximum(n, 1.0)
        mean = add_up([x[0:1] * x[1:2] for x in parts]) / below
        spread_up = add_up([x[2:3] + x[0:1] * (x[1:2] - mean) * (x[1:2] - mean) for x in parts])
        return jnp.concatenate([n, mean, spread_up, jnp.zeros((5, C), f32)], axis=0)

    def all_start(r, val):
        spread(arA, semA, r, d1, z.near, peer_0, val)

    def all_more(r, join):
        val = join(gather(arA, semA, r, d1, z.near))
        if z.p2 > 1:
            spread(arC, semC, r, c2, z.p2, peer_c, val)
            val = join(gather(arC, semC, r, c2, z.p2))
        arD[r, s] = val
        go(remote(arD.at[r, s], arD.at[r, s], semD.at[0, r], semD.at[1, r], across))

    def all_end(r, join):
        arrive(arD.at[r, o], semD.at[1, r])
        return join([arD[r, 0], arD[r, 1]])

    def moments(val_k, s1, s2):
        n = (p0 + p1) * (z.win - z.pad * side) * J
        below = jnp.maximum(n, 1.0)
        s1, s2 = row_sum(s1), row_sum(s2)
        return jnp.concatenate(
            [jnp.zeros((1, C), f32) + n, val_k + s1 / below, s2 - s1 * s1 / below, jnp.zeros((5, C), f32)], axis=0
        )

    def scaled(sums, rstd):
        return jnp.concatenate([sums[0:1], sums[1:2] * rstd], axis=0)

    zero16 = jnp.zeros((RW, C), f32)
    zero1 = jnp.zeros((1, C), f32)

    def spatial_chunk(a0, a1, carry):
        k_shift, s1, s2 = carry
        n = a1 - a0
        span, up_at, down_at, link = pl.ds(a0, n), pl.ds(0, n), pl.ds(n, n), pl.ds(2 * n, n)

        def body(i, _):
            f = whole(xh, a0 + i)
            put(fx, a0 + i, f)
            for k, (buf, at) in enumerate(((summed, a0 + i), (conv, i), (conv, n + i))):
                buf[at] = tiles(jnp.dot(f, ws[:, k * C : (k + 1) * C], preferred_element_type=f32))
            return 0

        lax.fori_loop(0, n, body, 0)
        conv[link, 0] = jnp.zeros((n, RW, C), f32)
        for v in range(J - 1, 0, -1):
            conv[link, v] = conv[down_at, v] * edge[2, v : v + 1] + conv[link, kin[0, v]]
        w = (pw * real if a0 >= cut else pw)[None]
        for v in range(J):
            t = summed[span, v] * edge[0, v : v + 1] + conv[link, kin[1, v]]
            if v:
                t = t + conv[up_at, par[v]] * edge[1, v : v + 1]
            summed[span, v] = t
            if a0 == 0 and v == 0:
                k_shift = row_sum(jnp.sum(t, axis=0)) * (1.0 / (n * RW))
            d = t - k_shift
            wd = d * w
            s1 = s1 + jnp.sum(wd, axis=0)
            s2 = s2 + jnp.sum(wd * d, axis=0)
        return k_shift, s1, s2

    carry = (zero1, zero16, zero16)
    n_local = len(z.locals) * NB
    for cp in local[:n_local]:
        cp.wait()
    for j, (a0, a1) in enumerate(z.chunks):
        with jax.named_scope("features_wait"):
            take_rows(xh, sem_f, j)
        with jax.named_scope("spatial"):
            carry = spatial_chunk(a0, a1, carry)

    per = 2 * J
    packed = -(-HALO * per // RW) * RW
    lane = lax.broadcasted_iota(jnp.int32, (packed, R), 1)
    line = lax.broadcasted_iota(jnp.int32, (packed, R), 0)
    off = (RW - 2) * o

    def pick(h):
        at = line - h * per
        hit = lane == lax.shift_right_arithmetic(at, 1) * RW + off + (at & 1)
        return jnp.where(hit & (at >= 0) & (at < per), 1.0, 0.0).astype(bf)

    edge_a = (L - HALO) * o

    def halo_rows(slot, ref):
        rows = jnp.zeros((packed, C), f32)
        for h in range(HALO):
            rows = rows + jnp.dot(pick(h), ref(edge_a + h).astype(bf), preferred_element_type=f32)
        halo_s[slot] = rows.astype(bf)

    def halo_send(r, n, src, dst, hop, dev):
        at = pl.ds(r, n)
        go(remote(src.at[at], dst.at[at], sem_h.at[0, r, hop], sem_h.at[1, r, hop], dev))

    def halo_wait(r, n, dst, hop):
        arrive(dst.at[pl.ds(r, n)], sem_h.at[1, r, hop])

    row_in = lax.broadcasted_iota(jnp.int32, (R, C), 0) & (RW - 1)
    fside = 1.0 - side

    def fill_halo(buf, fresh):
        for h in range(HALO):
            extra = lax.dot_general(pick(h), fresh, first, preferred_element_type=f32)
            lower = pltpu.roll(buf[L + h].reshape(R, C).astype(f32), 2, 0)
            lower = jnp.where(row_in < 2, extra * side, lower)
            buf[h] = tiles(lower.astype(bf))
            upper = pltpu.roll(buf[HALO + h].reshape(R, C).astype(f32), R - 2, 0)
            upper = jnp.where(row_in >= RW - 2, extra * fside, upper)
            buf[HALO + L + h] = tiles(upper.astype(bf))

    all_start(0, moments(*carry))
    halo_rows(0, lambda a: flat(summed[a]))
    halo_send(0, 1, halo_s, halo_m, 0, across)
    with jax.named_scope("st1"):
        all_more(0, merge)
        halo_wait(0, 1, halo_m, 0)
        halo_send(0, 1, halo_m, halo_r, 1, beside)
        st1 = all_end(0, merge)
    count = jnp.maximum(st1[0:1], 1.0)
    mean1 = st1[1:2]
    rstd1 = lax.rsqrt(st1[2:3] / count + norm_eps)
    gain1, shift1 = param(0), param(1)
    scale1 = rstd1 * gain1

    def act_body(late):
        def body(a, _):
            t = gelu((flat(summed[a]) - mean1) * scale1 + shift1)
            acth[a + HALO] = tiles(keep(t, late).astype(bf))
            return 0

        return body

    with jax.named_scope("act"):
        each(act_body, 0)
    halo_wait(0, 1, halo_r, 1)
    fill_halo(acth, gelu((halo_r[0].astype(f32) - mean1) * scale1 + shift1).astype(bf))

    arrive(wt_at(o, theirs, H), sem_w.at[1, 37])

    def conv_block(a0, late, carry):
        k_shift, s1, s2 = carry
        n = len(late)
        t = jnp.zeros((n * R, C), f32)
        for tap in range(TAPS):
            t = t + jnp.dot(acth[pl.ds(a0 + tap, n)].reshape(n * R, C), wt[tap], preferred_element_type=f32)
        conv[pl.ds(a0, n)] = t.reshape(n, J, RW, C)
        k_shift = jnp.where(a0 == 0, row_sum(t[:R]) * (1.0 / R), k_shift)
        for i in range(n):
            w = pw * real if late[i] else pw
            d = tiles(t[i * R : (i + 1) * R] - k_shift)
            wd = d * w[None]
            s1 = s1 + jnp.sum(wd, axis=0)
            s2 = s2 + jnp.sum(wd * d, axis=0)
        return k_shift, s1, s2

    def blocks(fun, carry):
        plain = cut // G
        carry = lax.fori_loop(0, plain, lambda i, c: fun(i * G, [False] * G, c), carry)
        for a0 in range(plain * G, L, G):
            carry = fun(a0, [a >= cut for a in range(a0, min(a0 + G, L))], carry)
        return carry

    with jax.named_scope("conv"):
        carry = blocks(conv_block, (zero1, zero16, zero16))
    all_start(1, moments(*carry))
    with jax.named_scope("st2"):
        all_more(1, merge)
        st2 = all_end(1, merge)
    mean2 = st2[1:2]
    rstd2 = lax.rsqrt(st2[2:3] / count + norm_eps)
    gain2, shift2 = param(2), param(3)

    for cp in local[n_local:]:
        cp.wait()

    scale2 = rstd2 * gain2

    def out_body(late):
        def body(a, carry):
            sa, sb = carry
            centred = flat(conv[a]) - mean2
            level = centred * scale2 + (shift2 + whole(fx, a).astype(f32))
            value, slope = gelu_both(level)
            land(xh, a, value.astype(bf))
            gp = whole(ct, a).astype(f32) * slope
            conv[a] = tiles(gp)
            put(iz, a, centred.astype(bf))
            gm = keep(gp, late)
            return sa + down_rows(gm), sb + down_rows(gm * centred)

        return body

    carry = (zero16, zero16)
    outs = []

    def ship(buf, own, rcv, sem, j):
        a0, a1 = z.chunks[j]
        at = pl.ds(a0, a1 - a0)
        go(remote(buf.at[o, at], rcv.at[at], sem.at[0, j], sem.at[1, j], partner))
        cp = pltpu.make_async_copy(buf.at[s, at], own.at[at], sem.at[2, j])
        cp.start()
        outs.append(cp)

    for i, j in enumerate(order):
        a0, a1 = z.chunks[j]
        with jax.named_scope("cotangent_wait"):
            take_rows(ct, sem_c, j)
        with jax.named_scope("level_two"):
            carry = lax.fori_loop(a0, a1, out_body(a0 >= cut), carry)
        if i == 1:
            halo_rows(1, lambda a: flat(conv[a]))
            halo_rows(2, lambda a: whole(iz, a))
            halo_send(1, 2, halo_s, halo_r, 0, partner)
            ship(xh, act_own, act_rcv, sem_a, order[0])
        if i >= 1:
            ship(xh, act_own, act_rcv, sem_a, j)

    pad6 = jnp.zeros((6, C), f32)
    all_start(2, jnp.concatenate([row_sum(carry[0]), row_sum(carry[1]), pad6], axis=0))
    with jax.named_scope("sum2"):
        all_more(2, add_up)
        sum2 = all_end(2, add_up)
    sum2 = scaled(sum2, rstd2)

    def corrections(scale, rstd, sums):
        shift = scale * sums[0:1] / count
        slope = scale * rstd * sums[1:2] / count
        return scale, (shift * pw)[None], (slope * pw)[None]

    def back(grad, centred, scale, shift, slope):
        return grad * scale - (tiles(centred) * slope + shift).reshape(grad.shape)

    out_corr = corrections(scale2, rstd2, sum2)

    def gconv_body(late):
        def body(a, _):
            gp = flat(conv[a])
            t = back(gp, whole(iz, a).astype(f32), *out_corr)
            gch[a + HALO] = tiles(keep(t, late).astype(bf))
            put(iz, a, gp.astype(bf))
            return 0

        return body

    with jax.named_scope("gconv"):
        each(gconv_body, 0)
    halo_wait(1, 2, halo_r, 0)
    fill_halo(
        gch,
        back(halo_r[1].astype(f32), halo_r[2].astype(f32), *out_corr).astype(bf),
    )

    def gact_block(a0, late, carry):
        sa, sb = carry
        n = len(late)
        t = jnp.zeros((n * R, C), f32)
        for tap in range(TAPS):
            t = t + lax.dot_general(
                gch[pl.ds(a0 + TAPS - 1 - tap, n)].reshape(n * R, C), wt[tap], last, preferred_element_type=f32
            )
        for i in range(n):
            centred = flat(summed[a0 + i]) - mean1
            _, slope = gelu_both(centred * scale1 + shift1)
            gl = t[i * R : (i + 1) * R] * slope
            conv[a0 + i] = tiles(gl)
            gm = keep(gl, late[i])
            sa = sa + down_rows(gm)
            sb = sb + down_rows(gm * centred)
        return sa, sb

    with jax.named_scope("grad_act"):
        carry = blocks(gact_block, (zero16, zero16))
    all_start(3, jnp.concatenate([row_sum(carry[0]), row_sum(carry[1]), pad6], axis=0))

    def tap_body(tap, _):
        t = lax.dot_general(
            acth[pl.ds(tap, L)].reshape(z.total, C),
            gch[pl.ds(HALO, L)].reshape(z.total, C),
            first,
            preferred_element_type=f32,
        )
        gb[0, tap] = t[:, :H]
        gb[1, tap] = t[:, H:]
        return 0

    with jax.named_scope("tap_grad"):
        lax.fori_loop(0, EARLY // 2, tap_body, 0)
        all_more(3, add_up)
        lax.fori_loop(EARLY // 2, EARLY, tap_body, 0)
    with jax.named_scope("sum1_wait"):
        sum1 = all_end(3, add_up)
    sum1 = scaled(sum1, rstd1)
    in_corr = corrections(scale1, rstd1, sum1)

    neighbour = (2 * chip + 1 - core, s)
    core_rows = pl.multiple_of(core * H, H)
    other_rows = pl.multiple_of((1 - core) * H, H)
    def slice_of(t):
        return pl.multiple_of(owned(t) * slice_rows, slice_rows)

    chip_rows = slice_of(c1)
    spans = (pl.ds(0, EARLY), pl.ds(EARLY, TAPS + 3 - EARLY))

    def grad_core(i):
        cut = (slice(None), spans[i])
        go(
            remote(
                gb.at[(*cut, pl.ds(other_rows, H))], gb_core.at[cut], sem_g.at[0, i, 0], sem_g.at[1, i, 0], neighbour
            )
        )

    def grad_chips(i):
        cut = (slice(None), spans[i])
        arrive(gb_core.at[cut], sem_g.at[1, i, 0])
        total = gb[(*cut, pl.ds(core_rows, H))] + gb_core[cut]
        gb_low[cut] = total.astype(bf)
        for d in range(1, z.p1):
            t = lax.rem(c1 + d, z.p1)
            go(
                remote(
                    gb_low.at[(*cut, pl.ds(slice_of(t), slice_rows))],
                    gb_chips.at[(c1, *cut)],
                    sem_g.at[0, i, d],
                    sem_g.at[1, i, d],
                    peer_b(t),
                )
            )

    def grad_pair(i):
        cut = (slice(None), spans[i])
        gb_chips[(c1, *cut)] = gb_low[(*cut, pl.ds(chip_rows, slice_rows))]
        for d in range(1, z.p1):
            arrive(gb_chips.at[(lax.rem(c1 + z.p1 - d, z.p1), *cut)], sem_g.at[1, i, d])
        gb_sum[cut] = add_up([gb_chips[(p, *cut)].astype(f32) for p in range(z.p1)])
        if z.p2 > 1:
            gb_far[(c2, *cut)] = gb_sum[cut].astype(bf)
            for d in range(1, z.p2):
                t = lax.rem(c2 + d, z.p2)
                go(
                    remote(
                        gb_far.at[(c2, *cut)],
                        gb_far.at[(c2, *cut)],
                        sem_g.at[0, i, 24 + d],
                        sem_g.at[1, i, 24 + d],
                        peer_c(t),
                    )
                )
            for d in range(1, z.p2):
                arrive(gb_far.at[(lax.rem(c2 + z.p2 - d, z.p2), *cut)], sem_g.at[1, i, 24 + d])
            gb_sum[cut] = add_up([gb_far[(p, *cut)].astype(f32) for p in range(z.p2)])
        go(remote(gb_sum.at[o, spans[i]], gb_pair.at[spans[i]], sem_g.at[0, i, 8], sem_g.at[1, i, 8], across))

    def grad_back(i):
        arrive(gb_pair.at[spans[i]], sem_g.at[1, i, 8])
        mine = gb_sum[s, spans[i]]
        other = gb_pair[spans[i]]
        own = pl.multiple_of(core_rows + chip_rows, slice_rows)
        gb_fin[spans[i], pl.ds(own, slice_rows)] = (mine + other).astype(bf)
        at = gb_fin.at[spans[i], pl.ds(own, slice_rows)]
        for d in range(1, z.p1):
            t = lax.rem(c1 + d, z.p1)
            go(remote(at, at, sem_g.at[0, i, 8 + d], sem_g.at[1, i, 8 + d], peer_b(t)))

    def grad_last(i):
        for d in range(1, z.p1):
            t = lax.rem(c1 + z.p1 - d, z.p1)
            at = pl.multiple_of(core_rows + slice_of(t), slice_rows)
            arrive(gb_fin.at[spans[i], pl.ds(at, slice_rows)], sem_g.at[1, i, 8 + d])
        at = gb_fin.at[spans[i], pl.ds(core_rows, H)]
        go(remote(at, at, sem_g.at[0, i, 16], sem_g.at[1, i, 16], neighbour))

    def grad_done(i):
        arrive(gb_fin.at[spans[i], pl.ds(other_rows, H)], sem_g.at[1, i, 16])

    grad_core(0)

    def grad_body(late):
        def body(a, _):
            gs = back(flat(conv[a]), flat(summed[a]) - mean1, *in_corr)
            gs = keep(gs, late).astype(bf)
            conv[a] = tiles(gs.astype(f32))
            return 0

        return body

    def grad_chunk(j):
        lax.fori_loop(*z.chunks[j], grad_body(z.chunks[j][0] >= cut), 0)

    def input_chunk(j):
        a0, a1 = z.chunks[j]
        n = a1 - a0
        span = pl.ds(a0, n)
        summed[span, 0] = jnp.zeros((n, RW, C), f32)
        for v in range(J - 1, 0, -1):
            summed[span, v] = conv[span, v] * edge[1, v : v + 1] + summed[span, kin[0, v]]
        for w in range(J):
            mixed[0, pl.ds(0, n), w] = summed[span, kin[1, w]].astype(bf)
            mixed[1, pl.ds(0, n), w] = (conv[span, par[w]] * edge[2, w : w + 1]).astype(bf)

        def out(i, _):
            t = whole(iz, a0 + i).astype(f32)
            own = (conv[a0 + i] * edge[0][:, None, :]).astype(bf)
            for k, rows in enumerate((own, mixed[0, i], mixed[1, i])):
                t = t + lax.dot_general(
                    flat(rows), ws[:, k * C : (k + 1) * C], last, preferred_element_type=f32
                )
            put(iz, a0 + i, t.astype(bf))
            return 0

        lax.fori_loop(0, n, out, 0)

        ship(iz, ing_own, ing_rcv, sem_i, j)

    def edge_rows_f(v):
        return jnp.concatenate(
            [fx[0, :, pl.ds(v, 1)].reshape(L * RW, H), fx[1, :, pl.ds(v, 1)].reshape(L * RW, H)], axis=1
        )

    def edge_rows_g(v):
        return conv[:, pl.ds(v, 1)].reshape(L * RW, C).astype(bf)

    gb[:, TAPS:] = jnp.zeros((2, 3, C, H), f32)

    dots[...] = jnp.zeros_like(dots)
    unroll = 5 if J % 5 == 0 else 1

    def edge_body(i, _):
        for u in range(unroll):
            v = i * unroll + u
            pv = par[v]
            f_v, f_p, g_v, g_p = edge_rows_f(v), edge_rows_f(pv), edge_rows_g(v), edge_rows_g(pv)
            both = lax.dot_general(
                f_v, jnp.concatenate([g_v, g_p], axis=1), first, preferred_element_type=f32
            )
            up_prod = lax.dot_general(f_p, g_v, first, preferred_element_type=f32)
            for k, prod in enumerate((both[:, :C], up_prod, both[:, C:])):
                part = prod * edge[k, pl.ds(v, 1)]
                for h in range(2):
                    j = 2 * k + h
                    gb[j // 3, TAPS + j % 3] += part[:, h * H : (h + 1) * H]
                dots[k, pl.ds(v, 1)] = row_sum(prod * ws[:, k * C : (k + 1) * C].astype(f32))
        return 0

    def edges():
        lax.fori_loop(0, J // unroll, edge_body, 0)
        ones = jnp.ones((8, C), f32)
        n = dots.shape[1]
        spread_out = jnp.where(
            lax.broadcasted_iota(jnp.int32, (n, C), 0) == lax.broadcasted_iota(jnp.int32, (n, C), 1), 1.0, 0.0
        )
        rows = []
        for k in range(3):
            t = lax.dot_general(ones, dots[k], last, precision=exact_mode, preferred_element_type=f32)
            t = jnp.dot(t, spread_out, precision=exact_mode, preferred_element_type=f32)
            rows.append(t[0:1])
        return jnp.concatenate(rows + [jnp.zeros((5, C), f32)], axis=0)

    grad_chunk(0)
    input_chunk(0)
    grad_chips(0)
    with jax.named_scope("tap_grad_late"):
        lax.fori_loop(EARLY, TAPS, tap_body, 0)
    for j in range(1, n_chunks):
        grad_chunk(j)
        if j < n_chunks - 1:
            input_chunk(j)
    with jax.named_scope("edges"):
        dvec = edges()
    grad_core(1)
    all_start(4, dvec)
    grad_pair(0)
    input_chunk(n_chunks - 1)
    with jax.named_scope("grad_reduce"):
        grad_chips(1)
        grad_back(0)
        all_more(4, add_up)
        grad_pair(1)
        grad_last(0)
        grad_back(1)
        dvec = all_end(4, add_up)
        grad_last(1)
    for k in range(3):
        per_edge = dvec[k : k + 1, :J]
        if k == 1:
            per_edge = lax.dot_general(
                eye, jnp.broadcast_to(per_edge, (J, J)), last, precision=exact_mode, preferred_element_type=f32
            )
        ig_out[k] = adj[k] * per_edge
    for i, row in enumerate((sum1[1:2], sum1[0:1], sum2[1:2], sum2[0:1])):
        sums_out[i : i + 1] = jnp.where(s == 0, row[:, :H], row[:, H:])
    sums_out[4:8] = jnp.zeros((4, H), f32)
    with jax.named_scope("grad_reduce_end"):
        grad_done(0)
        grad_done(1)
        last_out = [pltpu.make_async_copy(gb_fin.at[pl.ds(0, TAPS)], tg_out, sem_l.at[2, 2])]
        for j in range(3):
            last_out.append(
                pltpu.make_async_copy(gb_fin.at[TAPS + j], sg_out.at[:, pl.ds(j * H, H)], sem_l.at[2, 3 + j])
            )
        for cp in last_out:
            cp.start()

    with jax.named_scope("last_waits"):
        for j in range(n_chunks):
            a0, a1 = z.chunks[j]
            at = pl.ds(a0, a1 - a0)
            arrive(act_rcv.at[at], sem_a.at[1, j])
            arrive(ing_rcv.at[at], sem_i.at[1, j])
        for cp in outs + last_out:
            cp.wait()
        for cp in sends:
            cp.wait_send()


def finish(
    z,
    act_own,
    act_rcv,
    ing_own,
    ing_rcv,
    tg_in,
    sg_in,
    sums_in,
    ig_in,
    act_out,
    ing_out,
    tg_out,
    sg_out,
    r0,
    r1,
    r2,
    r3,
    ig_out,
    low_act,
    low_ing,
    full,
    tg,
    sg,
    tg_wide,
    sg_wide,
    sem_in,
    sem_out,
):
    J, L = z.joints, z.blk
    s = lax.axis_index("sub")
    jobs = [(act_own, act_out, s), (act_rcv, act_out, 1 - s), (ing_own, ing_out, s), (ing_rcv, ing_out, 1 - s)]
    ins = []
    for i, (src, _, _) in enumerate(jobs):
        cp = pltpu.make_async_copy(src, (low_act if i < 2 else low_ing).at[i % 2], sem_in.at[i])
        cp.start()
        ins.append(cp)
    grads = []
    for i, (src, mid, wide, dst) in enumerate(((tg_in, tg, tg_wide, tg_out), (sg_in, sg, sg_wide, sg_out))):
        cp = pltpu.make_async_copy(src, mid, sem_in.at[4 + i])
        cp.start()
        grads.append((cp, mid, wide, pltpu.make_async_copy(wide, dst, sem_in.at[6 + i])))
    for i, r in enumerate((r0, r1, r2, r3)):
        r[...] = sums_in[i : i + 1]
    ig_out[...] = ig_in[...]
    cut = L - z.pad
    fr = full.reshape(4, L, J, RW, z.half)
    lows = (low_act.reshape(2, L, J, RW, z.half), low_ing)

    def pieces(i, dst, w):
        for part, (a0, a1) in enumerate(z.locals):
            for b in range(NB):
                cp = pltpu.make_async_copy(
                    full.at[i, pl.ds(a0, a1 - a0), :, b],
                    dst.at[pl.ds(w * z.win + b * L + a0, a1 - a0)],
                    sem_out.at[i, part, b],
                )
                yield part == 1 and b == NB - 1, cp

    for i, (_, dst, w) in enumerate(jobs):
        ins[i].wait()

        def body(a, _, i=i):
            fr[i, a] = lows[i // 2][i % 2, a].astype(jnp.float32)
            return 0

        lax.fori_loop(0, L, body, 0)
        for beyond, cp in pieces(i, dst, w):
            if beyond:
                pl.when(w == 0)(cp.start)
            else:
                cp.start()
    for cp_in, mid, wide, cp_out in grads:
        cp_in.wait()
        wide[...] = mid[...].astype(jnp.float32)
        cp_out.start()
    for _, _, _, cp_out in grads:
        cp_out.wait()
    for i, (_, dst, w) in enumerate(jobs):
        for beyond, cp in pieces(i, dst, w):
            if beyond:
                pl.when(w == 0)(cp.wait)
            else:
                cp.wait()


def block(
    n_dp, features, presence, parents, w_spatial, importance, gain_one, shift_one, w_temporal, gain_two, shift_two, cotangent
):
    _, _, frames, joints, half = features.shape
    z = Sizes(n_dp, frames, joints, half)
    f32, bf = jnp.float32, jnp.bfloat16
    C, H, L, R, J = z.chan, z.half, z.blk, z.rows, z.joints

    def natural(x):
        return x.transpose(0, 2, 3, 1, 4).reshape(frames, joints, 2, half)

    any_, vmem, smem = (pl.BlockSpec(memory_space=m) for m in (pl.ANY, pltpu.VMEM, pltpu.SMEM))
    landing = (L, J, NB, 2, H)
    blocked = (L, J, RW, H)
    sds = jax.ShapeDtypeStruct
    VM, DMA = pltpu.VMEM, pltpu.SemaphoreType.DMA
    nch = len(z.chunks)
    packed = -(-HALO * 2 * J // RW) * RW
    outs = pl.pallas_call(
        functools.partial(mega, z),
        name="graph_conv_block",
        out_shape=[sds(landing, bf)] * 2
        + [sds(blocked, bf)] * 2
        + [sds((TAPS, C, H), bf), sds((C, 3 * H), bf), sds((8, H), f32), sds((3, J, J), f32)],
        in_specs=[any_] * 4 + [vmem, smem, smem] + [vmem] * 4,
        out_specs=[any_] * 6 + [vmem] * 2,
        scratch_shapes=[
            VM((2,) + landing, bf),
            VM((2,) + landing, bf),
            VM((2,) + blocked, bf),
            VM((TAPS, C, C), bf),
            VM((C, 3 * C), bf),
            VM((L, J, RW, C), f32),
            VM((L + 2 * HALO, J, RW, C), bf),
            VM((L, J, RW, C), f32),
            VM((L + 2 * HALO, J, RW, C), bf),
            VM((2,) + blocked, bf),
            VM((2, TAPS + 3, C, H), f32),
            VM((2, TAPS + 3, H, H), f32),
            VM((2, TAPS + 3, H, H), bf),
            VM((z.p1, 2, TAPS + 3, H // z.p1, H), bf),
            VM((z.p2, 2, TAPS + 3, H // z.p1, H), bf),
            VM((2, TAPS + 3, H // z.p1, H), f32),
            VM((TAPS + 3, H // z.p1, H), f32),
            VM((TAPS + 3, C, H), bf),
            VM((2, max(a1 - a0 for a0, a1 in z.chunks), J, RW, C), bf),
            VM((3, -(-J // 8) * 8, C), f32),
            VM((2, 8, H), f32),
            VM((3, J, J), f32),
            VM((3, J, C), f32),
            pltpu.SMEM((2, J), jnp.int32),
            VM((3, packed, C), bf),
            VM((1, packed, C), bf),
            VM((3, packed, C), bf),
            VM((5, z.near, 8, C), f32),
            VM((5, z.p2, 8, C), f32),
            VM((5, 2, 8, C), f32),
            DMA((3, 2 * NB)),
            DMA((2, nch, NB)),
            DMA((2, nch, NB)),
            DMA((3, nch)),
            DMA((3, nch)),
            DMA((2, 40)),
            DMA((2, 2, 2)),
            DMA((2, 2, 32)),
            DMA((2, 5, z.near)),
            DMA((2, 5, z.p2)),
            DMA((2, 5)),
        ],
        compiler_params=pltpu.CompilerParams(
            collective_id=0, has_side_effects=True, vmem_limit_bytes=63 * 2**20
        ),
    )(
        natural(features),
        natural(cotangent),
        w_temporal,
        w_spatial,
        importance,
        parents,
        presence,
        *(v.reshape(1, H) for v in (gain_one, shift_one, gain_two, shift_two)),
    )
    act, ing, tg, sg, r0, r1, r2, r3, ig = pl.pallas_call(
        functools.partial(finish, z),
        name="natural_order",
        out_shape=[sds((frames, joints, 2, H), f32)] * 2
        + [sds((TAPS, C, H), f32), sds((C, 3 * H), f32)]
        + [sds((1, H), f32)] * 4
        + [sds((3, J, J), f32)],
        in_specs=[any_] * 6 + [vmem] * 2,
        out_specs=[any_] * 4 + [vmem] * 5,
        scratch_shapes=[
            VM((2,) + landing, bf),
            VM((2,) + blocked, bf),
            VM((4,) + landing, f32),
            VM((TAPS, C, H), bf),
            VM((C, 3 * H), bf),
            VM((TAPS, C, H), f32),
            VM((C, 3 * H), f32),
            DMA((8,)),
            DMA((4, 2, NB)),
        ],
        compiler_params=pltpu.CompilerParams(vmem_limit_bytes=60 * 2**20),
    )(*outs)

    def back(x):
        return x.reshape(1, frames, joints, 2, half).transpose(0, 3, 1, 2, 4)

    return (
        back(act),
        back(ing),
        sg,
        ig,
        *(r.reshape(H) for r in (r0, r1)),
        tg,
        *(r.reshape(H) for r in (r2, r3)),
    )


def solution(mesh):
    in_specs = (
        P("dp", None, None, None, "sub"),
        P("dp", None),
        P(),
        P(None, "sub"),
        P(),
        P("sub"),
        P("sub"),
        P(None, None, "sub"),
        P("sub"),
        P("sub"),
        P("dp", None, None, None, "sub"),
    )
    out_specs = (
        P("dp", None, None, None, "sub"),
        P("dp", None, None, None, "sub"),
        P(None, "sub"),
        P(),
        P("sub"),
        P("sub"),
        P(None, None, "sub"),
        P("sub"),
        P("sub"),
    )
    return jax.shard_map(
        functools.partial(block, mesh.shape["dp"]), mesh=mesh, in_specs=in_specs, out_specs=out_specs, check_vma=False
    )
```

```python
import functools

import jax
import jax.numpy as jnp
from jax import lax
from jax.experimental import pallas as pl
from jax.experimental.pallas import tpu as pltpu
from jax.sharding import PartitionSpec as P

norm_eps = 1e-05
exact_mode = lax.Precision.HIGHEST
MESH = pl.DeviceIdType.MESH
TAPS = 9
EARLY = 6
LAST_STEPS = ('0', 'chips0', '1', '2', 'late', 'edges', 'pair0', '3', 'chips1', 'back0', '4', 'pair1', 'last0', 'back1', 'last1')
HALO = TAPS // 2
NB = 8
RW = 2 * NB
G = 4
tanh_scale = 0.7978845608028654
tanh_cubic = 0.044715


def gelu(x):
    t = jnp.tanh(x * (tanh_scale + (tanh_scale * tanh_cubic) * (x * x)))
    return x * (0.5 + 0.5 * t)


def gelu_both(x):
    x2 = x * x
    h = 0.5 + 0.5 * jnp.tanh(x * (tanh_scale + (tanh_scale * tanh_cubic) * x2))
    rise = x * (2.0 * tanh_scale + (6.0 * tanh_scale * tanh_cubic) * x2)
    return x * h, h + h * ((1.0 - h) * rise)


class Sizes:
    def __init__(self, n_dp, frames, joints, half):
        self.n_dp, self.frames, self.joints, self.half = n_dp, frames, joints, half
        self.chan = 2 * half
        self.blk = -(-frames // (2 * NB))
        self.win = self.blk * NB
        self.pad = 2 * self.win - frames
        self.rows = joints * RW
        self.total = self.blk * self.rows
        self.chips = n_dp // 2
        self.p1 = 8
        self.p2 = self.chips // self.p1
        self.near = 2 * self.p1
        cut = self.blk - self.pad
        step = -(-cut // 3)
        self.chunks = [(a, min(a + step, cut)) for a in range(0, cut, step)]
        if self.pad:
            self.chunks.append((cut, self.blk))
        lead = min(2, step)
        self.tail = [(0, lead), (lead, step)] + self.chunks[1:]
        self.groups = -(-frames // 8)
        per_slab = 8 * -(-self.groups // 6)
        self.slabs = [(f, min(per_slab, frames - f)) for f in range(0, frames, per_slab)]
        self.locals = [(0, cut)] + ([(cut, self.blk)] if self.pad else [])


def mega(
    z,
    feat,
    cot,
    wt_in,
    ws_in,
    imp,
    par,
    pres,
    g1,
    b1,
    g2,
    b2,
    act_nat,
    ing_nat,
    tg_out,
    sg_out,
    sums_out,
    ig_out,
    xh,
    ct,
    fx,
    wt,
    ws,
    summed,
    acth,
    conv,
    gch,
    iz,
    gb,
    gb_core,
    gb_low,
    gb_chips,
    gb_far,
    gb_sum,
    gb_pair,
    gb_fin,
    mixed,
    dots,
    prm,
    adj,
    edge,
    kin,
    halo_s,
    halo_m,
    halo_r,
    arA,
    arC,
    arD,
    sem_l,
    sem_f,
    sem_c,
    sem_a,
    sem_i,
    sem_w,
    sem_h,
    sem_g,
    semA,
    semC,
    semD,
):
    f32, bf = jnp.float32, jnp.bfloat16
    J, C, H, L, R = z.joints, z.chan, z.half, z.blk, z.rows
    s = lax.axis_index("sub")
    dp = lax.axis_index("dp")
    o = 1 - s
    core = lax.rem(dp, 2)
    chip = lax.div(dp, 2)
    c1 = lax.rem(chip, z.p1)
    c2 = lax.div(chip, z.p1)
    partner = (dp, o)

    d1 = lax.rem(dp, z.near)
    flip = dp + 4 - 8 * lax.rem(lax.div(dp, 4), 2)
    across = (flip, o)
    beside = (flip, s)

    def peer_b(t):
        return (2 * (c2 * z.p1 + t) + core, s)

    def peer_c(t):
        return (2 * (t * z.p1 + c1) + core, s)

    def peer_0(t):
        return (c2 * z.near + t, s)

    def other_chip(t):
        return t + 2 - 4 * lax.rem(lax.div(t, 2), 2)

    def owned(t):
        return t + s * (other_chip(t) - t)

    def remote(src, dst, ssem, rsem, dev):
        return pltpu.make_async_remote_copy(
            src_ref=src,
            dst_ref=dst,
            send_sem=ssem,
            recv_sem=rsem,
            device_id=dev,
            device_id_type=MESH,
        )

    bar = pltpu.get_barrier_semaphore()
    greeted = [partner, across]
    greeted += [peer_0(lax.rem(d1 + d, z.near)) for d in range(1, z.near)]
    greeted += [peer_c(lax.rem(c2 + d, z.p2)) for d in range(1, z.p2)]
    for dev in greeted:
        pl.semaphore_signal(bar, inc=1, device_id=dev, device_id_type=MESH)

    def frames_at(w, b, a0, a1):
        return pl.ds(w * z.win + (b * L + a0), a1 - a0)

    def beyond(b, a0):
        return z.pad > 0 and b == NB - 1 and a0 >= L - z.pad

    def when(cond, do):
        if cond is None:
            do()
        else:
            pl.when(cond)(do)

    local = []
    for which, (src, dst) in enumerate(((feat, xh), (cot, ct))):
        for i, (a0, a1) in enumerate(z.locals):
            for b in range(NB):
                cp = pltpu.make_async_copy(
                    src.at[frames_at(s, b, a0, a1)],
                    dst.at[s, pl.ds(a0, a1 - a0), :, b],
                    sem_l.at[which, i * NB + b],
                )
                cond = s == 0 if beyond(b, a0) else None
                when(cond, cp.start)
                local.append((cond, cp))
    if z.pad:

        @pl.when(s == 1)
        def _():
            for ref in (xh, ct):
                ref[:, L - z.pad :, :, NB - 1] = jnp.zeros((2, z.pad, J, 2, H), bf)

    lw = [
        pltpu.make_async_copy(ws_in, ws.at[:, pl.ds(pl.multiple_of(s * 3 * H, H), 3 * H)], sem_l.at[2, 0]),
        pltpu.make_async_copy(wt_in, wt.at[:, :, pl.ds(pl.multiple_of(s * H, H), H)], sem_l.at[2, 1]),
    ]
    for cp in lw:
        cp.start()
    for i, v in enumerate((g1, b1, g2, b2)):
        prm[s, i : i + 1] = v[...]

    with jax.named_scope("barrier"):
        pl.semaphore_wait(bar, len(greeted))

    slice_rows = H // z.p1
    row0 = pl.multiple_of(core * H + c1 * slice_rows, slice_rows)

    def ws_at(half, r0, n):
        return ws.at[pl.ds(r0, n), pl.ds(pl.multiple_of(half * 3 * H, H), 3 * H)]

    def wt_at(half, r0, n):
        return wt.at[:, pl.ds(r0, n), pl.ds(pl.multiple_of(half * H, H), H)]

    sends = []

    def go(cp, cond=None):
        when(cond, cp.start)
        sends.append((cond, cp))

    def arrive(dst, rsem):
        remote(dst, dst, rsem, rsem, partner).wait_recv()

    go(remote(prm.at[s], prm.at[s], sem_w.at[0, 0], sem_w.at[1, 0], partner))
    go(remote(ws_in.at[pl.ds(row0, slice_rows)], ws_at(s, row0, slice_rows), sem_w.at[0, 1], sem_w.at[1, 1], partner))
    go(remote(wt_in.at[:, pl.ds(row0, slice_rows)], wt_at(s, row0, slice_rows), sem_w.at[0, 2], sem_w.at[1, 2], partner))

    def send_rows(src, dst, sem, j):
        a0, a1 = z.chunks[j]
        for b in range(NB):
            go(
                remote(
                    src.at[frames_at(o, b, a0, a1)],
                    dst.at[s, pl.ds(a0, a1 - a0), :, b],
                    sem.at[0, j, b],
                    sem.at[1, j, b],
                    partner,
                ),
                o == 0 if beyond(b, a0) else None,
            )

    def take_rows(dst, sem, j):
        a0, a1 = z.chunks[j]
        for b in range(NB):
            at = dst.at[o, pl.ds(a0, a1 - a0), :, b]
            when(s == 0 if beyond(b, a0) else None, lambda at=at, b=b: arrive(at, sem.at[1, j, b]))

    n_chunks = len(z.chunks)
    for j in range(n_chunks):
        send_rows(feat, xh, sem_f, j)
    order = [n_chunks - 1] + list(range(n_chunks - 1))
    for j in order:
        send_rows(cot, ct, sem_c, j)

    ri = lax.broadcasted_iota(jnp.int32, (J, J), 0)
    ci = lax.broadcasted_iota(jnp.int32, (J, J), 1)
    eye = jnp.where(ri == ci, 1.0, 0.0).astype(f32)
    up = jnp.zeros((J, J), f32)
    down = jnp.zeros((J, J), f32)
    for v in range(1, J):
        pv = par[v]
        up = jnp.where((ri == v) & (ci == pv), 1.0, up)
        down = jnp.where((ci == v) & (ri == pv), 1.0, down)
    degree = jnp.sum(eye + up + down, axis=0, keepdims=True)
    adjacent = [eye / degree, up / degree, down / degree]
    mixing = [adjacent[k] * imp[k] for k in range(3)]
    for k in range(3):
        adj[k] = adjacent[k]
    last = (((1,), (1,)), ((), ()))
    first = (((0,), (0,)), ((), ()))
    wide = jnp.ones((J, C), f32)
    edge[0] = jnp.dot(mixing[0], wide, precision=exact_mode, preferred_element_type=f32)
    edge[1] = jnp.dot(mixing[1], wide, precision=exact_mode, preferred_element_type=f32)
    edge[2] = lax.dot_general(mixing[2], wide, first, precision=exact_mode, preferred_element_type=f32)

    def kin_body(v, _):
        pv = par[v]
        sibling = jnp.int32(0)
        child = jnp.int32(0)
        for w in range(J - 1, 0, -1):
            pw_ = par[w]
            sibling = jnp.where((pw_ == pv) & (w > v), w, sibling)
            child = jnp.where(pw_ == v, w, child)
        kin[0, v] = sibling
        kin[1, v] = child
        return 0

    lax.fori_loop(0, J, kin_body, 0)

    for i, at in ((0, ws_at), (1, wt_at)):
        arrive(at(o, row0, slice_rows), sem_w.at[1, 1 + i])
        for d in range(1, z.p1):
            t = lax.rem(c1 + d, z.p1)
            go(
                remote(
                    at(o, row0, slice_rows),
                    at(o, row0, slice_rows),
                    sem_w.at[0, 4 + i * 16 + d],
                    sem_w.at[1, 4 + i * 16 + d],
                    peer_b(t),
                )
            )
    for i, at in ((0, ws_at), (1, wt_at)):
        for d in range(1, z.p1):
            t = lax.rem(c1 + z.p1 - d, z.p1)
            arrive(
                at(o, pl.multiple_of(core * H + t * slice_rows, slice_rows), slice_rows),
                sem_w.at[1, 4 + i * 16 + d],
            )
        mine = pl.multiple_of(core * H, H)
        go(remote(at(o, mine, H), at(o, mine, H), sem_w.at[0, 36 + i], sem_w.at[1, 36 + i], (2 * chip + 1 - core, s)))
    theirs = pl.multiple_of((1 - core) * H, H)
    arrive(ws_at(o, theirs, H), sem_w.at[1, 36])
    for cp in lw:
        cp.wait()
    arrive(prm.at[o], sem_w.at[1, 0])
    p0 = pres[0, 0].astype(f32)
    p1 = pres[0, 1].astype(f32)
    ri16 = lax.broadcasted_iota(jnp.int32, (RW, C), 0)
    pw = jnp.where((ri16 & 1) == 0, p0, p1).astype(f32)
    tail = jnp.where(ri16 >= RW - 2, 1.0, 0.0).astype(f32)
    side = s.astype(f32)

    real = 1.0 - tail * side
    cut = L - z.pad

    def tiles(x):
        return x.reshape(-1, RW, C)

    def flat(x):
        return x.reshape(R, C)

    def keep(x, late):
        return (tiles(x) * real[None]).reshape(x.shape) if late else x

    def down_rows(x):
        return jnp.sum(tiles(x), axis=0)

    def each(body, carry):
        carry = lax.fori_loop(0, cut, body(False), carry)
        return lax.fori_loop(cut, L, body(True), carry) if z.pad else carry

    def row_sum(x):
        return jnp.sum(x, axis=0, keepdims=True)

    def param(i):
        return jnp.concatenate([prm[0, i : i + 1], prm[1, i : i + 1]], axis=1)

    def whole(ref, a):
        return jnp.concatenate([ref[0, a].reshape(R, H), ref[1, a].reshape(R, H)], axis=1)

    def put(ref, a, value):
        for h in range(2):
            ref[h, a] = value[:, h * H : (h + 1) * H].reshape(J, RW, H)

    def land(ref, a, value):
        for h in range(2):
            ref[h, a] = value[:, h * H : (h + 1) * H].reshape(J, NB, 2, H)

    def spread(buf, sem, r, q, n, peer, val):
        buf[r, q] = val
        for d in range(1, n):
            go(remote(buf.at[r, q], buf.at[r, q], sem.at[0, r, d], sem.at[1, r, d], peer(lax.rem(q + d, n))))

    def gather(buf, sem, r, q, n):
        for d in range(1, n):
            arrive(buf.at[r, lax.rem(q + n - d, n)], sem.at[1, r, d])
        return [buf[r, i] for i in range(n)]

    def add_up(parts):
        t = parts[0]
        for x in parts[1:]:
            t = t + x
        return t

    def merge(parts):
        n = add_up([x[0:1] for x in parts])
        below = jnp.maximum(n, 1.0)
        mean = add_up([x[0:1] * x[1:2] for x in parts]) / below
        spread_up = add_up([x[2:3] + x[0:1] * (x[1:2] - mean) * (x[1:2] - mean) for x in parts])
        return jnp.concatenate([n, mean, spread_up, jnp.zeros((5, C), f32)], axis=0)

    def all_start(r, val):
        spread(arA, semA, r, d1, z.near, peer_0, val)

    def all_more(r, join):
        val = join(gather(arA, semA, r, d1, z.near))
        if z.p2 > 1:
            spread(arC, semC, r, c2, z.p2, peer_c, val)
            val = join(gather(arC, semC, r, c2, z.p2))
        arD[r, s] = val
        go(remote(arD.at[r, s], arD.at[r, s], semD.at[0, r], semD.at[1, r], across))

    def all_end(r, join):
        arrive(arD.at[r, o], semD.at[1, r])
        return join([arD[r, 0], arD[r, 1]])

    def moments(val_k, s1, s2):
        n = (p0 + p1) * (z.win - z.pad * side) * J
        below = jnp.maximum(n, 1.0)
        s1, s2 = row_sum(s1), row_sum(s2)
        return jnp.concatenate(
            [jnp.zeros((1, C), f32) + n, val_k + s1 / below, s2 - s1 * s1 / below, jnp.zeros((5, C), f32)], axis=0
        )

    def scaled(sums, rstd):
        return jnp.concatenate([sums[0:1], sums[1:2] * rstd], axis=0)

    zero16 = jnp.zeros((RW, C), f32)
    zero1 = jnp.zeros((1, C), f32)

    def spatial_chunk(a0, a1, carry):
        k_shift, s1, s2 = carry
        n = a1 - a0
        span, up_at, down_at, link = pl.ds(a0, n), pl.ds(0, n), pl.ds(n, n), pl.ds(2 * n, n)

        def body(i, _):
            f = whole(xh, a0 + i)
            put(fx, a0 + i, f)
            for k, (buf, at) in enumerate(((summed, a0 + i), (conv, i), (conv, n + i))):
                buf[at] = tiles(jnp.dot(f, ws[:, k * C : (k + 1) * C], preferred_element_type=f32))
            return 0

        lax.fori_loop(0, n, body, 0)
        conv[link, 0] = jnp.zeros((n, RW, C), f32)
        for v in range(J - 1, 0, -1):
            conv[link, v] = conv[down_at, v] * edge[2, v : v + 1] + conv[link, kin[0, v]]
        w = (pw * real if a0 >= cut else pw)[None]
        for v in range(J):
            t = summed[span, v] * edge[0, v : v + 1] + conv[link, kin[1, v]]
            if v:
                t = t + conv[up_at, par[v]] * edge[1, v : v + 1]
            summed[span, v] = t
            if a0 == 0 and v == 0:
                k_shift = row_sum(jnp.sum(t, axis=0)) * (1.0 / (n * RW))
            d = t - k_shift
            wd = d * w
            s1 = s1 + jnp.sum(wd, axis=0)
            s2 = s2 + jnp.sum(wd * d, axis=0)
        return k_shift, s1, s2

    carry = (zero1, zero16, zero16)
    n_local = len(z.locals) * NB
    for cond, cp in local[:n_local]:
        when(cond, cp.wait)
    for j, (a0, a1) in enumerate(z.chunks):
        with jax.named_scope("features_wait"):
            take_rows(xh, sem_f, j)
        with jax.named_scope("spatial"):
            carry = spatial_chunk(a0, a1, carry)

    per = 2 * J
    packed = -(-HALO * per // RW) * RW
    lane = lax.broadcasted_iota(jnp.int32, (packed, R), 1)
    line = lax.broadcasted_iota(jnp.int32, (packed, R), 0)
    off = (RW - 2) * o

    def pick(h):
        at = line - h * per
        hit = lane == lax.shift_right_arithmetic(at, 1) * RW + off + (at & 1)
        return jnp.where(hit & (at >= 0) & (at < per), 1.0, 0.0).astype(bf)

    edge_a = (L - HALO) * o

    def halo_rows(slot, ref):
        rows = jnp.zeros((packed, C), f32)
        for h in range(HALO):
            rows = rows + jnp.dot(pick(h), ref(edge_a + h).astype(bf), preferred_element_type=f32)
        halo_s[slot] = rows.astype(bf)

    def halo_send(r, n, src, dst, hop, dev):
        at = pl.ds(r, n)
        go(remote(src.at[at], dst.at[at], sem_h.at[0, r, hop], sem_h.at[1, r, hop], dev))

    def halo_wait(r, n, dst, hop):
        arrive(dst.at[pl.ds(r, n)], sem_h.at[1, r, hop])

    row_in = lax.broadcasted_iota(jnp.int32, (R, C), 0) & (RW - 1)
    fside = 1.0 - side

    def fill_halo(buf, fresh):
        for h in range(HALO):
            extra = lax.dot_general(pick(h), fresh, first, preferred_element_type=f32)
            lower = pltpu.roll(buf[L + h].reshape(R, C).astype(f32), 2, 0)
            lower = jnp.where(row_in < 2, extra * side, lower)
            buf[h] = tiles(lower.astype(bf))
            upper = pltpu.roll(buf[HALO + h].reshape(R, C).astype(f32), R - 2, 0)
            upper = jnp.where(row_in >= RW - 2, extra * fside, upper)
            buf[HALO + L + h] = tiles(upper.astype(bf))

    all_start(0, moments(*carry))
    halo_rows(0, lambda a: flat(summed[a]))
    halo_send(0, 1, halo_s, halo_m, 0, across)
    with jax.named_scope("st1"):
        all_more(0, merge)
        halo_wait(0, 1, halo_m, 0)
        halo_send(0, 1, halo_m, halo_r, 1, beside)
        st1 = all_end(0, merge)
    count = jnp.maximum(st1[0:1], 1.0)
    mean1 = st1[1:2]
    rstd1 = lax.rsqrt(st1[2:3] / count + norm_eps)
    gain1, shift1 = param(0), param(1)
    scale1 = rstd1 * gain1

    def act_body(late):
        def body(a, _):
            t = gelu((flat(summed[a]) - mean1) * scale1 + shift1)
            acth[a + HALO] = tiles(keep(t, late).astype(bf))
            return 0

        return body

    with jax.named_scope("act"):
        each(act_body, 0)

    def act_halo():
        halo_wait(0, 1, halo_r, 1)
        fill_halo(acth, gelu((halo_r[0].astype(f32) - mean1) * scale1 + shift1).astype(bf))

    arrive(wt_at(o, theirs, H), sem_w.at[1, 37])

    def conv_block(a0, late, carry):
        k_shift, s1, s2 = carry
        n = len(late)
        t = jnp.zeros((n * R, C), f32)
        for tap in range(TAPS):
            t = t + jnp.dot(acth[pl.ds(a0 + tap, n)].reshape(n * R, C), wt[tap], preferred_element_type=f32)
        conv[pl.ds(a0, n)] = t.reshape(n, J, RW, C)
        if a0 == HALO:
            k_shift = row_sum(t[:R]) * (1.0 / R)
        for i in range(n):
            w = pw * real if late[i] else pw
            d = tiles(t[i * R : (i + 1) * R] - k_shift)
            wd = d * w[None]
            s1 = s1 + jnp.sum(wd, axis=0)
            s2 = s2 + jnp.sum(wd * d, axis=0)
        return k_shift, s1, s2

    def blocks(fun, carry, ready):
        def run(a0, a1, carry):
            return fun(a0, [a >= cut for a in range(a0, a1)], carry)

        for a0 in range(HALO, L - HALO, G):
            carry = run(a0, min(a0 + G, L - HALO), carry)
        ready()
        carry = run(0, HALO, carry)
        return run(L - HALO, L, carry)

    with jax.named_scope("conv"):
        carry = blocks(conv_block, (zero1, zero16, zero16), act_halo)
    all_start(1, moments(*carry))
    with jax.named_scope("st2"):
        all_more(1, merge)
        st2 = all_end(1, merge)
    mean2 = st2[1:2]
    rstd2 = lax.rsqrt(st2[2:3] / count + norm_eps)
    gain2, shift2 = param(2), param(3)

    for cond, cp in local[n_local:]:
        when(cond, cp.wait)

    scale2 = rstd2 * gain2

    def out_body(late):
        def body(a, carry):
            sa, sb = carry
            centred = flat(conv[a]) - mean2
            level = centred * scale2 + (shift2 + whole(fx, a).astype(f32))
            value, slope = gelu_both(level)
            land(xh, a, value.astype(bf))
            gp = whole(ct, a).astype(f32) * slope
            conv[a] = tiles(gp)
            put(iz, a, centred.astype(bf))
            gm = keep(gp, late)
            return sa + down_rows(gm), sb + down_rows(gm * centred)

        return body

    carry = (zero16, zero16)
    outs = []

    def ship(buf, nat, sem, j, chunks):
        a0, a1 = chunks[j]
        for b in range(NB):
            src, at = (pl.ds(a0, a1 - a0), slice(None), b), frames_at(s, b, a0, a1)
            cond = s == 0 if beyond(b, a0) else None
            go(remote(buf.at[(o, *src)], nat.at[at], sem.at[0, j, b], sem.at[1, j, b], partner), cond)
            cp = pltpu.make_async_copy(buf.at[(s, *src)], nat.at[at], sem.at[2, j, b])
            when(cond, cp.start)
            outs.append((cond, cp))

    def shipped(nat, sem, j, chunks):
        a0, a1 = chunks[j]
        for b in range(NB):
            at = nat.at[frames_at(o, b, a0, a1)]
            when(o == 0 if beyond(b, a0) else None, lambda at=at, b=b: arrive(at, sem.at[1, j, b]))

    for i, j in enumerate(order):
        a0, a1 = z.chunks[j]
        with jax.named_scope("cotangent_wait"):
            take_rows(ct, sem_c, j)
        with jax.named_scope("level_two"):
            carry = lax.fori_loop(a0, a1, out_body(a0 >= cut), carry)
        ship(xh, act_nat, sem_a, j, z.chunks)

    pad6 = jnp.zeros((6, C), f32)
    all_start(2, jnp.concatenate([row_sum(carry[0]), row_sum(carry[1]), pad6], axis=0))
    with jax.named_scope("sum2"):
        all_more(2, add_up)
        sum2 = all_end(2, add_up)
    sum2 = scaled(sum2, rstd2)

    def corrections(scale, rstd, sums):
        shift = scale * sums[0:1] / count
        slope = scale * rstd * sums[1:2] / count
        return scale, (shift * pw)[None], (slope * pw)[None]

    def back(grad, centred, scale, shift, slope):
        return grad * scale - (tiles(centred) * slope + shift).reshape(grad.shape)

    out_corr = corrections(scale2, rstd2, sum2)

    def gconv_body(late):
        def body(a, _):
            gp = flat(conv[a])
            t = back(gp, whole(iz, a).astype(f32), *out_corr)
            gch[a + HALO] = tiles(keep(t, late).astype(bf))
            put(iz, a, gp.astype(bf))
            return 0

        return body

    with jax.named_scope("gconv"):
        lax.fori_loop(cut, L, gconv_body(True), 0)
        lax.fori_loop(L - HALO, cut, gconv_body(False), 0)
        lax.fori_loop(0, HALO, gconv_body(False), 0)
        halo_rows(1, lambda a: flat(gch[a + HALO]))
        halo_send(1, 1, halo_s, halo_m, 0, across)
        lax.fori_loop(HALO, min(cut, L - HALO), gconv_body(False), 0)
        halo_wait(1, 1, halo_m, 0)
        halo_send(1, 1, halo_m, halo_r, 1, beside)

    def conv_halo():
        halo_wait(1, 1, halo_r, 1)
        fill_halo(gch, halo_r[1])

    def gact_block(a0, late, carry):
        sa, sb = carry
        n = len(late)
        t = jnp.zeros((n * R, C), f32)
        for tap in range(TAPS):
            t = t + lax.dot_general(
                gch[pl.ds(a0 + TAPS - 1 - tap, n)].reshape(n * R, C), wt[tap], last, preferred_element_type=f32
            )
        for i in range(n):
            centred = flat(summed[a0 + i]) - mean1
            _, slope = gelu_both(centred * scale1 + shift1)
            gl = t[i * R : (i + 1) * R] * slope
            conv[a0 + i] = tiles(gl)
            gm = keep(gl, late[i])
            sa = sa + down_rows(gm)
            sb = sb + down_rows(gm * centred)
        return sa, sb

    with jax.named_scope("grad_act"):
        carry = blocks(gact_block, (zero16, zero16), conv_halo)
    all_start(3, jnp.concatenate([row_sum(carry[0]), row_sum(carry[1]), pad6], axis=0))

    def tap_body(tap, _):
        t = lax.dot_general(
            acth[pl.ds(tap, L)].reshape(z.total, C),
            gch[pl.ds(HALO, L)].reshape(z.total, C),
            first,
            preferred_element_type=f32,
        )
        gb[0, tap] = t[:, :H]
        gb[1, tap] = t[:, H:]
        return 0

    with jax.named_scope("tap_grad"):
        lax.fori_loop(0, EARLY // 2, tap_body, 0)
        all_more(3, add_up)
        lax.fori_loop(EARLY // 2, EARLY, tap_body, 0)
    with jax.named_scope("sum1_wait"):
        sum1 = all_end(3, add_up)
    sum1 = scaled(sum1, rstd1)
    in_corr = corrections(scale1, rstd1, sum1)

    neighbour = (2 * chip + 1 - core, s)
    core_rows = pl.multiple_of(core * H, H)
    other_rows = pl.multiple_of((1 - core) * H, H)
    def slice_of(t):
        return pl.multiple_of(owned(t) * slice_rows, slice_rows)

    chip_rows = slice_of(c1)
    spans = (pl.ds(0, EARLY), pl.ds(EARLY, TAPS + 3 - EARLY))

    def grad_core(i):
        cut = (slice(None), spans[i])
        go(
            remote(
                gb.at[(*cut, pl.ds(other_rows, H))], gb_core.at[cut], sem_g.at[0, i, 0], sem_g.at[1, i, 0], neighbour
            )
        )

    def grad_chips(i):
        cut = (slice(None), spans[i])
        arrive(gb_core.at[cut], sem_g.at[1, i, 0])
        total = gb[(*cut, pl.ds(core_rows, H))] + gb_core[cut]
        gb_low[cut] = total.astype(bf)
        for d in range(1, z.p1):
            t = lax.rem(c1 + d, z.p1)
            go(
                remote(
                    gb_low.at[(*cut, pl.ds(slice_of(t), slice_rows))],
                    gb_chips.at[(c1, *cut)],
                    sem_g.at[0, i, d],
                    sem_g.at[1, i, d],
                    peer_b(t),
                )
            )

    def grad_pair(i):
        cut = (slice(None), spans[i])
        gb_chips[(c1, *cut)] = gb_low[(*cut, pl.ds(chip_rows, slice_rows))]
        for d in range(1, z.p1):
            arrive(gb_chips.at[(lax.rem(c1 + z.p1 - d, z.p1), *cut)], sem_g.at[1, i, d])
        gb_sum[cut] = add_up([gb_chips[(p, *cut)].astype(f32) for p in range(z.p1)])
        if z.p2 > 1:
            gb_far[(c2, *cut)] = gb_sum[cut].astype(bf)
            for d in range(1, z.p2):
                t = lax.rem(c2 + d, z.p2)
                go(
                    remote(
                        gb_far.at[(c2, *cut)],
                        gb_far.at[(c2, *cut)],
                        sem_g.at[0, i, 24 + d],
                        sem_g.at[1, i, 24 + d],
                        peer_c(t),
                    )
                )
            for d in range(1, z.p2):
                arrive(gb_far.at[(lax.rem(c2 + z.p2 - d, z.p2), *cut)], sem_g.at[1, i, 24 + d])
            gb_sum[cut] = add_up([gb_far[(p, *cut)].astype(f32) for p in range(z.p2)])
        go(remote(gb_sum.at[o, spans[i]], gb_pair.at[spans[i]], sem_g.at[0, i, 8], sem_g.at[1, i, 8], across))

    def grad_back(i):
        arrive(gb_pair.at[spans[i]], sem_g.at[1, i, 8])
        mine = gb_sum[s, spans[i]]
        other = gb_pair[spans[i]]
        own = pl.multiple_of(core_rows + chip_rows, slice_rows)
        gb_fin[spans[i], pl.ds(own, slice_rows)] = (mine + other).astype(bf)
        at = gb_fin.at[spans[i], pl.ds(own, slice_rows)]
        for d in range(1, z.p1):
            t = lax.rem(c1 + d, z.p1)
            go(remote(at, at, sem_g.at[0, i, 8 + d], sem_g.at[1, i, 8 + d], peer_b(t)))

    def grad_last(i):
        for d in range(1, z.p1):
            t = lax.rem(c1 + z.p1 - d, z.p1)
            at = pl.multiple_of(core_rows + slice_of(t), slice_rows)
            arrive(gb_fin.at[spans[i], pl.ds(at, slice_rows)], sem_g.at[1, i, 8 + d])
        at = gb_fin.at[spans[i], pl.ds(core_rows, H)]
        go(remote(at, at, sem_g.at[0, i, 16], sem_g.at[1, i, 16], neighbour))

    def grad_done(i):
        arrive(gb_fin.at[spans[i], pl.ds(other_rows, H)], sem_g.at[1, i, 16])

    grad_core(0)

    def grad_body(late):
        def body(a, _):
            gs = back(flat(conv[a]), flat(summed[a]) - mean1, *in_corr)
            gs = keep(gs, late).astype(bf)
            conv[a] = tiles(gs.astype(f32))
            return 0

        return body

    def grad_chunk(j):
        lax.fori_loop(*z.tail[j], grad_body(z.tail[j][0] >= cut), 0)

    def input_chunk(j):
        a0, a1 = z.tail[j]
        n = a1 - a0
        span = pl.ds(a0, n)
        summed[span, 0] = jnp.zeros((n, RW, C), f32)
        for v in range(J - 1, 0, -1):
            summed[span, v] = conv[span, v] * edge[1, v : v + 1] + summed[span, kin[0, v]]
        for w in range(J):
            mixed[0, pl.ds(0, n), w] = summed[span, kin[1, w]].astype(bf)
            mixed[1, pl.ds(0, n), w] = (conv[span, par[w]] * edge[2, w : w + 1]).astype(bf)

        def out(i, _):
            t = whole(iz, a0 + i).astype(f32)
            own = (conv[a0 + i] * edge[0][:, None, :]).astype(bf)
            for k, rows in enumerate((own, mixed[0, i], mixed[1, i])):
                t = t + lax.dot_general(
                    flat(rows), ws[:, k * C : (k + 1) * C], last, preferred_element_type=f32
                )
            land(ct, a0 + i, t.astype(bf))
            return 0

        lax.fori_loop(0, n, out, 0)

        ship(ct, ing_nat, sem_i, j, z.tail)

    def edge_rows_f(v):
        return jnp.concatenate(
            [fx[0, :, pl.ds(v, 1)].reshape(L * RW, H), fx[1, :, pl.ds(v, 1)].reshape(L * RW, H)], axis=1
        )

    def edge_rows_g(v):
        return conv[:, pl.ds(v, 1)].reshape(L * RW, C).astype(bf)

    gb[:, TAPS:] = jnp.zeros((2, 3, C, H), f32)

    dots[...] = jnp.zeros_like(dots)
    unroll = 5 if J % 5 == 0 else 1

    def edge_body(i, _):
        for u in range(unroll):
            v = i * unroll + u
            pv = par[v]
            f_v, f_p, g_v, g_p = edge_rows_f(v), edge_rows_f(pv), edge_rows_g(v), edge_rows_g(pv)
            both = lax.dot_general(
                f_v, jnp.concatenate([g_v, g_p], axis=1), first, preferred_element_type=f32
            )
            up_prod = lax.dot_general(f_p, g_v, first, preferred_element_type=f32)
            for k, prod in enumerate((both[:, :C], up_prod, both[:, C:])):
                part = prod * edge[k, pl.ds(v, 1)]
                for h in range(2):
                    j = 2 * k + h
                    gb[j // 3, TAPS + j % 3] += part[:, h * H : (h + 1) * H]
                dots[k, pl.ds(v, 1)] = row_sum(prod * ws[:, k * C : (k + 1) * C].astype(f32))
        return 0

    def edges():
        lax.fori_loop(0, J // unroll, edge_body, 0)
        ones = jnp.ones((8, C), f32)
        n = dots.shape[1]
        spread_out = jnp.where(
            lax.broadcasted_iota(jnp.int32, (n, C), 0) == lax.broadcasted_iota(jnp.int32, (n, C), 1), 1.0, 0.0
        )
        rows = []
        for k in range(3):
            t = lax.dot_general(ones, dots[k], last, precision=exact_mode, preferred_element_type=f32)
            t = jnp.dot(t, spread_out, precision=exact_mode, preferred_element_type=f32)
            rows.append(t[0:1])
        return jnp.concatenate(rows + [jnp.zeros((5, C), f32)], axis=0)

    ready = set()
    steps = {
        "chips0": lambda: grad_chips(0),
        "late": lambda: lax.fori_loop(EARLY, TAPS, tap_body, 0),
        "pair0": lambda: grad_pair(0),
        "chips1": lambda: grad_chips(1),
        "back0": lambda: grad_back(0),
        "pair1": lambda: (all_more(4, add_up), grad_pair(1)),
        "last0": lambda: grad_last(0),
        "back1": lambda: grad_back(1),
        "last1": lambda: grad_last(1),
    }

    def sums_ready(chunks):
        for j in chunks:
            if j not in ready:
                ready.add(j)
                grad_chunk(j)

    for step in LAST_STEPS:
        with jax.named_scope("step_" + step):
            if step == "edges":
                sums_ready(range(len(z.tail)))
                all_start(4, edges())
                grad_core(1)
            elif step in steps:
                steps[step]()
            else:
                sums_ready([int(step)])
                input_chunk(int(step))
    dvec = all_end(4, add_up)
    for k in range(3):
        per_edge = dvec[k : k + 1, :J]
        if k == 1:
            per_edge = lax.dot_general(
                eye, jnp.broadcast_to(per_edge, (J, J)), last, precision=exact_mode, preferred_element_type=f32
            )
        ig_out[k] = adj[k] * per_edge
    for i, row in enumerate((sum1[1:2], sum1[0:1], sum2[1:2], sum2[0:1])):
        sums_out[i : i + 1] = jnp.where(s == 0, row[:, :H], row[:, H:])
    sums_out[4:8] = jnp.zeros((4, H), f32)
    with jax.named_scope("grad_reduce_end"):
        grad_done(0)
        grad_done(1)
        last_out = [pltpu.make_async_copy(gb_fin.at[pl.ds(0, TAPS)], tg_out, sem_l.at[2, 2])]
        for j in range(3):
            last_out.append(
                pltpu.make_async_copy(gb_fin.at[TAPS + j], sg_out.at[:, pl.ds(j * H, H)], sem_l.at[2, 3 + j])
            )
        for cp in last_out:
            cp.start()

    with jax.named_scope("last_waits"):
        for j in range(n_chunks):
            shipped(act_nat, sem_a, j, z.chunks)
        for j in range(len(z.tail)):
            shipped(ing_nat, sem_i, j, z.tail)
        for cond, cp in outs + [(None, cp) for cp in last_out]:
            when(cond, cp.wait)
        for cond, cp in sends:
            when(cond, cp.wait_send)


def finish(
    z,
    act_in,
    ing_in,
    tg_in,
    sg_in,
    sums_in,
    ig_in,
    act_out,
    ing_out,
    tg_out,
    sg_out,
    r0,
    r1,
    r2,
    r3,
    ig_out,
    low,
    full,
    tg,
    sg,
    tg_wide,
    sg_wide,
    sem_in,
    sem_out,
    sem_g,
):
    f32 = jnp.float32
    n = len(z.slabs)
    jobs = [(i, q, src, dst) for q in range(n) for i, (src, dst) in enumerate(((act_in, act_out), (ing_in, ing_out)))]
    ins, outs = [], []
    for i, q, src, dst in jobs:
        at = pl.ds(z.slabs[q][0], z.slabs[q][1])
        ins.append(pltpu.make_async_copy(src.at[at], low.at[i, at], sem_in.at[i, q]))
        outs.append(pltpu.make_async_copy(full.at[i, at], dst.at[at], sem_out.at[i, q]))
        ins[-1].start()
    grads = []
    for i, (src, mid, wide, dst) in enumerate(((tg_in, tg, tg_wide, tg_out), (sg_in, sg, sg_wide, sg_out))):
        cp = pltpu.make_async_copy(src, mid, sem_g.at[0, i])
        cp.start()
        grads.append((cp, mid, wide, pltpu.make_async_copy(wide, dst, sem_g.at[1, i])))
    for i, r in enumerate((r0, r1, r2, r3)):
        r[...] = sums_in[i : i + 1]
    ig_out[...] = ig_in[...]
    shape = (2, z.groups, z.rows // RW * NB // 8, RW, z.half)
    lows, fulls = low.reshape(shape), full.reshape(shape)
    for (i, q, _, _), cp_in, cp_out in zip(jobs, ins, outs):
        first, count = z.slabs[q]
        cp_in.wait()

        def body(g, _, i=i):
            fulls[i, g] = lows[i, g].astype(f32)
            return 0

        lax.fori_loop(first // 8, -(-(first + count) // 8), body, 0)
        cp_out.start()
    for cp_in, mid, wide, cp_out in grads:
        cp_in.wait()
        wide[...] = mid[...].astype(f32)
        cp_out.start()
    for cp_out in outs + [g[3] for g in grads]:
        cp_out.wait()


def block(
    n_dp, features, presence, parents, w_spatial, importance, gain_one, shift_one, w_temporal, gain_two, shift_two, cotangent
):
    _, _, frames, joints, half = features.shape
    z = Sizes(n_dp, frames, joints, half)
    f32, bf = jnp.float32, jnp.bfloat16
    C, H, L, R, J = z.chan, z.half, z.blk, z.rows, z.joints

    def natural(x):
        return x.transpose(0, 2, 3, 1, 4).reshape(frames, joints, 2, half)

    any_, vmem, smem = (pl.BlockSpec(memory_space=m) for m in (pl.ANY, pltpu.VMEM, pltpu.SMEM))
    landing = (L, J, NB, 2, H)
    blocked = (L, J, RW, H)
    sds = jax.ShapeDtypeStruct
    VM, DMA = pltpu.VMEM, pltpu.SemaphoreType.DMA
    nch = len(z.chunks)
    packed = -(-HALO * 2 * J // RW) * RW
    outs = pl.pallas_call(
        functools.partial(mega, z),
        name="graph_conv_block",
        out_shape=[sds((frames, joints, 2, H), bf)] * 2
        + [sds((TAPS, C, H), bf), sds((C, 3 * H), bf), sds((8, H), f32), sds((3, J, J), f32)],
        in_specs=[any_] * 4 + [vmem, smem, smem] + [vmem] * 4,
        out_specs=[any_] * 4 + [vmem] * 2,
        scratch_shapes=[
            VM((2,) + landing, bf),
            VM((2,) + landing, bf),
            VM((2,) + blocked, bf),
            VM((TAPS, C, C), bf),
            VM((C, 3 * C), bf),
            VM((L, J, RW, C), f32),
            VM((L + 2 * HALO, J, RW, C), bf),
            VM((L, J, RW, C), f32),
            VM((L + 2 * HALO, J, RW, C), bf),
            VM((2,) + blocked, bf),
            VM((2, TAPS + 3, C, H), f32),
            VM((2, TAPS + 3, H, H), f32),
            VM((2, TAPS + 3, H, H), bf),
            VM((z.p1, 2, TAPS + 3, H // z.p1, H), bf),
            VM((z.p2, 2, TAPS + 3, H // z.p1, H), bf),
            VM((2, TAPS + 3, H // z.p1, H), f32),
            VM((TAPS + 3, H // z.p1, H), f32),
            VM((TAPS + 3, C, H), bf),
            VM((2, max(a1 - a0 for a0, a1 in z.chunks), J, RW, C), bf),
            VM((3, -(-J // 8) * 8, C), f32),
            VM((2, 8, H), f32),
            VM((3, J, J), f32),
            VM((3, J, C), f32),
            pltpu.SMEM((2, J), jnp.int32),
            VM((2, packed, C), bf),
            VM((2, packed, C), bf),
            VM((2, packed, C), bf),
            VM((5, z.near, 8, C), f32),
            VM((5, z.p2, 8, C), f32),
            VM((5, 2, 8, C), f32),
            DMA((3, 2 * NB)),
            DMA((2, nch, NB)),
            DMA((2, nch, NB)),
            DMA((3, nch, NB)),
            DMA((3, len(z.tail), NB)),
            DMA((2, 40)),
            DMA((2, 2, 2)),
            DMA((2, 2, 32)),
            DMA((2, 5, z.near)),
            DMA((2, 5, z.p2)),
            DMA((2, 5)),
        ],
        compiler_params=pltpu.CompilerParams(
            collective_id=0, has_side_effects=True, vmem_limit_bytes=63 * 2**20
        ),
    )(
        natural(features),
        natural(cotangent),
        w_temporal,
        w_spatial,
        importance,
        parents,
        presence,
        *(v.reshape(1, H) for v in (gain_one, shift_one, gain_two, shift_two)),
    )
    act, ing, tg, sg, r0, r1, r2, r3, ig = pl.pallas_call(
        functools.partial(finish, z),
        name="natural_order",
        out_shape=[sds((frames, joints, 2, H), f32)] * 2
        + [sds((TAPS, C, H), f32), sds((C, 3 * H), f32)]
        + [sds((1, H), f32)] * 4
        + [sds((3, J, J), f32)],
        in_specs=[any_] * 4 + [vmem] * 2,
        out_specs=[any_] * 4 + [vmem] * 5,
        scratch_shapes=[
            VM((2, 8 * z.groups, joints, 2, H), bf),
            VM((2, 8 * z.groups, joints, 2, H), f32),
            VM((TAPS, C, H), bf),
            VM((C, 3 * H), bf),
            VM((TAPS, C, H), f32),
            VM((C, 3 * H), f32),
            DMA((2, len(z.slabs))),
            DMA((2, len(z.slabs))),
            DMA((2, 2)),
        ],
        compiler_params=pltpu.CompilerParams(vmem_limit_bytes=60 * 2**20),
    )(*outs)

    def back(x):
        return x.reshape(1, frames, joints, 2, half).transpose(0, 3, 1, 2, 4)

    return (
        back(act),
        back(ing),
        sg,
        ig,
        *(r.reshape(H) for r in (r0, r1)),
        tg,
        *(r.reshape(H) for r in (r2, r3)),
    )


def solution(mesh):
    in_specs = (
        P("dp", None, None, None, "sub"),
        P("dp", None),
        P(),
        P(None, "sub"),
        P(),
        P("sub"),
        P("sub"),
        P(None, None, "sub"),
        P("sub"),
        P("sub"),
        P("dp", None, None, None, "sub"),
    )
    out_specs = (
        P("dp", None, None, None, "sub"),
        P("dp", None, None, None, "sub"),
        P(None, "sub"),
        P(),
        P("sub"),
        P("sub"),
        P(None, None, "sub"),
        P("sub"),
        P("sub"),
    )
    return jax.shard_map(
        functools.partial(block, mesh.shape["dp"]), mesh=mesh, in_specs=in_specs, out_specs=out_specs, check_vma=False
    )
```

```python
import functools

import jax
import jax.numpy as jnp
from jax import lax
from jax.experimental import pallas as pl
from jax.experimental.pallas import tpu as pltpu
from jax.sharding import PartitionSpec as P

norm_eps = 1e-05
exact_mode = lax.Precision.HIGHEST
MESH = pl.DeviceIdType.MESH
TAPS = 9
EARLY = 6
LAST_STEPS = (
    "0", "chips0", "1", "2", "late", "pair0", "edges_a", "back0", "edges_b",
    "3", "chips1", "4", "last0", "pair1", "back1", "last1",
)
HALO = TAPS // 2
NB = 8
RW = 2 * NB
G = 4
tanh_scale = 0.7978845608028654
tanh_cubic = 0.044715


def gelu(x):
    t = jnp.tanh(x * (tanh_scale + (tanh_scale * tanh_cubic) * (x * x)))
    return x * (0.5 + 0.5 * t)


def gelu_both(x):
    x2 = x * x
    h = 0.5 + 0.5 * jnp.tanh(x * (tanh_scale + (tanh_scale * tanh_cubic) * x2))
    rise = x * (2.0 * tanh_scale + (6.0 * tanh_scale * tanh_cubic) * x2)
    return x * h, h + h * ((1.0 - h) * rise)


class Sizes:
    def __init__(self, n_dp, frames, joints, half):
        self.n_dp, self.frames, self.joints, self.half = n_dp, frames, joints, half
        self.chan = 2 * half
        self.blk = -(-frames // (2 * NB))
        self.win = self.blk * NB
        self.pad = 2 * self.win - frames
        self.rows = joints * RW
        self.total = self.blk * self.rows
        self.chips = n_dp // 2
        self.p1 = 8
        self.p2 = self.chips // self.p1
        self.near = 2 * self.p1
        cut = self.blk - self.pad
        step = -(-cut // 3)
        self.chunks = [(a, min(a + step, cut)) for a in range(0, cut, step)]
        lead = min(2, step)
        self.tail = [(0, lead), (lead, step)] + self.chunks[1:]
        if self.pad:
            self.tail.append((cut, self.blk))
            half = cut + (self.pad + 1) // 2
            self.chunks += [(cut, half)] + ([(half, self.blk)] if half < self.blk else [])
        self.groups = -(-frames // 8)
        per_slab = 8 * -(-self.groups // 6)
        self.slabs = [(f, min(per_slab, frames - f)) for f in range(0, frames, per_slab)]
        self.locals = [(0, cut)] + ([(cut, self.blk)] if self.pad else [])


def mega(
    z,
    feat,
    cot,
    wt_in,
    ws_in,
    imp,
    par,
    pres,
    g1,
    b1,
    g2,
    b2,
    act_nat,
    ing_nat,
    tg_out,
    sg_out,
    sums_out,
    ig_out,
    xh,
    ct,
    fx,
    wt,
    ws,
    summed,
    acth,
    conv,
    gch,
    iz,
    gb,
    gb_core,
    gb_low,
    gb_chips,
    gb_far,
    gb_sum,
    gb_pair,
    gb_fin,
    mixed,
    dots,
    prm,
    adj,
    edge,
    kin,
    halo_s,
    halo_m,
    halo_r,
    arA,
    arC,
    arD,
    sem_l,
    sem_f,
    sem_c,
    sem_a,
    sem_i,
    sem_w,
    sem_h,
    sem_g,
    semA,
    semC,
    semD,
):
    f32, bf = jnp.float32, jnp.bfloat16
    J, C, H, L, R = z.joints, z.chan, z.half, z.blk, z.rows
    s = lax.axis_index("sub")
    dp = lax.axis_index("dp")
    o = 1 - s
    core = lax.rem(dp, 2)
    chip = lax.div(dp, 2)
    c1 = lax.rem(chip, z.p1)
    c2 = lax.div(chip, z.p1)
    partner = (dp, o)

    d1 = lax.rem(dp, z.near)
    flip = dp + 4 - 8 * lax.rem(lax.div(dp, 4), 2)
    across = (flip, o)
    beside = (flip, s)

    def peer_b(t):
        return (2 * (c2 * z.p1 + t) + core, s)

    def peer_c(t):
        return (2 * (t * z.p1 + c1) + core, s)

    def peer_0(t):
        return (c2 * z.near + t, s)

    def other_chip(t):
        return t + 2 - 4 * lax.rem(lax.div(t, 2), 2)

    def owned(t):
        return t + s * (other_chip(t) - t)

    def remote(src, dst, ssem, rsem, dev):
        return pltpu.make_async_remote_copy(
            src_ref=src,
            dst_ref=dst,
            send_sem=ssem,
            recv_sem=rsem,
            device_id=dev,
            device_id_type=MESH,
        )

    bar = pltpu.get_barrier_semaphore()
    greeted = [partner, across]
    greeted += [peer_0(lax.rem(d1 + d, z.near)) for d in range(1, z.near)]
    greeted += [peer_c(lax.rem(c2 + d, z.p2)) for d in range(1, z.p2)]
    for dev in greeted:
        pl.semaphore_signal(bar, inc=1, device_id=dev, device_id_type=MESH)

    def frames_at(w, b, a0, a1):
        return pl.ds(w * z.win + (b * L + a0), a1 - a0)

    def beyond(b, a0):
        return z.pad > 0 and b == NB - 1 and a0 >= L - z.pad

    def when(cond, do):
        if cond is None:
            do()
        else:
            pl.when(cond)(do)

    local = []
    for which, (src, dst) in enumerate(((feat, xh), (cot, ct))):
        for i, (a0, a1) in enumerate(z.locals):
            for b in range(NB):
                cp = pltpu.make_async_copy(
                    src.at[frames_at(s, b, a0, a1)],
                    dst.at[s, pl.ds(a0, a1 - a0), :, b],
                    sem_l.at[which, i * NB + b],
                )
                cond = s == 0 if beyond(b, a0) else None
                when(cond, cp.start)
                local.append((cond, cp))
    if z.pad:

        @pl.when(s == 1)
        def _():
            for ref in (xh, ct):
                ref[:, L - z.pad :, :, NB - 1] = jnp.zeros((2, z.pad, J, 2, H), bf)

    lw = [
        pltpu.make_async_copy(ws_in, ws.at[:, pl.ds(pl.multiple_of(s * 3 * H, H), 3 * H)], sem_l.at[2, 0]),
        pltpu.make_async_copy(wt_in, wt.at[:, :, pl.ds(pl.multiple_of(s * H, H), H)], sem_l.at[2, 1]),
    ]
    for cp in lw:
        cp.start()
    for i, v in enumerate((g1, b1, g2, b2)):
        prm[s, i : i + 1] = v[...]

    with jax.named_scope("barrier"):
        pl.semaphore_wait(bar, len(greeted))

    slice_rows = H // z.p1
    row0 = pl.multiple_of(core * H + c1 * slice_rows, slice_rows)

    def ws_at(half, r0, n):
        return ws.at[pl.ds(r0, n), pl.ds(pl.multiple_of(half * 3 * H, H), 3 * H)]

    def wt_at(half, r0, n):
        return wt.at[:, pl.ds(r0, n), pl.ds(pl.multiple_of(half * H, H), H)]

    sends = []

    def go(cp, cond=None):
        when(cond, cp.start)
        sends.append((cond, cp))

    def arrive(dst, rsem):
        remote(dst, dst, rsem, rsem, partner).wait_recv()

    go(remote(prm.at[s], prm.at[s], sem_w.at[0, 0], sem_w.at[1, 0], partner))
    go(remote(ws_in.at[pl.ds(row0, slice_rows)], ws_at(s, row0, slice_rows), sem_w.at[0, 1], sem_w.at[1, 1], partner))
    go(remote(wt_in.at[:, pl.ds(row0, slice_rows)], wt_at(s, row0, slice_rows), sem_w.at[0, 2], sem_w.at[1, 2], partner))

    def send_rows(src, dst, sem, j):
        a0, a1 = z.chunks[j]
        for b in range(NB):
            go(
                remote(
                    src.at[frames_at(o, b, a0, a1)],
                    dst.at[s, pl.ds(a0, a1 - a0), :, b],
                    sem.at[0, j, b],
                    sem.at[1, j, b],
                    partner,
                ),
                o == 0 if beyond(b, a0) else None,
            )

    def take_rows(dst, sem, j):
        a0, a1 = z.chunks[j]
        for b in range(NB):
            at = dst.at[o, pl.ds(a0, a1 - a0), :, b]
            when(s == 0 if beyond(b, a0) else None, lambda at=at, b=b: arrive(at, sem.at[1, j, b]))

    n_chunks = len(z.chunks)
    for j in range(n_chunks):
        send_rows(feat, xh, sem_f, j)
    for j in range(n_chunks):
        send_rows(cot, ct, sem_c, j)

    ri = lax.broadcasted_iota(jnp.int32, (J, J), 0)
    ci = lax.broadcasted_iota(jnp.int32, (J, J), 1)
    eye = jnp.where(ri == ci, 1.0, 0.0).astype(f32)
    up = jnp.zeros((J, J), f32)
    down = jnp.zeros((J, J), f32)
    for v in range(1, J):
        pv = par[v]
        up = jnp.where((ri == v) & (ci == pv), 1.0, up)
        down = jnp.where((ci == v) & (ri == pv), 1.0, down)
    degree = jnp.sum(eye + up + down, axis=0, keepdims=True)
    adjacent = [eye / degree, up / degree, down / degree]
    mixing = [adjacent[k] * imp[k] for k in range(3)]
    for k in range(3):
        adj[k] = adjacent[k]
    last = (((1,), (1,)), ((), ()))
    first = (((0,), (0,)), ((), ()))
    wide = jnp.ones((J, C), f32)
    edge[0] = jnp.dot(mixing[0], wide, precision=exact_mode, preferred_element_type=f32)
    edge[1] = jnp.dot(mixing[1], wide, precision=exact_mode, preferred_element_type=f32)
    edge[2] = lax.dot_general(mixing[2], wide, first, precision=exact_mode, preferred_element_type=f32)

    def kin_body(v, _):
        pv = par[v]
        sibling = jnp.int32(0)
        child = jnp.int32(0)
        for w in range(J - 1, 0, -1):
            pw_ = par[w]
            sibling = jnp.where((pw_ == pv) & (w > v), w, sibling)
            child = jnp.where(pw_ == v, w, child)
        kin[0, v] = sibling
        kin[1, v] = child
        return 0

    lax.fori_loop(0, J, kin_body, 0)

    for i, at in ((0, ws_at), (1, wt_at)):
        arrive(at(o, row0, slice_rows), sem_w.at[1, 1 + i])
        for d in range(1, z.p1):
            t = lax.rem(c1 + d, z.p1)
            go(
                remote(
                    at(o, row0, slice_rows),
                    at(o, row0, slice_rows),
                    sem_w.at[0, 4 + i * 16 + d],
                    sem_w.at[1, 4 + i * 16 + d],
                    peer_b(t),
                )
            )
    for i, at in ((0, ws_at), (1, wt_at)):
        for d in range(1, z.p1):
            t = lax.rem(c1 + z.p1 - d, z.p1)
            arrive(
                at(o, pl.multiple_of(core * H + t * slice_rows, slice_rows), slice_rows),
                sem_w.at[1, 4 + i * 16 + d],
            )
        mine = pl.multiple_of(core * H, H)
        go(remote(at(o, mine, H), at(o, mine, H), sem_w.at[0, 36 + i], sem_w.at[1, 36 + i], (2 * chip + 1 - core, s)))
    theirs = pl.multiple_of((1 - core) * H, H)
    arrive(ws_at(o, theirs, H), sem_w.at[1, 36])
    for cp in lw:
        cp.wait()
    arrive(prm.at[o], sem_w.at[1, 0])
    p0 = pres[0, 0].astype(f32)
    p1 = pres[0, 1].astype(f32)
    ri16 = lax.broadcasted_iota(jnp.int32, (RW, C), 0)
    pw = jnp.where((ri16 & 1) == 0, p0, p1).astype(f32)
    tail = jnp.where(ri16 >= RW - 2, 1.0, 0.0).astype(f32)
    side = s.astype(f32)

    real = 1.0 - tail * side
    cut = L - z.pad

    def tiles(x):
        return x.reshape(-1, RW, C)

    def flat(x):
        return x.reshape(R, C)

    def keep(x, late):
        return (tiles(x) * real[None]).reshape(x.shape) if late else x

    def down_rows(x):
        return jnp.sum(tiles(x), axis=0)

    def each(body, carry):
        carry = lax.fori_loop(0, cut, body(False), carry)
        return lax.fori_loop(cut, L, body(True), carry) if z.pad else carry

    def row_sum(x):
        return jnp.sum(x, axis=0, keepdims=True)

    def param(i):
        return jnp.concatenate([prm[0, i : i + 1], prm[1, i : i + 1]], axis=1)

    def whole(ref, a):
        return jnp.concatenate([ref[0, a].reshape(R, H), ref[1, a].reshape(R, H)], axis=1)

    def put(ref, a, value):
        for h in range(2):
            ref[h, a] = value[:, h * H : (h + 1) * H].reshape(J, RW, H)

    def land(ref, a, value):
        for h in range(2):
            ref[h, a] = value[:, h * H : (h + 1) * H].reshape(J, NB, 2, H)

    def spread(buf, sem, r, q, n, peer, val):
        buf[r, q] = val
        for d in range(1, n):
            go(remote(buf.at[r, q], buf.at[r, q], sem.at[0, r, d], sem.at[1, r, d], peer(lax.rem(q + d, n))))

    def gather(buf, sem, r, q, n):
        for d in range(1, n):
            arrive(buf.at[r, lax.rem(q + n - d, n)], sem.at[1, r, d])
        return [buf[r, i] for i in range(n)]

    def add_up(parts):
        t = parts[0]
        for x in parts[1:]:
            t = t + x
        return t

    def merge(parts):
        n = add_up([x[0:1] for x in parts])
        below = jnp.maximum(n, 1.0)
        mean = add_up([x[0:1] * x[1:2] for x in parts]) / below
        spread_up = add_up([x[2:3] + x[0:1] * (x[1:2] - mean) * (x[1:2] - mean) for x in parts])
        return jnp.concatenate([n, mean, spread_up, jnp.zeros((5, C), f32)], axis=0)

    def all_start(r, val):
        spread(arA, semA, r, d1, z.near, peer_0, val)

    def all_more(r, join):
        val = join(gather(arA, semA, r, d1, z.near))
        if z.p2 > 1:
            spread(arC, semC, r, c2, z.p2, peer_c, val)
            val = join(gather(arC, semC, r, c2, z.p2))
        arD[r, s] = val
        go(remote(arD.at[r, s], arD.at[r, s], semD.at[0, r], semD.at[1, r], across))

    def all_end(r, join):
        arrive(arD.at[r, o], semD.at[1, r])
        return join([arD[r, 0], arD[r, 1]])

    def moments(val_k, s1, s2):
        n = (p0 + p1) * (z.win - z.pad * side) * J
        below = jnp.maximum(n, 1.0)
        s1, s2 = row_sum(s1), row_sum(s2)
        return jnp.concatenate(
            [jnp.zeros((1, C), f32) + n, val_k + s1 / below, s2 - s1 * s1 / below, jnp.zeros((5, C), f32)], axis=0
        )

    def scaled(sums, rstd):
        return jnp.concatenate([sums[0:1], sums[1:2] * rstd], axis=0)

    zero16 = jnp.zeros((RW, C), f32)
    zero1 = jnp.zeros((1, C), f32)

    def spatial_chunk(a0, a1, carry):
        k_shift, s1, s2 = carry
        n = a1 - a0
        span, up_at, down_at, link = pl.ds(a0, n), pl.ds(0, n), pl.ds(n, n), pl.ds(2 * n, n)

        def body(i, _):
            f = whole(xh, a0 + i)
            put(fx, a0 + i, f)
            for k, (buf, at) in enumerate(((summed, a0 + i), (conv, i), (conv, n + i))):
                buf[at] = tiles(jnp.dot(f, ws[:, k * C : (k + 1) * C], preferred_element_type=f32))
            return 0

        lax.fori_loop(0, n, body, 0)
        conv[link, 0] = jnp.zeros((n, RW, C), f32)
        for v in range(J - 1, 0, -1):
            conv[link, v] = conv[down_at, v] * edge[2, v : v + 1] + conv[link, kin[0, v]]
        w = (pw * real if a0 >= cut else pw)[None]
        for v in range(J):
            t = summed[span, v] * edge[0, v : v + 1] + conv[link, kin[1, v]]
            if v:
                t = t + conv[up_at, par[v]] * edge[1, v : v + 1]
            summed[span, v] = t
            if a0 == 0 and v == 0:
                k_shift = row_sum(jnp.sum(t, axis=0)) * (1.0 / (n * RW))
            d = t - k_shift
            wd = d * w
            s1 = s1 + jnp.sum(wd, axis=0)
            s2 = s2 + jnp.sum(wd * d, axis=0)
        return k_shift, s1, s2

    carry = (zero1, zero16, zero16)
    n_local = len(z.locals) * NB
    for cond, cp in local[:n_local]:
        when(cond, cp.wait)
    for j, (a0, a1) in enumerate(z.chunks):
        with jax.named_scope("features_wait"):
            take_rows(xh, sem_f, j)
        with jax.named_scope("spatial"):
            carry = spatial_chunk(a0, a1, carry)

    per = 2 * J
    packed = -(-HALO * per // RW) * RW
    lane = lax.broadcasted_iota(jnp.int32, (packed, R), 1)
    line = lax.broadcasted_iota(jnp.int32, (packed, R), 0)
    off = (RW - 2) * o

    def pick(h):
        at = line - h * per
        hit = lane == lax.shift_right_arithmetic(at, 1) * RW + off + (at & 1)
        return jnp.where(hit & (at >= 0) & (at < per), 1.0, 0.0).astype(bf)

    edge_a = (L - HALO) * o

    def halo_rows(slot, ref):
        rows = jnp.zeros((packed, C), f32)
        for h in range(HALO):
            rows = rows + jnp.dot(pick(h), ref(edge_a + h).astype(bf), preferred_element_type=f32)
        halo_s[slot] = rows.astype(bf)

    def halo_send(r, n, src, dst, hop, dev):
        at = pl.ds(r, n)
        go(remote(src.at[at], dst.at[at], sem_h.at[0, r, hop], sem_h.at[1, r, hop], dev))

    def halo_wait(r, n, dst, hop):
        arrive(dst.at[pl.ds(r, n)], sem_h.at[1, r, hop])

    row_in = lax.broadcasted_iota(jnp.int32, (R, C), 0) & (RW - 1)
    fside = 1.0 - side

    def fill_halo(buf, fresh):
        for h in range(HALO):
            extra = lax.dot_general(pick(h), fresh, first, preferred_element_type=f32)
            lower = pltpu.roll(buf[L + h].reshape(R, C).astype(f32), 2, 0)
            lower = jnp.where(row_in < 2, extra * side, lower)
            buf[h] = tiles(lower.astype(bf))
            upper = pltpu.roll(buf[HALO + h].reshape(R, C).astype(f32), R - 2, 0)
            upper = jnp.where(row_in >= RW - 2, extra * fside, upper)
            buf[HALO + L + h] = tiles(upper.astype(bf))

    all_start(0, moments(*carry))
    halo_rows(0, lambda a: flat(summed[a]))
    halo_send(0, 1, halo_s, halo_m, 0, across)
    with jax.named_scope("st1"):
        all_more(0, merge)
        halo_wait(0, 1, halo_m, 0)
        halo_send(0, 1, halo_m, halo_r, 1, beside)
        st1 = all_end(0, merge)
    count = jnp.maximum(st1[0:1], 1.0)
    mean1 = st1[1:2]
    rstd1 = lax.rsqrt(st1[2:3] / count + norm_eps)
    gain1, shift1 = param(0), param(1)
    scale1 = rstd1 * gain1

    def act_body(late):
        def body(a, _):
            t = gelu((flat(summed[a]) - mean1) * scale1 + shift1)
            acth[a + HALO] = tiles(keep(t, late).astype(bf))
            return 0

        return body

    with jax.named_scope("act"):
        each(act_body, 0)

    def act_halo():
        halo_wait(0, 1, halo_r, 1)
        fill_halo(acth, gelu((halo_r[0].astype(f32) - mean1) * scale1 + shift1).astype(bf))

    arrive(wt_at(o, theirs, H), sem_w.at[1, 37])

    def conv_block(a0, late, carry):
        k_shift, s1, s2 = carry
        n = len(late)
        t = jnp.zeros((n * R, C), f32)
        for tap in range(TAPS):
            t = t + jnp.dot(acth[pl.ds(a0 + tap, n)].reshape(n * R, C), wt[tap], preferred_element_type=f32)
        conv[pl.ds(a0, n)] = t.reshape(n, J, RW, C)
        if a0 == HALO:
            k_shift = row_sum(t[:R]) * (1.0 / R)
        for i in range(n):
            w = pw * real if late[i] else pw
            d = tiles(t[i * R : (i + 1) * R] - k_shift)
            wd = d * w[None]
            s1 = s1 + jnp.sum(wd, axis=0)
            s2 = s2 + jnp.sum(wd * d, axis=0)
        return k_shift, s1, s2

    def blocks(fun, carry, ready):
        def run(a0, a1, carry):
            return fun(a0, [a >= cut for a in range(a0, a1)], carry)

        for a0 in range(HALO, L - HALO, G):
            carry = run(a0, min(a0 + G, L - HALO), carry)
        ready()
        carry = run(0, HALO, carry)
        return run(L - HALO, L, carry)

    with jax.named_scope("conv"):
        carry = blocks(conv_block, (zero1, zero16, zero16), act_halo)
    all_start(1, moments(*carry))
    n_early = min(2, n_chunks)
    for cond, cp in local[n_local:]:
        when(cond, cp.wait)

    def tile_body(a, _):
        put(iz, a, whole(ct, a))
        return 0

    for j in range(n_early):
        take_rows(ct, sem_c, j)
        lax.fori_loop(*z.chunks[j], tile_body, 0)
    with jax.named_scope("st2"):
        all_more(1, merge)
        st2 = all_end(1, merge)
    mean2 = st2[1:2]
    rstd2 = lax.rsqrt(st2[2:3] / count + norm_eps)
    gain2, shift2 = param(2), param(3)

    scale2 = rstd2 * gain2

    def out_body(late, cots):
        def body(a, carry):
            sa, sb = carry
            centred = flat(conv[a]) - mean2
            level = centred * scale2 + (shift2 + whole(fx, a).astype(f32))
            value, slope = gelu_both(level)
            land(xh, a, value.astype(bf))
            gp = whole(cots, a).astype(f32) * slope
            conv[a] = tiles(gp)
            put(iz, a, centred.astype(bf))
            gm = keep(gp, late)
            return sa + down_rows(gm), sb + down_rows(gm * centred)

        return body

    carry = (zero16, zero16)
    outs = []

    def ship(buf, nat, sem, j, chunks):
        a0, a1 = chunks[j]
        for b in range(NB):
            src, at = (pl.ds(a0, a1 - a0), slice(None), b), frames_at(s, b, a0, a1)
            cond = s == 0 if beyond(b, a0) else None
            go(remote(buf.at[(o, *src)], nat.at[at], sem.at[0, j, b], sem.at[1, j, b], partner), cond)
            cp = pltpu.make_async_copy(buf.at[(s, *src)], nat.at[at], sem.at[2, j, b])
            when(cond, cp.start)
            outs.append((cond, cp))

    def shipped(nat, sem, j, chunks):
        a0, a1 = chunks[j]
        for b in range(NB):
            at = nat.at[frames_at(o, b, a0, a1)]
            when(o == 0 if beyond(b, a0) else None, lambda at=at, b=b: arrive(at, sem.at[1, j, b]))

    for j, (a0, a1) in enumerate(z.chunks):
        if j >= n_early:
            with jax.named_scope("cotangent_wait"):
                take_rows(ct, sem_c, j)
        with jax.named_scope("level_two"):
            carry = lax.fori_loop(a0, a1, out_body(a0 >= cut, iz if j < n_early else ct), carry)
        ship(xh, act_nat, sem_a, j, z.chunks)

    pad6 = jnp.zeros((6, C), f32)
    all_start(2, jnp.concatenate([row_sum(carry[0]), row_sum(carry[1]), pad6], axis=0))
    with jax.named_scope("sum2"):
        all_more(2, add_up)
        sum2 = all_end(2, add_up)
    sum2 = scaled(sum2, rstd2)

    def corrections(scale, rstd, sums):
        shift = scale * sums[0:1] / count
        slope = scale * rstd * sums[1:2] / count
        return scale, (shift * pw)[None], (slope * pw)[None]

    def back(grad, centred, scale, shift, slope):
        return grad * scale - (tiles(centred) * slope + shift).reshape(grad.shape)

    out_corr = corrections(scale2, rstd2, sum2)

    def gconv_body(late):
        def body(a, _):
            gp = flat(conv[a])
            t = back(gp, whole(iz, a).astype(f32), *out_corr)
            gch[a + HALO] = tiles(keep(t, late).astype(bf))
            put(iz, a, gp.astype(bf))
            return 0

        return body

    with jax.named_scope("gconv"):
        lax.fori_loop(cut, L, gconv_body(True), 0)
        lax.fori_loop(L - HALO, cut, gconv_body(False), 0)
        lax.fori_loop(0, HALO, gconv_body(False), 0)
        halo_rows(1, lambda a: flat(gch[a + HALO]))
        halo_send(1, 1, halo_s, halo_m, 0, across)
        lax.fori_loop(HALO, min(cut, L - HALO), gconv_body(False), 0)
        halo_wait(1, 1, halo_m, 0)
        halo_send(1, 1, halo_m, halo_r, 1, beside)

    def conv_halo():
        halo_wait(1, 1, halo_r, 1)
        fill_halo(gch, halo_r[1])

    def gact_block(a0, late, carry):
        sa, sb = carry
        n = len(late)
        t = jnp.zeros((n * R, C), f32)
        for tap in range(TAPS):
            t = t + lax.dot_general(
                gch[pl.ds(a0 + TAPS - 1 - tap, n)].reshape(n * R, C), wt[tap], last, preferred_element_type=f32
            )
        for i in range(n):
            centred = flat(summed[a0 + i]) - mean1
            _, slope = gelu_both(centred * scale1 + shift1)
            gl = t[i * R : (i + 1) * R] * slope
            conv[a0 + i] = tiles(gl)
            gm = keep(gl, late[i])
            sa = sa + down_rows(gm)
            sb = sb + down_rows(gm * centred)
        return sa, sb

    with jax.named_scope("grad_act"):
        carry = blocks(gact_block, (zero16, zero16), conv_halo)
    all_start(3, jnp.concatenate([row_sum(carry[0]), row_sum(carry[1]), pad6], axis=0))

    def tap_body(tap, _):
        t = lax.dot_general(
            acth[pl.ds(tap, L)].reshape(z.total, C),
            gch[pl.ds(HALO, L)].reshape(z.total, C),
            first,
            preferred_element_type=f32,
        )
        gb[0, tap] = t[:, :H]
        gb[1, tap] = t[:, H:]
        return 0

    with jax.named_scope("tap_grad"):
        lax.fori_loop(0, EARLY // 2, tap_body, 0)
        all_more(3, add_up)
        lax.fori_loop(EARLY // 2, EARLY, tap_body, 0)
    with jax.named_scope("sum1_wait"):
        sum1 = all_end(3, add_up)
    sum1 = scaled(sum1, rstd1)
    in_corr = corrections(scale1, rstd1, sum1)

    neighbour = (2 * chip + 1 - core, s)
    core_rows = pl.multiple_of(core * H, H)
    other_rows = pl.multiple_of((1 - core) * H, H)
    def slice_of(t):
        return pl.multiple_of(owned(t) * slice_rows, slice_rows)

    chip_rows = slice_of(c1)
    spans = (pl.ds(0, EARLY), pl.ds(EARLY, TAPS + 3 - EARLY))

    def grad_core(i):
        cut = (slice(None), spans[i])
        go(
            remote(
                gb.at[(*cut, pl.ds(other_rows, H))], gb_core.at[cut], sem_g.at[0, i, 0], sem_g.at[1, i, 0], neighbour
            )
        )

    def grad_chips(i):
        cut = (slice(None), spans[i])
        arrive(gb_core.at[cut], sem_g.at[1, i, 0])
        total = gb[(*cut, pl.ds(core_rows, H))] + gb_core[cut]
        gb_low[cut] = total.astype(bf)
        for d in range(1, z.p1):
            t = lax.rem(c1 + d, z.p1)
            go(
                remote(
                    gb_low.at[(*cut, pl.ds(slice_of(t), slice_rows))],
                    gb_chips.at[(c1, *cut)],
                    sem_g.at[0, i, d],
                    sem_g.at[1, i, d],
                    peer_b(t),
                )
            )

    def grad_pair(i):
        cut = (slice(None), spans[i])
        gb_chips[(c1, *cut)] = gb_low[(*cut, pl.ds(chip_rows, slice_rows))]
        for d in range(1, z.p1):
            arrive(gb_chips.at[(lax.rem(c1 + z.p1 - d, z.p1), *cut)], sem_g.at[1, i, d])
        gb_sum[cut] = add_up([gb_chips[(p, *cut)].astype(f32) for p in range(z.p1)])
        if z.p2 > 1:
            gb_far[(c2, *cut)] = gb_sum[cut].astype(bf)
            for d in range(1, z.p2):
                t = lax.rem(c2 + d, z.p2)
                go(
                    remote(
                        gb_far.at[(c2, *cut)],
                        gb_far.at[(c2, *cut)],
                        sem_g.at[0, i, 24 + d],
                        sem_g.at[1, i, 24 + d],
                        peer_c(t),
                    )
                )
            for d in range(1, z.p2):
                arrive(gb_far.at[(lax.rem(c2 + z.p2 - d, z.p2), *cut)], sem_g.at[1, i, 24 + d])
            gb_sum[cut] = add_up([gb_far[(p, *cut)].astype(f32) for p in range(z.p2)])
        go(remote(gb_sum.at[o, spans[i]], gb_pair.at[spans[i]], sem_g.at[0, i, 8], sem_g.at[1, i, 8], across))

    def grad_back(i):
        arrive(gb_pair.at[spans[i]], sem_g.at[1, i, 8])
        mine = gb_sum[s, spans[i]]
        other = gb_pair[spans[i]]
        own = pl.multiple_of(core_rows + chip_rows, slice_rows)
        gb_fin[spans[i], pl.ds(own, slice_rows)] = (mine + other).astype(bf)
        at = gb_fin.at[spans[i], pl.ds(own, slice_rows)]
        for d in range(1, z.p1):
            t = lax.rem(c1 + d, z.p1)
            go(remote(at, at, sem_g.at[0, i, 8 + d], sem_g.at[1, i, 8 + d], peer_b(t)))

    def grad_last(i):
        for d in range(1, z.p1):
            t = lax.rem(c1 + z.p1 - d, z.p1)
            at = pl.multiple_of(core_rows + slice_of(t), slice_rows)
            arrive(gb_fin.at[spans[i], pl.ds(at, slice_rows)], sem_g.at[1, i, 8 + d])
        at = gb_fin.at[spans[i], pl.ds(core_rows, H)]
        go(remote(at, at, sem_g.at[0, i, 16], sem_g.at[1, i, 16], neighbour))

    def grad_done(i):
        arrive(gb_fin.at[spans[i], pl.ds(other_rows, H)], sem_g.at[1, i, 16])

    grad_core(0)

    def grad_body(late):
        def body(a, _):
            gs = back(flat(conv[a]), flat(summed[a]) - mean1, *in_corr)
            gs = keep(gs, late).astype(bf)
            conv[a] = tiles(gs.astype(f32))
            return 0

        return body

    def grad_chunk(j):
        lax.fori_loop(*z.tail[j], grad_body(z.tail[j][0] >= cut), 0)

    def input_chunk(j):
        a0, a1 = z.tail[j]
        n = a1 - a0
        span = pl.ds(a0, n)
        summed[span, 0] = jnp.zeros((n, RW, C), f32)
        for v in range(J - 1, 0, -1):
            summed[span, v] = conv[span, v] * edge[1, v : v + 1] + summed[span, kin[0, v]]
        for w in range(J):
            mixed[0, pl.ds(0, n), w] = summed[span, kin[1, w]].astype(bf)
            mixed[1, pl.ds(0, n), w] = (conv[span, par[w]] * edge[2, w : w + 1]).astype(bf)

        def out(i, _):
            t = whole(iz, a0 + i).astype(f32)
            own = (conv[a0 + i] * edge[0][:, None, :]).astype(bf)
            for k, rows in enumerate((own, mixed[0, i], mixed[1, i])):
                t = t + lax.dot_general(
                    flat(rows), ws[:, k * C : (k + 1) * C], last, preferred_element_type=f32
                )
            land(ct, a0 + i, t.astype(bf))
            return 0

        lax.fori_loop(0, n, out, 0)

        ship(ct, ing_nat, sem_i, j, z.tail)

    def edge_rows_f(v):
        return jnp.concatenate(
            [fx[0, :, pl.ds(v, 1)].reshape(L * RW, H), fx[1, :, pl.ds(v, 1)].reshape(L * RW, H)], axis=1
        )

    def edge_rows_g(v):
        return conv[:, pl.ds(v, 1)].reshape(L * RW, C).astype(bf)

    gb[:, TAPS:] = jnp.zeros((2, 3, C, H), f32)

    dots[...] = jnp.zeros_like(dots)
    unroll = 5 if J % 5 == 0 else 1

    def edge_body(i, _):
        for u in range(unroll):
            v = i * unroll + u
            pv = par[v]
            f_v, f_p, g_v, g_p = edge_rows_f(v), edge_rows_f(pv), edge_rows_g(v), edge_rows_g(pv)
            both = lax.dot_general(
                f_v, jnp.concatenate([g_v, g_p], axis=1), first, preferred_element_type=f32
            )
            up_prod = lax.dot_general(f_p, g_v, first, preferred_element_type=f32)
            for k, prod in enumerate((both[:, :C], up_prod, both[:, C:])):
                part = prod * edge[k, pl.ds(v, 1)]
                for h in range(2):
                    j = 2 * k + h
                    gb[j // 3, TAPS + j % 3] += part[:, h * H : (h + 1) * H]
                dots[k, pl.ds(v, 1)] = row_sum(prod * ws[:, k * C : (k + 1) * C].astype(f32))
        return 0

    edge_steps = J // unroll

    def edge_sums():
        ones = jnp.ones((8, C), f32)
        n = dots.shape[1]
        spread_out = jnp.where(
            lax.broadcasted_iota(jnp.int32, (n, C), 0) == lax.broadcasted_iota(jnp.int32, (n, C), 1), 1.0, 0.0
        )
        rows = []
        for k in range(3):
            t = lax.dot_general(ones, dots[k], last, precision=exact_mode, preferred_element_type=f32)
            t = jnp.dot(t, spread_out, precision=exact_mode, preferred_element_type=f32)
            rows.append(t[0:1])
        return jnp.concatenate(rows + [jnp.zeros((5, C), f32)], axis=0)

    ready = set()
    steps = {
        "chips0": lambda: grad_chips(0),
        "late": lambda: lax.fori_loop(EARLY, TAPS, tap_body, 0),
        "pair0": lambda: grad_pair(0),
        "chips1": lambda: grad_chips(1),
        "back0": lambda: grad_back(0),
        "pair1": lambda: (all_more(4, add_up), grad_pair(1)),
        "last0": lambda: grad_last(0),
        "back1": lambda: grad_back(1),
        "last1": lambda: grad_last(1),
    }

    def sums_ready(chunks):
        for j in chunks:
            if j not in ready:
                ready.add(j)
                grad_chunk(j)

    for step in LAST_STEPS:
        with jax.named_scope("step_" + step):
            if step == "edges_a":
                sums_ready(range(len(z.tail)))
                lax.fori_loop(0, edge_steps // 2, edge_body, 0)
            elif step == "edges_b":
                lax.fori_loop(edge_steps // 2, edge_steps, edge_body, 0)
                grad_core(1)
                all_start(4, edge_sums())
            elif step in steps:
                steps[step]()
            else:
                sums_ready([int(step)])
                input_chunk(int(step))
    dvec = all_end(4, add_up)
    for k in range(3):
        per_edge = dvec[k : k + 1, :J]
        if k == 1:
            per_edge = lax.dot_general(
                eye, jnp.broadcast_to(per_edge, (J, J)), last, precision=exact_mode, preferred_element_type=f32
            )
        ig_out[k] = adj[k] * per_edge
    for i, row in enumerate((sum1[1:2], sum1[0:1], sum2[1:2], sum2[0:1])):
        sums_out[i : i + 1] = jnp.where(s == 0, row[:, :H], row[:, H:])
    sums_out[4:8] = jnp.zeros((4, H), f32)
    with jax.named_scope("grad_reduce_end"):
        grad_done(0)
        grad_done(1)
        last_out = [pltpu.make_async_copy(gb_fin.at[pl.ds(0, TAPS)], tg_out, sem_l.at[2, 2])]
        for j in range(3):
            last_out.append(
                pltpu.make_async_copy(gb_fin.at[TAPS + j], sg_out.at[:, pl.ds(j * H, H)], sem_l.at[2, 3 + j])
            )
        for cp in last_out:
            cp.start()

    with jax.named_scope("last_waits"):
        for j in range(n_chunks):
            shipped(act_nat, sem_a, j, z.chunks)
        for j in range(len(z.tail)):
            shipped(ing_nat, sem_i, j, z.tail)
        for cond, cp in outs + [(None, cp) for cp in last_out]:
            when(cond, cp.wait)
        for cond, cp in sends:
            when(cond, cp.wait_send)


def finish(
    z,
    act_in,
    ing_in,
    tg_in,
    sg_in,
    sums_in,
    ig_in,
    act_out,
    ing_out,
    tg_out,
    sg_out,
    r0,
    r1,
    r2,
    r3,
    ig_out,
    low,
    full,
    tg,
    sg,
    tg_wide,
    sg_wide,
    sem_in,
    sem_out,
    sem_g,
):
    f32 = jnp.float32
    n = len(z.slabs)
    jobs = [(i, q, src, dst) for q in range(n) for i, (src, dst) in enumerate(((act_in, act_out), (ing_in, ing_out)))]
    ins, outs = [], []
    for i, q, src, dst in jobs:
        at = pl.ds(z.slabs[q][0], z.slabs[q][1])
        ins.append(pltpu.make_async_copy(src.at[at], low.at[i, at], sem_in.at[i, q]))
        outs.append(pltpu.make_async_copy(full.at[i, at], dst.at[at], sem_out.at[i, q]))
        ins[-1].start()
    grads = []
    for i, (src, mid, wide, dst) in enumerate(((tg_in, tg, tg_wide, tg_out), (sg_in, sg, sg_wide, sg_out))):
        cp = pltpu.make_async_copy(src, mid, sem_g.at[0, i])
        cp.start()
        grads.append((cp, mid, wide, pltpu.make_async_copy(wide, dst, sem_g.at[1, i])))
    for i, r in enumerate((r0, r1, r2, r3)):
        r[...] = sums_in[i : i + 1]
    ig_out[...] = ig_in[...]
    shape = (2, z.groups, z.rows // RW * NB // 8, RW, z.half)
    lows, fulls = low.reshape(shape), full.reshape(shape)
    for (i, q, _, _), cp_in, cp_out in zip(jobs, ins, outs):
        first, count = z.slabs[q]
        cp_in.wait()

        def body(g, _, i=i):
            fulls[i, g] = lows[i, g].astype(f32)
            return 0

        lax.fori_loop(first // 8, -(-(first + count) // 8), body, 0)
        cp_out.start()
    for cp_in, mid, wide, cp_out in grads:
        cp_in.wait()
        wide[...] = mid[...].astype(f32)
        cp_out.start()
    for cp_out in outs + [g[3] for g in grads]:
        cp_out.wait()


def block(
    n_dp, features, presence, parents, w_spatial, importance, gain_one, shift_one, w_temporal, gain_two, shift_two, cotangent
):
    _, _, frames, joints, half = features.shape
    z = Sizes(n_dp, frames, joints, half)
    f32, bf = jnp.float32, jnp.bfloat16
    C, H, L, R, J = z.chan, z.half, z.blk, z.rows, z.joints

    def natural(x):
        return x.transpose(0, 2, 3, 1, 4).reshape(frames, joints, 2, half)

    any_, vmem, smem = (pl.BlockSpec(memory_space=m) for m in (pl.ANY, pltpu.VMEM, pltpu.SMEM))
    landing = (L, J, NB, 2, H)
    blocked = (L, J, RW, H)
    sds = jax.ShapeDtypeStruct
    VM, DMA = pltpu.VMEM, pltpu.SemaphoreType.DMA
    nch = len(z.chunks)
    packed = -(-HALO * 2 * J // RW) * RW
    outs = pl.pallas_call(
        functools.partial(mega, z),
        name="graph_conv_block",
        out_shape=[sds((frames, joints, 2, H), bf)] * 2
        + [sds((TAPS, C, H), bf), sds((C, 3 * H), bf), sds((8, H), f32), sds((3, J, J), f32)],
        in_specs=[any_] * 4 + [vmem, smem, smem] + [vmem] * 4,
        out_specs=[any_] * 4 + [vmem] * 2,
        scratch_shapes=[
            VM((2,) + landing, bf),
            VM((2,) + landing, bf),
            VM((2,) + blocked, bf),
            VM((TAPS, C, C), bf),
            VM((C, 3 * C), bf),
            VM((L, J, RW, C), f32),
            VM((L + 2 * HALO, J, RW, C), bf),
            VM((L, J, RW, C), f32),
            VM((L + 2 * HALO, J, RW, C), bf),
            VM((2,) + blocked, bf),
            VM((2, TAPS + 3, C, H), f32),
            VM((2, TAPS + 3, H, H), f32),
            VM((2, TAPS + 3, H, H), bf),
            VM((z.p1, 2, TAPS + 3, H // z.p1, H), bf),
            VM((z.p2, 2, TAPS + 3, H // z.p1, H), bf),
            VM((2, TAPS + 3, H // z.p1, H), f32),
            VM((TAPS + 3, H // z.p1, H), f32),
            VM((TAPS + 3, C, H), bf),
            VM((2, max(a1 - a0 for a0, a1 in z.tail), J, RW, C), bf),
            VM((3, -(-J // 8) * 8, C), f32),
            VM((2, 8, H), f32),
            VM((3, J, J), f32),
            VM((3, J, C), f32),
            pltpu.SMEM((2, J), jnp.int32),
            VM((2, packed, C), bf),
            VM((2, packed, C), bf),
            VM((2, packed, C), bf),
            VM((5, z.near, 8, C), f32),
            VM((5, z.p2, 8, C), f32),
            VM((5, 2, 8, C), f32),
            DMA((3, 2 * NB)),
            DMA((2, nch, NB)),
            DMA((2, nch, NB)),
            DMA((3, nch, NB)),
            DMA((3, len(z.tail), NB)),
            DMA((2, 40)),
            DMA((2, 2, 2)),
            DMA((2, 2, 32)),
            DMA((2, 5, z.near)),
            DMA((2, 5, z.p2)),
            DMA((2, 5)),
        ],
        compiler_params=pltpu.CompilerParams(
            collective_id=0, has_side_effects=True, vmem_limit_bytes=63 * 2**20
        ),
    )(
        natural(features),
        natural(cotangent),
        w_temporal,
        w_spatial,
        importance,
        parents,
        presence,
        *(v.reshape(1, H) for v in (gain_one, shift_one, gain_two, shift_two)),
    )
    act, ing, tg, sg, r0, r1, r2, r3, ig = pl.pallas_call(
        functools.partial(finish, z),
        name="natural_order",
        out_shape=[sds((frames, joints, 2, H), f32)] * 2
        + [sds((TAPS, C, H), f32), sds((C, 3 * H), f32)]
        + [sds((1, H), f32)] * 4
        + [sds((3, J, J), f32)],
        in_specs=[any_] * 4 + [vmem] * 2,
        out_specs=[any_] * 4 + [vmem] * 5,
        scratch_shapes=[
            VM((2, 8 * z.groups, joints, 2, H), bf),
            VM((2, 8 * z.groups, joints, 2, H), f32),
            VM((TAPS, C, H), bf),
            VM((C, 3 * H), bf),
            VM((TAPS, C, H), f32),
            VM((C, 3 * H), f32),
            DMA((2, len(z.slabs))),
            DMA((2, len(z.slabs))),
            DMA((2, 2)),
        ],
        compiler_params=pltpu.CompilerParams(vmem_limit_bytes=60 * 2**20),
    )(*outs)

    def back(x):
        return x.reshape(1, frames, joints, 2, half).transpose(0, 3, 1, 2, 4)

    return (
        back(act),
        back(ing),
        sg,
        ig,
        *(r.reshape(H) for r in (r0, r1)),
        tg,
        *(r.reshape(H) for r in (r2, r3)),
    )


def solution(mesh):
    in_specs = (
        P("dp", None, None, None, "sub"),
        P("dp", None),
        P(),
        P(None, "sub"),
        P(),
        P("sub"),
        P("sub"),
        P(None, None, "sub"),
        P("sub"),
        P("sub"),
        P("dp", None, None, None, "sub"),
    )
    out_specs = (
        P("dp", None, None, None, "sub"),
        P("dp", None, None, None, "sub"),
        P(None, "sub"),
        P(),
        P("sub"),
        P("sub"),
        P(None, None, "sub"),
        P("sub"),
        P("sub"),
    )
    return jax.shard_map(
        functools.partial(block, mesh.shape["dp"]), mesh=mesh, in_specs=in_specs, out_specs=out_specs, check_vma=False
    )
```
